512 devices in a mesh: row: 16 (over z), col: 32 (over y, x, core).
Axes of the slice: x: 4, y: 4, z: 16, core: 2. Of those that a mesh axis runs over, the one named last changes fastest.
Arguments:
- kernel: float32 [8, 16, 128, 4, 32, 128], P(None, 'row', None, None, 'col'), may hold values from -6 to 6, as said below
Outputs:
- updated: float32 [8, 16, 128, 4, 32, 128], P(None, 'row', None, None, 'col')
The draws below stay inside these ranges and needn't reach their ends.
Inputs may be any that keep to these rules, and one draw needn't show every extreme that they name: kernel is symmetric as a matrix: entry (i, j) equals entry (j, i) up to rounding.
All inputs are finite; a program needn't handle non-finite values.
Results may differ from the reference program's by a relative error of at most 0.0003.
Values sent between devices are 32-bit elements; how exact they have to be, the bound alone decides.
No kernel may reach another device: no remote copies, remote signals or barrier semaphores. Data moves between devices by JAX's collectives and lax.ppermute only.
A program may use at most 64 MiB of HBM per device.

```python
import jax
import jax.numpy as jnp
from jax import lax

NB = 128
RB_DEV = 8
ORDER = 16384
CB_DEV = 4
N_ROW = 16
N_COL = 32


def draw_kernel(key, part):
    key = jax.random.fold_in(key, 7)
    noise_key = jax.random.fold_in(key, 0)
    common_key = jax.random.fold_in(key, 2)
    order_key = jax.random.fold_in(key, 3)
    index_line = jnp.arange(ORDER)
    upper_half = index_line[:, None] <= index_line[None, :]
    lowest = jnp.minimum(index_line[:, None], index_line[None, :])
    highest = jnp.maximum(index_line[:, None], index_line[None, :])
    band = (lowest < NB) & (highest >= NB)
    ranks = jax.random.permutation(order_key, NB).astype(jnp.float32) / (NB - 1)
    raw = jax.random.normal(noise_key, (ORDER, ORDER), jnp.float32)
    column_scale = jnp.power(0.25, ranks)
    symmetric = (raw + raw.T) * 0.7071
    scale_line = jnp.concatenate([column_scale, jnp.ones((ORDER - NB,), jnp.float32)])
    common_line = jax.random.uniform(common_key, (ORDER,), jnp.float32, 0.6, 1.4)
    low_scale = jnp.where(upper_half, scale_line[:, None], scale_line[None, :])
    high_common = jnp.where(upper_half, common_line[None, :], common_line[:, None])
    mixed = jnp.where(band, high_common + low_scale * symmetric, symmetric)
    mixed = jnp.clip(mixed, -6.0, 6.0)
    return mixed.reshape(RB_DEV, N_ROW, NB, CB_DEV, N_COL, NB)


def setup_inputs(seed: int = 0) -> dict:
    splits = jax.random.split(jax.random.key(seed), 2)
    kernel = draw_kernel(jax.random.fold_in(splits[1], 71), 0)
    return dict(kernel=kernel)


def mult(left, right):
    return jnp.dot(left.astype(jnp.float32), right.astype(jnp.float32), precision=lax.Precision.HIGHEST, preferred_element_type=jnp.float32)

def factor_unit(square):
    count = square.shape[0]
    index_line = jnp.arange(count)

    def step(k, matrix):
        column = matrix[:, k] / matrix[k, k]
        below = index_line > k
        low_col = jnp.where(below, column, 0.0)
        up_row = jnp.where(below, matrix[k, :], 0.0)
        matrix = matrix - low_col[:, None] * up_row[None, :]
        return jnp.where(below[:, None] & (index_line == k)[None, :], low_col[:, None], matrix)
    matrix = lax.fori_loop(0, count, step, square)
    lower_factor = jnp.tril(matrix, -1) + jnp.eye(count, dtype=square.dtype)
    return (lower_factor, jnp.triu(matrix))

def block_factor(leading):
    sign_diag = jnp.where(jnp.diagonal(leading) >= 0, -1.0, 1.0).astype(leading.dtype)
    lower_factor, upper_factor = factor_unit(leading - jnp.diag(sign_diag))
    right_side = jax.scipy.linalg.solve_triangular(lower_factor, (upper_factor * sign_diag[None, :]).T, lower=True, unit_diagonal=True)
    return (sign_diag, upper_factor, -right_side.T)

def reference(kernel):
    whole = kernel.reshape(ORDER, ORDER)
    panel_cols = whole[NB:, :NB]
    first_factor = jnp.linalg.cholesky(mult(panel_cols.T, panel_cols))
    orthonormal = jax.scipy.linalg.solve_triangular(first_factor, panel_cols.T, lower=True).T
    sign_diag, upper_factor, coupling = block_factor(orthonormal[:NB])
    shifted = orthonormal.at[:NB].add(-jnp.diag(sign_diag))
    vectors = jax.scipy.linalg.solve_triangular(upper_factor.T, shifted.T, lower=True).T
    vectors = jnp.concatenate([jnp.zeros((NB, NB), whole.dtype), vectors], 0)
    projected = mult(mult(whole, vectors), coupling)
    middle_term = mult(vectors.T, projected)
    weights = projected - 0.5 * mult(vectors, mult(coupling.T, middle_term))
    updated = whole - mult(jnp.concatenate([vectors, weights], 1), jnp.concatenate([weights, vectors], 1).T)
    return updated.reshape(kernel.shape)
```

```python
import jax
import jax.numpy as jnp
from jax import lax
from jax.experimental import pallas as pl
from jax.experimental.pallas import tpu as pltpu
from jax.sharding import PartitionSpec as P

NB = 128
SUB = 8


def mult(left, right, left_dim=1, right_dim=0):
    return lax.dot_general(
        left,
        right,
        (((left_dim,), (right_dim,)), ((), ())),
        precision=lax.Precision.HIGHEST,
        preferred_element_type=jnp.float32,
    )


def lane(block, k):
    return jnp.broadcast_to(block[:, k : k + 1], (SUB, NB))


def row(block, s):
    return jnp.broadcast_to(block[s : s + 1, :], (SUB, NB))


def lane_ids():
    sub_id = lax.broadcasted_iota(jnp.int32, (SUB, NB), 0)
    lane_id = lax.broadcasted_iota(jnp.int32, (SUB, NB), 1)
    return sub_id, lane_id


def cholesky_kernel(gram_ref, lead_ref, inv_ref, sign_ref, shift_ref):
    count = NB // SUB
    sub_id, lane_id = lane_ids()
    eye = [jnp.where(lane_id == sub_id + SUB * i, 1.0, 0.0) for i in range(count)]
    left = [gram_ref[SUB * i : SUB * i + SUB, :] for i in range(count)]
    right = list(eye)
    for k in range(NB):
        b, s = divmod(k, SUB)
        pivot_left, pivot_right = row(left[b], s), row(right[b], s)
        scale = 1.0 / lane(pivot_left, k)
        pivot_left, pivot_right = pivot_left * scale, pivot_right * scale
        for i in range(b, count):
            factor = lane(left[i], k)
            if i == b:
                factor = jnp.where(sub_id > s, factor, 0.0)
            left[i] = left[i] - factor * pivot_left
            right[i] = right[i] - factor * pivot_right
    for i in range(count):
        diagonal = jnp.sum(left[i] * eye[i], axis=1, keepdims=True)
        inv_ref[SUB * i : SUB * i + SUB, :] = right[i] * lax.rsqrt(diagonal)
    inverse = inv_ref[...]
    lead = lead_ref[...]
    sign = jnp.where(jnp.sum(lead * inverse, axis=1, keepdims=True) >= 0, -1.0, 1.0)
    for i in range(count):
        sign_ref[SUB * i : SUB * i + SUB, :] = eye[i] * sign[SUB * i : SUB * i + SUB]
    shift_ref[...] = sign * mult(lead, inverse, 1, 1)


def invert_kernel(shift_ref, out_ref):
    count = NB // SUB
    sub_id, lane_id = lane_ids()
    held = [
        jnp.where(lane_id == sub_id + SUB * i, 1.0, 0.0) - shift_ref[SUB * i : SUB * i + SUB, :] for i in range(count)
    ]
    for k in range(NB):
        b, s = divmod(k, SUB)
        pivot = row(held[b], s)
        scale = 1.0 / lane(pivot, k)
        scaled = pivot * scale
        here = lane_id == k
        other = jnp.where(here, 1.0 + scale, scaled)
        own = jnp.where(here, scale, scaled)
        for i in range(count):
            new = held[i] - lane(held[i], k) * other
            if i == b:
                new = jnp.where(sub_id == s, own, new)
            held[i] = new
    for i in range(count):
        out_ref[SUB * i : SUB * i + SUB, :] = held[i]


SQUARE = jax.ShapeDtypeStruct((NB, NB), jnp.float32)


def cholesky_parts(gram, lead):
    return pl.pallas_call(
        cholesky_kernel,
        out_shape=(SQUARE, SQUARE, SQUARE),
        name="cholesky_parts",
        cost_estimate=pl.CostEstimate(flops=40_000_000, bytes_accessed=400_000, transcendentals=0),
    )(gram, lead)


def invert(shift):
    return pl.pallas_call(
        invert_kernel,
        out_shape=SQUARE,
        name="invert",
        cost_estimate=pl.CostEstimate(flops=40_000_000, bytes_accessed=400_000, transcendentals=0),
    )(shift)


def exchange(pieces, axis):
    return lax.all_to_all(pieces, axis, 0, 0)


def gather(piece, axis):
    count = lax.axis_size(axis)
    return exchange(jnp.broadcast_to(piece[None], (count,) + piece.shape), axis)


def body(kernel):
    row_blocks, _, _, col_blocks, _, _ = kernel.shape
    rows, cols = row_blocks * NB, col_blocks * NB
    row_count, col_count = lax.axis_size("row"), lax.axis_size("col")
    fold = col_count // row_count
    row_index, col_index = lax.axis_index("row"), lax.axis_index("col")
    local = kernel.reshape(rows, cols)
    by_block = kernel.reshape(row_blocks, NB, col_blocks, NB)

    own_panel = jnp.where(
        (row_index == 0) & (jnp.arange(row_blocks) == 0)[:, None, None], 0.0, by_block[:, :, 0, :]
    ).reshape(rows, NB)
    own_gram = mult(own_panel, own_panel, 0, 0)
    own_lead = jnp.where(row_index == 1, own_panel[:NB], 0.0)

    step = NB // col_count
    pair = jnp.concatenate([own_gram.reshape(col_count, step, NB), own_lead.reshape(col_count, step, NB)], 1)
    piece = exchange(pair, "col")[0]
    piece = jnp.sum(gather(piece, "row"), 0)
    whole = gather(piece, "col")
    gram = whole[:, :step].reshape(NB, NB)
    lead = whole[:, step:].reshape(NB, NB)

    share = exchange(own_panel.reshape(col_count, rows // col_count, NB), "col")[0]
    panel_rows = gather(share, "col").reshape(rows, NB)

    own_top = jnp.where(
        (col_index == 0) & (jnp.arange(col_blocks) == 0)[:, None, None], 0.0, by_block[0].transpose(1, 2, 0)
    ).reshape(cols, NB)
    col_share = exchange(own_top.reshape(row_count, cols // row_count, NB), "row")[0]
    panel_cols = gather(col_share, "row").reshape(cols, NB)

    inverse, sign, shift = cholesky_parts(gram, lead)
    sign_rows = jnp.where(row_index == 1, sign, 0.0)
    y_rows = mult(panel_rows, inverse, 1, 1)
    y_rows = jnp.concatenate([y_rows[:NB] - sign_rows, y_rows[NB:]], 0)
    partial = mult(local, y_rows, 0, 0)

    part = jnp.sum(exchange(partial.reshape(row_count, cols // row_count, NB), "row"), 0)
    z_cols = gather(part, "row").reshape(cols, NB)

    coupling = invert(shift).T
    y_cols = mult(panel_cols, inverse, 1, 1)
    y_cols = jnp.concatenate([y_cols[:NB] - jnp.where(col_index == 1, sign, 0.0), y_cols[NB:]], 0)
    v_cols = mult(y_cols, coupling, 1, 1)
    u_cols = mult(z_cols, coupling)

    middle = mult(y_cols, z_cols, 0, 0)
    thin = cols // col_count
    sent = jnp.concatenate([z_cols.reshape(col_count, thin, NB), middle.reshape(col_count, step, NB)], 1)
    got = exchange(sent, "col")
    middle_piece = jnp.sum(got[:, thin:], 0)
    by_fold = got[:, :thin].reshape(fold, row_count, thin, NB)
    mine = lax.dynamic_index_in_dim(by_fold, row_index, 1, keepdims=False).reshape(fold * thin, NB)
    last = gather(jnp.concatenate([mine, middle_piece], 0), "col")
    middle = last[:, fold * thin :].reshape(NB, NB)
    z_rows = last[:, : fold * thin].reshape(col_count, fold, thin, NB).transpose(1, 0, 2, 3)
    z_rows = z_rows.reshape(fold, col_blocks, NB, NB).transpose(1, 0, 2, 3).reshape(rows, NB)

    inner = mult(mult(coupling, middle, 0, 0), coupling)
    u_cols = u_cols - mult(y_cols, inner)
    updated = local - mult(jnp.concatenate([y_rows, z_rows], 1), jnp.concatenate([u_cols, v_cols], 1), 1, 1)
    return updated.reshape(kernel.shape)


def solution(mesh):
    return jax.shard_map(
        body,
        mesh=mesh,
        in_specs=(P(None, "row", None, None, "col", None),),
        out_specs=P(None, "row", None, None, "col", None),
        check_vma=False,
    )
```

```python
import jax
import jax.numpy as jnp
from jax import lax
from jax.experimental import pallas as pl
from jax.experimental.pallas import tpu as pltpu
from jax.sharding import PartitionSpec as P

NB = 128
SUB = 8
VMEM = pl.BlockSpec(memory_space=pltpu.VMEM)
SMEM = pl.BlockSpec(memory_space=pltpu.SMEM)
PARAMS = pltpu.CompilerParams(vmem_limit_bytes=40 * 1024 * 1024)


def mult(left, right, left_dim=1, right_dim=0):
    return lax.dot_general(
        left,
        right,
        (((left_dim,), (right_dim,)), ((), ())),
        precision=lax.Precision.HIGHEST,
        preferred_element_type=jnp.float32,
    )


def shape(*dims):
    return jax.ShapeDtypeStruct(dims, jnp.float32)


def cost(flops, nbytes):
    return pl.CostEstimate(flops=flops, bytes_accessed=nbytes, transcendentals=0)


def lane(block, k):
    return jnp.broadcast_to(block[:, k : k + 1], (SUB, NB))


def row(block, s):
    return jnp.broadcast_to(block[s : s + 1, :], (SUB, NB))


def lane_ids():
    sub_id = lax.broadcasted_iota(jnp.int32, (SUB, NB), 0)
    lane_id = lax.broadcasted_iota(jnp.int32, (SUB, NB), 1)
    return sub_id, lane_id


def inverse_factor(left):
    count = NB // SUB
    sub_id, lane_id = lane_ids()
    eye = [jnp.where(lane_id == sub_id + SUB * i, 1.0, 0.0) for i in range(count)]
    right = list(eye)
    for k in range(0, NB, 2):
        b, s = divmod(k, SUB)
        one, two = row(left[b], s), row(left[b], s + 1)
        eone, etwo = row(right[b], s), row(right[b], s + 1)
        a11, a12, a22 = lane(one, k), lane(one, k + 1), lane(two, k + 1)
        scale = 1.0 / (a11 * a22 - a12 * a12)
        i11, i12, i22 = a22 * scale, a12 * scale, a11 * scale
        p1, p2 = i11 * one - i12 * two, i22 * two - i12 * one
        q1, q2 = i11 * eone - i12 * etwo, i22 * etwo - i12 * eone
        for i in range(b, count):
            c1, c2 = lane(left[i], k), lane(left[i], k + 1)
            if i == b:
                c1 = jnp.where(sub_id > s + 1, c1, 0.0)
                c2 = jnp.where(sub_id > s + 1, c2, 0.0)
            left[i] = left[i] - c1 * p1 - c2 * p2
            right[i] = right[i] - c1 * q1 - c2 * q2
    odd = (sub_id % 2) == 1
    out = []
    for i in range(count):
        diag = jnp.sum(left[i] * eye[i], axis=1, keepdims=True)
        below = jnp.sum(jnp.where(lane_id == sub_id + (SUB * i - 1), left[i], 0.0), axis=1, keepdims=True)
        diag, below = jnp.broadcast_to(diag, (SUB, NB)), jnp.broadcast_to(below, (SUB, NB))
        ratio = jnp.where(odd, below / pltpu.roll(diag, 1, 0), 0.0)
        rows = right[i] - ratio * pltpu.roll(right[i], 1, 0)
        out.append(rows * lax.rsqrt(diag - ratio * below))
    return out


def invert_kernel(shift_ref, out_ref):
    count = NB // SUB
    sub_id, lane_id = lane_ids()
    held = [
        jnp.where(lane_id == sub_id + SUB * i, 1.0, 0.0) - shift_ref[SUB * i : SUB * i + SUB, :] for i in range(count)
    ]
    for k in range(0, NB, 2):
        b, s = divmod(k, SUB)
        one, two = row(held[b], s), row(held[b], s + 1)
        a11, a12, a21, a22 = lane(one, k), lane(one, k + 1), lane(two, k), lane(two, k + 1)
        scale = 1.0 / (a11 * a22 - a12 * a21)
        i11, i12, i21, i22 = a22 * scale, -a12 * scale, -a21 * scale, a11 * scale
        h1, h2 = lane_id == k, lane_id == k + 1
        o1 = jnp.where(h1, 1.0, jnp.where(h2, 0.0, one))
        o2 = jnp.where(h1, 0.0, jnp.where(h2, 1.0, two))
        n1, n2 = i11 * o1 + i12 * o2, i21 * o1 + i22 * o2
        for i in range(count):
            c1, c2 = lane(held[i], k), lane(held[i], k + 1)
            new = jnp.where(h1 | h2, 0.0, held[i]) - c1 * n1 - c2 * n2
            if i == b:
                new = jnp.where(sub_id == s, n1, jnp.where(sub_id == s + 1, n2, new))
            held[i] = new
    for i in range(count):
        out_ref[SUB * i : SUB * i + SUB, :] = held[i]


def prepare_kernel(col_blocks, ids_ref, a_ref, send_ref, top_ref):
    rows = a_ref.shape[0] // col_blocks
    col_count, row_count = send_ref.shape[0], top_ref.shape[0]
    share, step = rows // col_count, NB // col_count
    panel = a_ref[pl.ds(0, rows, col_blocks), :]
    first = jnp.where(ids_ref[0] == 0, 0.0, panel[:NB])
    panel = jnp.concatenate([first, panel[NB:]], 0)
    gram = mult(panel, panel, 0, 0)
    lead = jnp.where(ids_ref[0] == 1, first, 0.0)
    send_ref[:, :share, :] = panel.reshape(col_count, share, NB)
    for c in range(col_count):
        send_ref[c, share : share + step, :] = gram[c * step : (c + 1) * step]
        send_ref[c, share + step : share + 2 * step, :] = lead[c * step : (c + 1) * step]
    thin = col_blocks * NB // row_count
    per = NB // thin
    for k in range(col_blocks):
        block = a_ref[pl.ds(k, NB, col_blocks), :].T
        if k == 0:
            block = jnp.where(ids_ref[1] == 0, 0.0, block)
        top_ref[k * per : (k + 1) * per] = block.reshape(per, thin, NB)


def factor_kernel(col_blocks, ids_ref, got_ref, a_ref, inv_ref, sign_ref, shift_ref, y_ref, part_ref, hold_ref, lead_ref):
    col_count = got_ref.shape[0]
    rows = a_ref.shape[0] // col_blocks
    share, step = rows // col_count, NB // col_count
    count = NB // SUB
    sub_id, lane_id = lane_ids()
    for c in range(col_count):
        hold_ref[c * step : (c + 1) * step, :] = got_ref[c, share : share + step, :]
        lead_ref[c * step : (c + 1) * step, :] = got_ref[c, share + step : share + 2 * step, :]
    out = inverse_factor([hold_ref[SUB * i : SUB * i + SUB, :] for i in range(count)])
    for i in range(count):
        inv_ref[SUB * i : SUB * i + SUB, :] = out[i]
    inverse = inv_ref[...]
    lead = lead_ref[...]
    signs = jnp.where(jnp.sum(lead * inverse, axis=1, keepdims=True) >= 0, -1.0, 1.0)
    shift_ref[...] = signs * mult(lead, inverse, 1, 1)
    for i in range(count):
        here = jnp.where(lane_id == sub_id + SUB * i, 1.0, 0.0)
        sign_ref[SUB * i : SUB * i + SUB, :] = here * signs[SUB * i : SUB * i + SUB]
    panel = got_ref[:, :share, :].reshape(rows, NB)
    y_ref[...] = mult(panel, inverse, 1, 1)

    @pl.when(ids_ref[0] == 1)
    def _():
        y_ref[:NB, :] = y_ref[:NB, :] - sign_ref[...]

    flipped = y_ref[...].T
    for k in range(col_blocks):
        part_ref[k * NB : (k + 1) * NB, :] = mult(flipped, a_ref[pl.ds(k, rows, col_blocks), :]).T


def middle_kernel(ids_ref, got_ref, inv_ref, sign_ref, y_ref, send_ref, hold_ref):
    row_count, both, _ = got_ref.shape
    thin = both // 2
    cols = row_count * thin
    col_count = send_ref.shape[0]
    step, share = NB // col_count, cols // col_count
    z = got_ref[:, :thin, :].reshape(cols, NB)
    y_ref[...] = mult(got_ref[:, thin:, :].reshape(cols, NB), inv_ref[...], 1, 1)

    @pl.when(ids_ref[1] == 1)
    def _():
        y_ref[:NB, :] = y_ref[:NB, :] - sign_ref[...]

    hold_ref[...] = mult(y_ref[...], z, 0, 0)
    send_ref[:, :share, :] = z.reshape(col_count, share, NB)
    for c in range(col_count):
        send_ref[c, share : share + step, :] = hold_ref[c * step : (c + 1) * step, :]
        if send_ref.shape[1] > share + step:
            send_ref[c, share + step :, :] = jnp.zeros((send_ref.shape[1] - share - step, NB), jnp.float32)


def columns_kernel(got_ref, y_ref, coupling_ref, u_ref, v_ref):
    row_count, both, _ = got_ref.shape
    z = got_ref[:, : both // 2, :].reshape(row_count * (both // 2), NB)
    v_ref[...] = mult(y_ref[...], coupling_ref[...])
    u_ref[...] = mult(z, coupling_ref[...], 1, 1)


def update_kernel(col_blocks, fold, got_ref, coupling_ref, u_ref, v_ref, y_col_ref, y_ref, a_ref, out_ref, right_ref, hold_ref):
    col_count = got_ref.shape[0]
    thin = col_blocks * NB // col_count
    step = NB // col_count
    per = NB // thin
    at = pl.program_id(0)

    @pl.when(at == 0)
    def _():
        for c in range(col_count):
            hold_ref[c * step : (c + 1) * step, :] = got_ref[c, fold * thin : fold * thin + step, :]
        coupling = coupling_ref[...]
        inner = mult(mult(coupling, hold_ref[...]), coupling, 1, 1)
        right_ref[:, :NB] = u_ref[...] - mult(y_col_ref[...], inner)
        right_ref[:, NB:] = v_ref[...]

    for f in range(fold):
        z = got_ref[pl.ds(at * per, per), f * thin : (f + 1) * thin, :].reshape(NB, NB)
        y = y_ref[f * NB : (f + 1) * NB, :]
        change = mult(jnp.concatenate([y, z], 1), right_ref[...], 1, 1)
        for k in range(col_blocks):
            here = pl.ds(f * NB * col_blocks + k, NB, col_blocks)
            out_ref[here, :] = a_ref[here, :] - change[:, k * NB : (k + 1) * NB]


def exchange(pieces, axis):
    return lax.all_to_all(pieces, axis, 0, 0)


def gather(piece, axis):
    count = lax.axis_size(axis)
    return exchange(jnp.broadcast_to(piece[None], (count,) + piece.shape), axis)


def body(kernel):
    row_blocks, _, _, col_blocks, _, _ = kernel.shape
    rows, cols = row_blocks * NB, col_blocks * NB
    row_count, col_count = lax.axis_size("row"), lax.axis_size("col")
    fold = col_count // row_count
    row_index, col_index = lax.axis_index("row"), lax.axis_index("col")
    ids = jnp.stack([row_index, col_index]).astype(jnp.int32)
    lines = kernel.reshape(rows * col_blocks, NB)
    share, step = rows // col_count, NB // col_count
    thin = cols // row_count
    slim = cols // col_count
    pad = pl.cdiv(step, SUB) * SUB

    send, top = pl.pallas_call(
        lambda *refs: prepare_kernel(col_blocks, *refs),
        out_shape=(shape(col_count, share + 2 * step, NB), shape(row_count, thin, NB)),
        in_specs=[SMEM, VMEM],
        out_specs=(VMEM, VMEM),
        compiler_params=PARAMS,
        name="prepare",
        cost_estimate=cost(2 * rows * NB * NB * 6, 3_000_000),
    )(ids, lines)
    got = exchange(send, "col")[0]
    panel_share, piece = got[:share], got[share:]
    got = exchange(jnp.concatenate([top, jnp.broadcast_to(piece[None], (row_count,) + piece.shape)], 1), "row")
    top_share = got[0, :thin]
    piece = jnp.sum(got[:, thin:], 0)
    got = gather(jnp.concatenate([panel_share, piece], 0), "col")

    inverse, sign, shift, y_rows, partial = pl.pallas_call(
        lambda *refs: factor_kernel(col_blocks, *refs),
        out_shape=(shape(NB, NB), shape(NB, NB), shape(NB, NB), shape(rows, NB), shape(cols, NB)),
        in_specs=[SMEM, VMEM, VMEM],
        out_specs=(VMEM,) * 5,
        scratch_shapes=[pltpu.VMEM((NB, NB), jnp.float32)] * 2,
        compiler_params=PARAMS,
        name="factor",
        cost_estimate=cost(2 * rows * cols * NB * 6, 4_000_000),
    )(ids, got, lines)

    got = exchange(partial.reshape(row_count, thin, NB), "row")
    coupling = pl.pallas_call(
        invert_kernel,
        out_shape=shape(NB, NB),
        in_specs=[VMEM],
        out_specs=VMEM,
        name="invert",
        cost_estimate=cost(4_000_000_000, 200_000),
    )(shift)
    got, coupling = lax.optimization_barrier((got, coupling))
    got = gather(jnp.concatenate([jnp.sum(got, 0), top_share], 0), "row")

    y_cols, send = pl.pallas_call(
        middle_kernel,
        out_shape=(shape(cols, NB), shape(col_count, slim + pad, NB)),
        in_specs=[SMEM, VMEM, VMEM, VMEM],
        out_specs=(VMEM, VMEM),
        scratch_shapes=[pltpu.VMEM((NB, NB), jnp.float32)],
        compiler_params=PARAMS,
        name="middle",
        cost_estimate=cost(4 * cols * NB * NB * 6, 2_000_000),
    )(ids, got, inverse, sign)
    back = exchange(send, "col")
    u_cols, v_cols = pl.pallas_call(
        columns_kernel,
        out_shape=(shape(cols, NB), shape(cols, NB)),
        in_specs=[VMEM] * 3,
        out_specs=(VMEM, VMEM),
        compiler_params=PARAMS,
        name="columns",
        cost_estimate=cost(4 * cols * NB * NB * 6, 2_000_000),
    )(got, y_cols, coupling)
    back, u_cols, v_cols = lax.optimization_barrier((back, u_cols, v_cols))
    by_fold = back[:, :slim].reshape(fold, row_count, slim, NB)
    mine = lax.dynamic_index_in_dim(by_fold, row_index, 1, keepdims=False).reshape(fold * slim, NB)
    last = gather(jnp.concatenate([mine, jnp.sum(back[:, slim:], 0)], 0), "col")

    whole = lambda *dims: pl.BlockSpec(dims, lambda i: (0,) * len(dims))
    updated = pl.pallas_call(
        lambda *refs: update_kernel(col_blocks, fold, *refs),
        grid=(row_blocks // fold,),
        out_shape=shape(rows * col_blocks, NB),
        in_specs=[
            whole(col_count, fold * slim + pad, NB),
            whole(NB, NB),
            whole(cols, NB),
            whole(cols, NB),
            whole(cols, NB),
            pl.BlockSpec((fold * NB, NB), lambda i: (i, 0)),
            pl.BlockSpec((fold * NB * col_blocks, NB), lambda i: (i, 0)),
        ],
        out_specs=pl.BlockSpec((fold * NB * col_blocks, NB), lambda i: (i, 0)),
        scratch_shapes=[pltpu.VMEM((cols, 2 * NB), jnp.float32), pltpu.VMEM((NB, NB), jnp.float32)],
        compiler_params=PARAMS,
        name="update",
        cost_estimate=cost(4 * rows * cols * NB * 6, 6_000_000),
    )(last, coupling, u_cols, v_cols, y_cols, y_rows, lines)
    return updated.reshape(kernel.shape)


def solution(mesh):
    return jax.shard_map(
        body,
        mesh=mesh,
        in_specs=(P(None, "row", None, None, "col", None),),
        out_specs=P(None, "row", None, None, "col", None),
        check_vma=False,
    )
```

```python
import jax
import jax.numpy as jnp
from jax import lax
from jax.experimental import pallas as pl
from jax.experimental.pallas import tpu as pltpu
from jax.sharding import PartitionSpec as P

NB = 128
SUB = 8
VMEM = pl.BlockSpec(memory_space=pltpu.VMEM)
SMEM = pl.BlockSpec(memory_space=pltpu.SMEM)
PARAMS = pltpu.CompilerParams(vmem_limit_bytes=40 * 1024 * 1024)


def mult(left, right, left_dim=1, right_dim=0):
    return lax.dot_general(
        left,
        right,
        (((left_dim,), (right_dim,)), ((), ())),
        precision=lax.Precision.HIGHEST,
        preferred_element_type=jnp.float32,
    )


def shape(*dims):
    return jax.ShapeDtypeStruct(dims, jnp.float32)


def cost(flops, nbytes):
    return pl.CostEstimate(flops=flops, bytes_accessed=nbytes, transcendentals=0)


def lane(block, k):
    return jnp.broadcast_to(block[:, k : k + 1], (SUB, NB))


def row(block, s):
    return jnp.broadcast_to(block[s : s + 1, :], (SUB, NB))


def lane_ids():
    sub_id = lax.broadcasted_iota(jnp.int32, (SUB, NB), 0)
    lane_id = lax.broadcasted_iota(jnp.int32, (SUB, NB), 1)
    return sub_id, lane_id


def inverse_factor(left):
    count = NB // SUB
    sub_id, lane_id = lane_ids()
    eye = [jnp.where(lane_id == sub_id + SUB * i, 1.0, 0.0) for i in range(count)]
    right = list(eye)
    for k in range(0, NB, 2):
        b, s = divmod(k, SUB)
        one, two = row(left[b], s), row(left[b], s + 1)
        eone, etwo = row(right[b], s), row(right[b], s + 1)
        a11, a12, a22 = lane(one, k), lane(one, k + 1), lane(two, k + 1)
        scale = 1.0 / (a11 * a22 - a12 * a12)
        i11, i12, i22 = a22 * scale, a12 * scale, a11 * scale
        p1, p2 = i11 * one - i12 * two, i22 * two - i12 * one
        q1, q2 = i11 * eone - i12 * etwo, i22 * etwo - i12 * eone
        for i in range(b, count):
            c1, c2 = lane(left[i], k), lane(left[i], k + 1)
            if i == b:
                c1 = jnp.where(sub_id > s + 1, c1, 0.0)
                c2 = jnp.where(sub_id > s + 1, c2, 0.0)
            left[i] = left[i] - c1 * p1 - c2 * p2
            right[i] = right[i] - c1 * q1 - c2 * q2
    odd = (sub_id % 2) == 1
    out = []
    for i in range(count):
        diag = jnp.sum(left[i] * eye[i], axis=1, keepdims=True)
        below = jnp.sum(jnp.where(lane_id == sub_id + (SUB * i - 1), left[i], 0.0), axis=1, keepdims=True)
        diag, below = jnp.broadcast_to(diag, (SUB, NB)), jnp.broadcast_to(below, (SUB, NB))
        ratio = jnp.where(odd, below / pltpu.roll(diag, 1, 0), 0.0)
        rows = right[i] - ratio * pltpu.roll(right[i], 1, 0)
        out.append(rows * lax.rsqrt(diag - ratio * below))
    return out


def invert_kernel(shift_ref, y_ref, out_ref, v_ref):
    count = NB // SUB
    sub_id, lane_id = lane_ids()
    held = [
        jnp.where(lane_id == sub_id + SUB * i, 1.0, 0.0) - shift_ref[SUB * i : SUB * i + SUB, :] for i in range(count)
    ]
    for k in range(0, NB, 2):
        b, s = divmod(k, SUB)
        one, two = row(held[b], s), row(held[b], s + 1)
        a11, a12, a21, a22 = lane(one, k), lane(one, k + 1), lane(two, k), lane(two, k + 1)
        scale = 1.0 / (a11 * a22 - a12 * a21)
        i11, i12, i21, i22 = a22 * scale, -a12 * scale, -a21 * scale, a11 * scale
        h1, h2 = lane_id == k, lane_id == k + 1
        o1 = jnp.where(h1, 1.0, jnp.where(h2, 0.0, one))
        o2 = jnp.where(h1, 0.0, jnp.where(h2, 1.0, two))
        n1, n2 = i11 * o1 + i12 * o2, i21 * o1 + i22 * o2
        for i in range(count):
            c1, c2 = lane(held[i], k), lane(held[i], k + 1)
            new = jnp.where(h1 | h2, 0.0, held[i]) - c1 * n1 - c2 * n2
            if i == b:
                new = jnp.where(sub_id == s, n1, jnp.where(sub_id == s + 1, n2, new))
            held[i] = new
    for i in range(count):
        out_ref[SUB * i : SUB * i + SUB, :] = held[i]
    v_ref[...] = mult(y_ref[...], out_ref[...])


def prepare_kernel(col_blocks, fold, slim, ids_ref, a_ref, send_ref):
    rows = a_ref.shape[0] // col_blocks
    col_count = send_ref.shape[0]
    share, step, per = fold * slim, NB // col_count, NB // slim
    panel = a_ref[pl.ds(0, rows, col_blocks), :]
    first = jnp.where(ids_ref[0] == 0, 0.0, panel[:NB])
    panel = jnp.concatenate([first, panel[NB:]], 0)
    gram = mult(panel, panel, 0, 0)
    lead = jnp.where(ids_ref[0] == 1, first, 0.0)
    for m in range(rows // NB):
        k, f = divmod(m, fold)
        send_ref[k * per : (k + 1) * per, f * slim : (f + 1) * slim, :] = panel[m * NB : (m + 1) * NB].reshape(per, slim, NB)
    for c in range(col_count):
        send_ref[c, share : share + step, :] = gram[c * step : (c + 1) * step]
        send_ref[c, share + step : share + 2 * step, :] = lead[c * step : (c + 1) * step]


def relay_kernel(fold, slim, ids_ref, got_ref, send_ref):
    row_count = got_ref.shape[0]
    share = fold * slim
    mine = got_ref[ids_ref[0], :share, :]
    piece = jnp.sum(got_ref[:, share:, :], 0)
    send_ref[:, :share, :] = jnp.broadcast_to(mine[None], (fold * row_count,) + mine.shape)
    send_ref[:, share + slim :, :] = jnp.broadcast_to(piece[None], (fold * row_count,) + piece.shape)
    for f in range(fold):
        send_ref[f * row_count : (f + 1) * row_count, share : share + slim, :] = got_ref[:, f * slim : (f + 1) * slim, :]


def factor_kernel(
    col_blocks, fold, slim, ids_ref, got_ref, a_ref, sign_shift_ref, y_ref, y_col_ref, send_ref, inv_ref, sign_ref, hold_ref, lead_ref
):
    col_count = got_ref.shape[0]
    rows, cols = a_ref.shape[0] // col_blocks, col_blocks * NB
    share, step, per = fold * slim, NB // col_count, NB // slim
    count = NB // SUB
    sub_id, lane_id = lane_ids()
    for c in range(col_count):
        hold_ref[c * step : (c + 1) * step, :] = got_ref[c, share + slim : share + slim + step, :]
        lead_ref[c * step : (c + 1) * step, :] = got_ref[c, share + slim + step : share + slim + 2 * step, :]
    out = inverse_factor([hold_ref[SUB * i : SUB * i + SUB, :] for i in range(count)])
    for i in range(count):
        inv_ref[SUB * i : SUB * i + SUB, :] = out[i]
    inverse = inv_ref[...]
    lead = lead_ref[...]
    signs = jnp.where(jnp.sum(lead * inverse, axis=1, keepdims=True) >= 0, -1.0, 1.0)
    sign_shift_ref[...] = signs * mult(lead, inverse, 1, 1)
    for i in range(count):
        here = jnp.where(lane_id == sub_id + SUB * i, 1.0, 0.0)
        sign_ref[SUB * i : SUB * i + SUB, :] = here * signs[SUB * i : SUB * i + SUB]
    y_col_ref[...] = mult(got_ref[:, share : share + slim, :].reshape(cols, NB), inverse, 1, 1)
    for m in range(rows // NB):
        k, f = divmod(m, fold)
        block = got_ref[k * per : (k + 1) * per, f * slim : (f + 1) * slim, :].reshape(NB, NB)
        y_ref[m * NB : (m + 1) * NB, :] = mult(block, inverse, 1, 1)

    @pl.when(ids_ref[0] == 1)
    def _():
        y_ref[:NB, :] = y_ref[:NB, :] - sign_ref[...]

    @pl.when(ids_ref[1] == 1)
    def _():
        y_col_ref[:NB, :] = y_col_ref[:NB, :] - sign_ref[...]

    part = jnp.zeros((rows, NB), jnp.float32)
    for k in range(col_blocks):
        part = part + mult(a_ref[pl.ds(k, rows, col_blocks), :], y_col_ref[k * NB : (k + 1) * NB, :])
    for m in range(rows // NB):
        k, f = divmod(m, fold)
        send_ref[k * per : (k + 1) * per, f * slim : (f + 1) * slim, :] = part[m * NB : (m + 1) * NB].reshape(per, slim, NB)
    hold_ref[...] = mult(y_ref[...], part, 0, 0)
    for c in range(col_count):
        send_ref[c, share : share + step, :] = hold_ref[c * step : (c + 1) * step, :]
        if send_ref.shape[1] > share + step:
            send_ref[c, share + step :, :] = jnp.zeros((send_ref.shape[1] - share - step, NB), jnp.float32)


def spread_kernel(got_ref, send_ref):
    total = jnp.sum(got_ref[...], 0)
    send_ref[...] = jnp.broadcast_to(total[None], send_ref.shape)


def update_kernel(col_blocks, fold, slim, got_ref, coupling_ref, v_ref, y_col_ref, y_ref, a_ref, out_ref, right_ref, hold_ref):
    col_count = got_ref.shape[0]
    share, step, per = fold * slim, NB // col_count, NB // slim
    at = pl.program_id(0)

    @pl.when(at == 0)
    def _():
        for c in range(col_count):
            hold_ref[c * step : (c + 1) * step, :] = got_ref[c, share + slim : share + slim + step, :]
        coupling = coupling_ref[...]
        inner = mult(mult(coupling, hold_ref[...]), coupling, 1, 1)
        z = got_ref[:, share : share + slim, :].reshape(col_blocks * NB, NB)
        right_ref[:, :NB] = mult(z, coupling, 1, 1) - mult(y_col_ref[...], inner)
        right_ref[:, NB:] = v_ref[...]

    for f in range(fold):
        z = got_ref[pl.ds(at * per, per), f * slim : (f + 1) * slim, :].reshape(NB, NB)
        y = y_ref[f * NB : (f + 1) * NB, :]
        change = mult(jnp.concatenate([y, z], 1), right_ref[...], 1, 1)
        for k in range(col_blocks):
            here = pl.ds(f * NB * col_blocks + k, NB, col_blocks)
            out_ref[here, :] = a_ref[here, :] - change[:, k * NB : (k + 1) * NB]


def exchange(pieces, axis):
    return lax.all_to_all(pieces, axis, 0, 0)


def body(kernel):
    row_blocks, _, _, col_blocks, _, _ = kernel.shape
    rows, cols = row_blocks * NB, col_blocks * NB
    row_count, col_count = lax.axis_size("row"), lax.axis_size("col")
    fold = col_count // row_count
    row_index, col_index = lax.axis_index("row"), lax.axis_index("col")
    ids = jnp.stack([row_index, col_index]).astype(jnp.int32)
    lines = kernel.reshape(rows * col_blocks, NB)
    slim, step = cols // col_count, NB // col_count
    share = fold * slim
    pad = 2 * step

    def relay(got):
        return pl.pallas_call(
            lambda *refs: relay_kernel(fold, slim, *refs),
            out_shape=shape(col_count, share + slim + pad, NB),
            in_specs=[SMEM, VMEM],
            out_specs=VMEM,
            compiler_params=PARAMS,
            name="relay",
            cost_estimate=cost(1_000_000, 1_000_000),
        )(ids, got)

    send = pl.pallas_call(
        lambda *refs: prepare_kernel(col_blocks, fold, slim, *refs),
        out_shape=shape(col_count, share + pad, NB),
        in_specs=[SMEM, VMEM],
        out_specs=VMEM,
        compiler_params=PARAMS,
        name="prepare",
        cost_estimate=cost(2 * rows * NB * NB * 6, 3_000_000),
    )(ids, lines)
    got = exchange(send, "col")[0]
    got = exchange(jnp.broadcast_to(got[None], (row_count,) + got.shape), "row")
    got = exchange(relay(got), "col")

    shift, y_rows, y_cols, send = pl.pallas_call(
        lambda *refs: factor_kernel(col_blocks, fold, slim, *refs),
        out_shape=(shape(NB, NB), shape(rows, NB), shape(cols, NB), shape(col_count, share + pad, NB)),
        in_specs=[SMEM, VMEM, VMEM],
        out_specs=(VMEM,) * 4,
        scratch_shapes=[pltpu.VMEM((NB, NB), jnp.float32)] * 4,
        compiler_params=PARAMS,
        name="factor",
        cost_estimate=cost(2 * rows * cols * NB * 6, 4_000_000),
    )(ids, got, lines)

    got = exchange(send, "col")
    send = pl.pallas_call(
        spread_kernel,
        out_shape=shape(row_count, share + pad, NB),
        in_specs=[VMEM],
        out_specs=VMEM,
        compiler_params=PARAMS,
        name="spread",
        cost_estimate=cost(1_000_000, 1_000_000),
    )(got)
    got = exchange(send, "row")
    coupling, v_cols = pl.pallas_call(
        invert_kernel,
        out_shape=(shape(NB, NB), shape(cols, NB)),
        in_specs=[VMEM, VMEM],
        out_specs=(VMEM, VMEM),
        compiler_params=PARAMS,
        name="invert",
        cost_estimate=cost(4_000_000_000, 1_000_000),
    )(shift, y_cols)
    got, coupling, v_cols = lax.optimization_barrier((got, coupling, v_cols))
    last = exchange(relay(got), "col")

    whole = lambda *dims: pl.BlockSpec(dims, lambda i: (0,) * len(dims))
    updated = pl.pallas_call(
        lambda *refs: update_kernel(col_blocks, fold, slim, *refs),
        grid=(row_blocks // fold,),
        out_shape=shape(rows * col_blocks, NB),
        in_specs=[
            whole(col_count, share + slim + pad, NB),
            whole(NB, NB),
            whole(cols, NB),
            whole(cols, NB),
            pl.BlockSpec((fold * NB, NB), lambda i: (i, 0)),
            pl.BlockSpec((fold * NB * col_blocks, NB), lambda i: (i, 0)),
        ],
        out_specs=pl.BlockSpec((fold * NB * col_blocks, NB), lambda i: (i, 0)),
        scratch_shapes=[pltpu.VMEM((cols, 2 * NB), jnp.float32), pltpu.VMEM((NB, NB), jnp.float32)],
        compiler_params=PARAMS,
        name="update",
        cost_estimate=cost(4 * rows * cols * NB * 6, 6_000_000),
    )(last, coupling, v_cols, y_cols, y_rows, lines)
    return updated.reshape(kernel.shape)


def solution(mesh):
    return jax.shard_map(
        body,
        mesh=mesh,
        in_specs=(P(None, "row", None, None, "col", None),),
        out_specs=P(None, "row", None, None, "col", None),
        check_vma=False,
    )
```

```python
import jax
import jax.numpy as jnp
from jax import lax
from jax.experimental import pallas as pl
from jax.experimental.pallas import tpu as pltpu
from jax.sharding import PartitionSpec as P

NB = 128
SUB = 8
VMEM = pl.BlockSpec(memory_space=pltpu.VMEM)
SMEM = pl.BlockSpec(memory_space=pltpu.SMEM)
PARAMS = pltpu.CompilerParams(vmem_limit_bytes=40 * 1024 * 1024)


def mult(left, right, left_dim=1, right_dim=0):
    return lax.dot_general(
        left,
        right,
        (((left_dim,), (right_dim,)), ((), ())),
        precision=lax.Precision.HIGHEST,
        preferred_element_type=jnp.float32,
    )


def shape(*dims):
    return jax.ShapeDtypeStruct(dims, jnp.float32)


def cost(flops, nbytes):
    return pl.CostEstimate(flops=flops, bytes_accessed=nbytes, transcendentals=0)


def lane(block, k):
    return jnp.broadcast_to(block[:, k : k + 1], (SUB, NB))


def row(block, s):
    return jnp.broadcast_to(block[s : s + 1, :], (SUB, NB))


def lane_ids():
    sub_id = lax.broadcasted_iota(jnp.int32, (SUB, NB), 0)
    lane_id = lax.broadcasted_iota(jnp.int32, (SUB, NB), 1)
    return sub_id, lane_id


def inverse_factor(left):
    count = NB // SUB
    sub_id, lane_id = lane_ids()
    eye = [jnp.where(lane_id == sub_id + SUB * i, 1.0, 0.0) for i in range(count)]
    right = list(eye)
    for k in range(0, NB, 2):
        b, s = divmod(k, SUB)
        one, two = row(left[b], s), row(left[b], s + 1)
        eone, etwo = row(right[b], s), row(right[b], s + 1)
        a11, a12, a22 = lane(one, k), lane(one, k + 1), lane(two, k + 1)
        scale = 1.0 / (a11 * a22 - a12 * a12)
        i11, i12, i22 = a22 * scale, a12 * scale, a11 * scale
        p1, p2 = i11 * one - i12 * two, i22 * two - i12 * one
        q1, q2 = i11 * eone - i12 * etwo, i22 * etwo - i12 * eone
        for i in range(b, count):
            c1, c2 = lane(left[i], k), lane(left[i], k + 1)
            if i == b:
                c1 = jnp.where(sub_id > s + 1, c1, 0.0)
                c2 = jnp.where(sub_id > s + 1, c2, 0.0)
            left[i] = left[i] - c1 * p1 - c2 * p2
            right[i] = right[i] - c1 * q1 - c2 * q2
    odd = (sub_id % 2) == 1
    out = []
    for i in range(count):
        diag = jnp.sum(left[i] * eye[i], axis=1, keepdims=True)
        below = jnp.sum(jnp.where(lane_id == sub_id + (SUB * i - 1), left[i], 0.0), axis=1, keepdims=True)
        diag, below = jnp.broadcast_to(diag, (SUB, NB)), jnp.broadcast_to(below, (SUB, NB))
        ratio = jnp.where(odd, below / pltpu.roll(diag, 1, 0), 0.0)
        rows = right[i] - ratio * pltpu.roll(right[i], 1, 0)
        out.append(rows * lax.rsqrt(diag - ratio * below))
    return out


def invert_kernel(shift_ref, y_ref, out_ref, v_ref):
    count = NB // SUB
    sub_id, lane_id = lane_ids()
    held = [
        jnp.where(lane_id == sub_id + SUB * i, 1.0, 0.0) - shift_ref[SUB * i : SUB * i + SUB, :] for i in range(count)
    ]
    for k in range(0, NB, 2):
        b, s = divmod(k, SUB)
        one, two = row(held[b], s), row(held[b], s + 1)
        a11, a12, a21, a22 = lane(one, k), lane(one, k + 1), lane(two, k), lane(two, k + 1)
        scale = 1.0 / (a11 * a22 - a12 * a21)
        i11, i12, i21, i22 = a22 * scale, -a12 * scale, -a21 * scale, a11 * scale
        h1, h2 = lane_id == k, lane_id == k + 1
        o1 = jnp.where(h1, 1.0, jnp.where(h2, 0.0, one))
        o2 = jnp.where(h1, 0.0, jnp.where(h2, 1.0, two))
        n1, n2 = i11 * o1 + i12 * o2, i21 * o1 + i22 * o2
        for i in range(count):
            c1, c2 = lane(held[i], k), lane(held[i], k + 1)
            new = jnp.where(h1 | h2, 0.0, held[i]) - c1 * n1 - c2 * n2
            if i == b:
                new = jnp.where(sub_id == s, n1, jnp.where(sub_id == s + 1, n2, new))
            held[i] = new
    for i in range(count):
        out_ref[SUB * i : SUB * i + SUB, :] = held[i]
    v_ref[...] = mult(y_ref[...], out_ref[...])


def prepare_kernel(col_blocks, fold, slim, ids_ref, a_ref, send_ref):
    rows = a_ref.shape[0] // col_blocks
    col_count = send_ref.shape[0]
    share, step, per = fold * slim, NB // col_count, NB // slim
    panel = a_ref[pl.ds(0, rows, col_blocks), :]
    first = jnp.where((ids_ref[0] == 0) & (ids_ref[1] == 0), 0.0, panel[:NB])
    panel = jnp.concatenate([first, panel[NB:]], 0)
    gram = mult(panel, panel, 0, 0)
    lead = jnp.where(ids_ref[0] == 1, first, 0.0)
    for m in range(rows // NB):
        k, f = divmod(m, fold)
        send_ref[k * per : (k + 1) * per, f * slim : (f + 1) * slim, :] = panel[m * NB : (m + 1) * NB].reshape(per, slim, NB)
    for c in range(col_count):
        send_ref[c, share : share + step, :] = gram[c * step : (c + 1) * step]
        send_ref[c, share + step : share + 2 * step, :] = lead[c * step : (c + 1) * step]


def relay_kernel(fold, slim, ids_ref, got_ref, send_ref):
    row_count = got_ref.shape[0]
    share = fold * slim
    mine = got_ref[ids_ref[0], :share, :]
    piece = jnp.sum(got_ref[:, share:, :], 0)
    send_ref[:, :share, :] = jnp.broadcast_to(mine[None], (fold * row_count,) + mine.shape)
    send_ref[:, share + slim :, :] = jnp.broadcast_to(piece[None], (fold * row_count,) + piece.shape)
    for f in range(fold):
        send_ref[f * row_count : (f + 1) * row_count, share : share + slim, :] = got_ref[:, f * slim : (f + 1) * slim, :]


def product_kernel(col_blocks, fold, slim, ids_ref, got_ref, a_ref, send_ref, panel_ref, hold_ref):
    col_count = got_ref.shape[0]
    rows, cols = a_ref.shape[0] // col_blocks, col_blocks * NB
    share, step, per = fold * slim, NB // col_count, NB // slim
    panel_cols = got_ref[:, share : share + slim, :].reshape(cols, NB)
    part = jnp.zeros((rows, NB), jnp.float32)
    for k in range(col_blocks):
        part = part + mult(a_ref[pl.ds(k, rows, col_blocks), :], panel_cols[k * NB : (k + 1) * NB])
    for m in range(rows // NB):
        k, f = divmod(m, fold)
        panel_ref[m * NB : (m + 1) * NB, :] = got_ref[k * per : (k + 1) * per, f * slim : (f + 1) * slim, :].reshape(NB, NB)
        send_ref[k * per : (k + 1) * per, f * slim : (f + 1) * slim, :] = part[m * NB : (m + 1) * NB].reshape(per, slim, NB)
    hold_ref[...] = mult(panel_ref[...], part, 0, 0)
    lead = jnp.where(ids_ref[0] == 1, part[:NB], 0.0)
    for c in range(col_count):
        send_ref[c, share : share + step, :] = hold_ref[c * step : (c + 1) * step, :]
        send_ref[c, share + step : share + 2 * step, :] = lead[c * step : (c + 1) * step]


def factor_kernel(col_blocks, fold, slim, ids_ref, got_ref, inv_ref, sign_ref, shift_ref, y_ref, y_col_ref, hold_ref, lead_ref):
    col_count = got_ref.shape[0]
    rows, cols = y_ref.shape[0], col_blocks * NB
    share, step, per = fold * slim, NB // col_count, NB // slim
    count = NB // SUB
    sub_id, lane_id = lane_ids()
    for c in range(col_count):
        hold_ref[c * step : (c + 1) * step, :] = got_ref[c, share + slim : share + slim + step, :]
        lead_ref[c * step : (c + 1) * step, :] = got_ref[c, share + slim + step : share + slim + 2 * step, :]
    out = inverse_factor([hold_ref[SUB * i : SUB * i + SUB, :] for i in range(count)])
    for i in range(count):
        inv_ref[SUB * i : SUB * i + SUB, :] = out[i]
    inverse = inv_ref[...]
    lead = lead_ref[...]
    signs = jnp.where(jnp.sum(lead * inverse, axis=1, keepdims=True) >= 0, -1.0, 1.0)
    shift_ref[...] = signs * mult(lead, inverse, 1, 1)
    for i in range(count):
        here = jnp.where(lane_id == sub_id + SUB * i, 1.0, 0.0)
        sign_ref[SUB * i : SUB * i + SUB, :] = here * signs[SUB * i : SUB * i + SUB]
    y_col_ref[...] = mult(got_ref[:, share : share + slim, :].reshape(cols, NB), inverse, 1, 1)
    for m in range(rows // NB):
        k, f = divmod(m, fold)
        block = got_ref[k * per : (k + 1) * per, f * slim : (f + 1) * slim, :].reshape(NB, NB)
        y_ref[m * NB : (m + 1) * NB, :] = mult(block, inverse, 1, 1)

    @pl.when(ids_ref[0] == 1)
    def _():
        y_ref[:NB, :] = y_ref[:NB, :] - sign_ref[...]

    @pl.when(ids_ref[1] == 1)
    def _():
        y_col_ref[:NB, :] = y_col_ref[:NB, :] - sign_ref[...]


def spread_kernel(share, step, ids_ref, got_ref, own_ref, inv_ref, sign_ref, send_ref):
    total = jnp.sum(got_ref[...], 0)
    own = own_ref[...]
    line = jnp.sum(sign_ref[...], axis=0, keepdims=True)
    turned = mult(total, inv_ref[...], 1, 1)
    rows = turned[:share] - own[:share] * line
    lead = jnp.where(ids_ref[0] == 1, turned[share + step :] - 0.5 * own[share + step :] * line, 0.0)
    out = jnp.concatenate([rows, total[share : share + step], lead], 0)
    send_ref[...] = jnp.broadcast_to(out[None], send_ref.shape)


def halves(value):
    high = value.astype(jnp.bfloat16)
    return high, (value - high.astype(jnp.float32)).astype(jnp.bfloat16)


def mult_half(left, right):
    return lax.dot_general(left, right, (((1,), (1,)), ((), ())), preferred_element_type=jnp.float32)


def update_kernel(
    col_blocks, fold, slim, got_ref, inv_ref, sign_ref, coupling_ref, v_ref, y_ref, a_ref, out_ref, high_ref, low_ref, hold_ref, lead_ref, new_ref, sems
):
    col_count = got_ref.shape[0]
    share, step, per = fold * slim, NB // col_count, NB // slim
    cols = col_blocks * NB
    for c in range(col_count):
        hold_ref[c * step : (c + 1) * step, :] = got_ref[c, share + slim : share + slim + step, :]
        lead_ref[c * step : (c + 1) * step, :] = got_ref[c, share + slim + step : share + slim + 2 * step, :]
    inverse, v = inv_ref[...], v_ref[...]
    cross = jnp.sum(sign_ref[...], axis=1, keepdims=True) * lead_ref[...]
    middle = mult(mult(inverse, hold_ref[...]), inverse, 1, 1) - cross - cross.T
    z_cols = got_ref[:, share : share + slim, :].reshape(cols, NB)
    u = mult(z_cols - mult(v, middle), coupling_ref[...], 1, 1)
    for at, part in enumerate((u, v)):
        high, low = halves(part)
        high_ref[:, at * NB : (at + 1) * NB] = high
        low_ref[:, at * NB : (at + 1) * NB] = low
    right_high, right_low = high_ref[...], low_ref[...]
    copies = []
    for m in range(y_ref.shape[0] // NB):
        k, f = divmod(m, fold)
        z = got_ref[k * per : (k + 1) * per, f * slim : (f + 1) * slim, :].reshape(NB, NB)
        high, low = halves(jnp.concatenate([y_ref[m * NB : (m + 1) * NB, :], z], 1))
        change = mult_half(low, right_high) + mult_half(high, right_low) + mult_half(high, right_high)
        for n in range(col_blocks):
            here = pl.ds(m * NB * col_blocks + n, NB, col_blocks)
            new_ref[here, :] = a_ref[here, :] - change[:, n * NB : (n + 1) * NB]
        there = pl.ds(m * NB * col_blocks, NB * col_blocks)
        copy = pltpu.make_async_copy(new_ref.at[there, :], out_ref.at[there, :], sems.at[m])
        copy.start()
        copies.append(copy)
    for copy in copies:
        copy.wait()


def exchange(pieces, axis):
    return lax.all_to_all(pieces, axis, 0, 0)


def body(kernel):
    row_blocks, _, _, col_blocks, _, _ = kernel.shape
    rows, cols = row_blocks * NB, col_blocks * NB
    row_count, col_count = lax.axis_size("row"), lax.axis_size("col")
    fold = col_count // row_count
    row_index, col_index = lax.axis_index("row"), lax.axis_index("col")
    ids = jnp.stack([row_index, col_index]).astype(jnp.int32)
    lines = kernel.reshape(rows * col_blocks, NB)
    slim, step = cols // col_count, NB // col_count
    share = fold * slim
    pad = 2 * step

    def relay(got):
        return pl.pallas_call(
            lambda *refs: relay_kernel(fold, slim, *refs),
            out_shape=shape(col_count, share + slim + pad, NB),
            in_specs=[SMEM, VMEM],
            out_specs=VMEM,
            compiler_params=PARAMS,
            name="relay",
            cost_estimate=cost(1_000_000, 1_000_000),
        )(ids, got)

    send = pl.pallas_call(
        lambda *refs: prepare_kernel(col_blocks, fold, slim, *refs),
        out_shape=shape(col_count, share + pad, NB),
        in_specs=[SMEM, VMEM],
        out_specs=VMEM,
        compiler_params=PARAMS,
        name="prepare",
        cost_estimate=cost(2 * rows * NB * NB * 6, 3_000_000),
    )(ids, lines)
    got = exchange(send, "col")
    own = got[1]
    got = jnp.broadcast_to(got[0][None], (row_count,) + got.shape[1:])
    got = exchange(relay(exchange(got, "row")), "col")

    send = pl.pallas_call(
        lambda *refs: product_kernel(col_blocks, fold, slim, *refs),
        out_shape=shape(col_count, share + pad, NB),
        in_specs=[SMEM, VMEM, VMEM],
        out_specs=VMEM,
        scratch_shapes=[pltpu.VMEM((rows, NB), jnp.float32), pltpu.VMEM((NB, NB), jnp.float32)],
        compiler_params=PARAMS,
        name="product",
        cost_estimate=cost(2 * rows * cols * NB * 6, 4_000_000),
    )(ids, got, lines)
    summed = exchange(send, "col")
    inverse, sign, shift, y_rows, y_cols = pl.pallas_call(
        lambda *refs: factor_kernel(col_blocks, fold, slim, *refs),
        out_shape=(shape(NB, NB), shape(NB, NB), shape(NB, NB), shape(rows, NB), shape(cols, NB)),
        in_specs=[SMEM, VMEM],
        out_specs=(VMEM,) * 5,
        scratch_shapes=[pltpu.VMEM((NB, NB), jnp.float32)] * 2,
        compiler_params=PARAMS,
        name="factor",
        cost_estimate=cost(4_000_000_000, 2_000_000),
    )(ids, got)

    send = pl.pallas_call(
        lambda *refs: spread_kernel(share, step, *refs),
        out_shape=shape(row_count, share + pad, NB),
        in_specs=[SMEM] + [VMEM] * 4,
        out_specs=VMEM,
        compiler_params=PARAMS,
        name="spread",
        cost_estimate=cost(10_000_000, 1_000_000),
    )(ids, summed, own, inverse, sign)
    got = exchange(send, "row")
    coupling, v_cols = pl.pallas_call(
        invert_kernel,
        out_shape=(shape(NB, NB), shape(cols, NB)),
        in_specs=[VMEM, VMEM],
        out_specs=(VMEM, VMEM),
        compiler_params=PARAMS,
        name="invert",
        cost_estimate=cost(4_000_000_000, 1_000_000),
    )(shift, y_cols)
    got, coupling, v_cols = lax.optimization_barrier((got, coupling, v_cols))
    last = exchange(relay(got), "col")

    updated = pl.pallas_call(
        lambda *refs: update_kernel(col_blocks, fold, slim, *refs),
        out_shape=shape(rows * col_blocks, NB),
        in_specs=[VMEM] * 7,
        out_specs=pl.BlockSpec(memory_space=pl.ANY),
        scratch_shapes=[
            pltpu.VMEM((cols, 2 * NB), jnp.bfloat16),
            pltpu.VMEM((cols, 2 * NB), jnp.bfloat16),
            pltpu.VMEM((NB, NB), jnp.float32),
            pltpu.VMEM((NB, NB), jnp.float32),
            pltpu.VMEM((rows * col_blocks, NB), jnp.float32),
            pltpu.SemaphoreType.DMA((row_blocks,)),
        ],
        compiler_params=PARAMS,
        name="update",
        cost_estimate=cost(4 * rows * cols * NB * 6, 6_000_000),
    )(last, inverse, sign, coupling, v_cols, y_rows, lines)
    return updated.reshape(kernel.shape)


def solution(mesh):
    return jax.shard_map(
        body,
        mesh=mesh,
        in_specs=(P(None, "row", None, None, "col", None),),
        out_specs=P(None, "row", None, None, "col", None),
        check_vma=False,
    )
```

```python
import jax
import jax.numpy as jnp
from jax import lax
from jax.experimental import pallas as pl
from jax.experimental.pallas import tpu as pltpu
from jax.sharding import PartitionSpec as P

NB = 128
SUB = 8
VMEM = pl.BlockSpec(memory_space=pltpu.VMEM)
SMEM = pl.BlockSpec(memory_space=pltpu.SMEM)
HBM = pl.BlockSpec(memory_space=pltpu.HBM)
PARAMS = pltpu.CompilerParams(vmem_limit_bytes=40 * 1024 * 1024)


def mult(left, right, left_dim=1, right_dim=0):
    return lax.dot_general(
        left,
        right,
        (((left_dim,), (right_dim,)), ((), ())),
        precision=lax.Precision.HIGHEST,
        preferred_element_type=jnp.float32,
    )


def shape(*dims):
    return jax.ShapeDtypeStruct(dims, jnp.float32)


def cost(flops, nbytes):
    return pl.CostEstimate(flops=flops, bytes_accessed=nbytes, transcendentals=0)


def lane(block, k):
    return jnp.broadcast_to(block[:, k : k + 1], (SUB, NB))


def row(block, s):
    return jnp.broadcast_to(block[s : s + 1, :], (SUB, NB))


def lane_ids():
    sub_id = lax.broadcasted_iota(jnp.int32, (SUB, NB), 0)
    lane_id = lax.broadcasted_iota(jnp.int32, (SUB, NB), 1)
    return sub_id, lane_id


def inverse_factor(left):
    count = NB // SUB
    sub_id, lane_id = lane_ids()
    eye = [jnp.where(lane_id == sub_id + SUB * i, 1.0, 0.0) for i in range(count)]
    right = list(eye)
    for k in range(0, NB, 4):
        b, s = divmod(k, SUB)
        r = [row(left[b], s + j) for j in range(4)]
        e = [row(right[b], s + j) for j in range(4)]
        a = [[lane(r[i], k + j) if j >= i else None for j in range(4)] for i in range(4)]
        scale = 1.0 / (a[0][0] * a[1][1] - a[0][1] * a[0][1])
        i00, i01, i11 = a[1][1] * scale, -a[0][1] * scale, a[0][0] * scale
        t = [(i00 * a[0][j] + i01 * a[1][j], i01 * a[0][j] + i11 * a[1][j]) for j in (2, 3)]
        s22 = a[2][2] - t[0][0] * a[0][2] - t[0][1] * a[1][2]
        s23 = a[2][3] - t[0][0] * a[0][3] - t[0][1] * a[1][3]
        s33 = a[3][3] - t[1][0] * a[0][3] - t[1][1] * a[1][3]
        scale = 1.0 / (s22 * s33 - s23 * s23)
        j22, j23, j33 = s33 * scale, -s23 * scale, s22 * scale

        def rank(x):
            x2 = x[2] - t[0][0] * x[0] - t[0][1] * x[1]
            x3 = x[3] - t[1][0] * x[0] - t[1][1] * x[1]
            q2, q3 = j22 * x2 + j23 * x3, j23 * x2 + j33 * x3
            u0 = i00 * x[0] + i01 * x[1] - t[0][0] * q2 - t[1][0] * q3
            u1 = i01 * x[0] + i11 * x[1] - t[0][1] * q2 - t[1][1] * q3
            return x2, x3, (u0, u1, q2, q3)

        l2, l3, lu = rank(r)
        e2, e3, eu = rank(e)
        for i in range(b, count):
            c = [lane(left[i], k + j) for j in range(4)]
            if i == b:
                c = [jnp.where(sub_id > s + 3, x, 0.0) for x in c]
            left[i] = left[i] - (c[0] * lu[0] + c[1] * lu[1]) - (c[2] * lu[2] + c[3] * lu[3])
            right[i] = right[i] - (c[0] * eu[0] + c[1] * eu[1]) - (c[2] * eu[2] + c[3] * eu[3])
        left[b] = jnp.where(sub_id == s + 2, l2, jnp.where(sub_id == s + 3, l3, left[b]))
        right[b] = jnp.where(sub_id == s + 2, e2, jnp.where(sub_id == s + 3, e3, right[b]))
    odd = (sub_id % 2) == 1
    out = []
    for i in range(count):
        diag = jnp.sum(left[i] * eye[i], axis=1, keepdims=True)
        below = jnp.sum(jnp.where(lane_id == sub_id + (SUB * i - 1), left[i], 0.0), axis=1, keepdims=True)
        diag, below = jnp.broadcast_to(diag, (SUB, NB)), jnp.broadcast_to(below, (SUB, NB))
        ratio = jnp.where(odd, below / pltpu.roll(diag, 1, 0), 0.0)
        rows = right[i] - ratio * pltpu.roll(right[i], 1, 0)
        out.append(rows * lax.rsqrt(diag - ratio * below))
    return out


def fetch(copies):
    for copy in copies:
        copy.start()
    for copy in copies:
        copy.wait()


def invert_kernel(rows, cols, ids_ref, state_hbm, panel_hbm, pack_ref, state_ref, panel_ref, sems):
    get_state = pltpu.make_async_copy(state_hbm, state_ref, sems.at[0])
    get_panel = pltpu.make_async_copy(panel_hbm, panel_ref, sems.at[1])
    get_state.start()
    get_panel.start()
    get_state.wait()
    count = NB // SUB
    sub_id, lane_id = lane_ids()
    held = [
        jnp.where(lane_id == sub_id + SUB * i, 1.0, 0.0) - state_ref[2 * NB + SUB * i : 2 * NB + SUB * i + SUB, :] for i in range(count)
    ]
    for k in range(0, NB, 2):
        b, s = divmod(k, SUB)
        one, two = row(held[b], s), row(held[b], s + 1)
        a11, a12, a21, a22 = lane(one, k), lane(one, k + 1), lane(two, k), lane(two, k + 1)
        scale = 1.0 / (a11 * a22 - a12 * a21)
        i11, i12, i21, i22 = a22 * scale, -a12 * scale, -a21 * scale, a11 * scale
        h1, h2 = lane_id == k, lane_id == k + 1
        o1 = jnp.where(h1, 1.0, jnp.where(h2, 0.0, one))
        o2 = jnp.where(h1, 0.0, jnp.where(h2, 1.0, two))
        n1, n2 = i11 * o1 + i12 * o2, i21 * o1 + i22 * o2
        for i in range(count):
            c1, c2 = lane(held[i], k), lane(held[i], k + 1)
            new = jnp.where(h1 | h2, 0.0, held[i]) - c1 * n1 - c2 * n2
            if i == b:
                new = jnp.where(sub_id == s, n1, jnp.where(sub_id == s + 1, n2, new))
            held[i] = new
    for i in range(count):
        pack_ref[SUB * i : SUB * i + SUB, :] = held[i]
    pack_ref[NB : 3 * NB, :] = state_ref[: 2 * NB, :]
    get_panel.wait()
    inverse, sign = state_ref[:NB, :], state_ref[NB : 2 * NB, :]
    y = mult(panel_ref[...], inverse, 1, 1)
    y_cols = jnp.concatenate([y[rows : rows + NB] - jnp.where(ids_ref[1] == 1, sign, 0.0), y[rows + NB :]], 0)
    pack_ref[3 * NB : 3 * NB + cols, :] = mult(y_cols, pack_ref[:NB, :])
    pack_ref[3 * NB + cols : 4 * NB + cols, :] = y[:NB] - jnp.where(ids_ref[0] == 1, sign, 0.0)
    pack_ref[4 * NB + cols :, :] = y[NB:rows]


def prepare_kernel(col_blocks, fold, slim, ids_ref, a_ref, send_ref):
    rows = a_ref.shape[0] // col_blocks
    col_count = send_ref.shape[0]
    share, step, per = fold * slim, NB // col_count, NB // slim
    panel = a_ref[pl.ds(0, rows, col_blocks), :]
    first = jnp.where((ids_ref[0] == 0) & (ids_ref[1] == 0), 0.0, panel[:NB])
    panel = jnp.concatenate([first, panel[NB:]], 0)
    gram = mult(panel, panel, 0, 0)
    lead = jnp.where(ids_ref[0] == 1, first, 0.0)
    for m in range(rows // NB):
        k, f = divmod(m, fold)
        send_ref[k * per : (k + 1) * per, f * slim : (f + 1) * slim, :] = panel[m * NB : (m + 1) * NB].reshape(per, slim, NB)
    for c in range(col_count):
        send_ref[c, share : share + step, :] = gram[c * step : (c + 1) * step]
        send_ref[c, share + step : share + 2 * step, :] = lead[c * step : (c + 1) * step]


def relay_kernel(fold, slim, ids_ref, got_ref, send_ref):
    row_count = got_ref.shape[0]
    share = fold * slim
    mine = got_ref[ids_ref[0], :share, :]
    piece = jnp.sum(got_ref[:, share:, :], 0)
    send_ref[:, :share, :] = jnp.broadcast_to(mine[None], (fold * row_count,) + mine.shape)
    send_ref[:, share + slim :, :] = jnp.broadcast_to(piece[None], (fold * row_count,) + piece.shape)
    for f in range(fold):
        send_ref[f * row_count : (f + 1) * row_count, share : share + slim, :] = got_ref[:, f * slim : (f + 1) * slim, :]


def product_kernel(col_blocks, fold, slim, ids_ref, got_ref, a_ref, send_hbm, panel_hbm, send_ref, panel_ref, hold_ref, sems):
    col_count = got_ref.shape[0]
    rows, cols = a_ref.shape[0] // col_blocks, col_blocks * NB
    share, step, per = fold * slim, NB // col_count, NB // slim
    panel_ref[rows:, :] = got_ref[:, share : share + slim, :].reshape(cols, NB)
    for m in range(rows // NB):
        k, f = divmod(m, fold)
        panel_ref[m * NB : (m + 1) * NB, :] = got_ref[k * per : (k + 1) * per, f * slim : (f + 1) * slim, :].reshape(NB, NB)
    put_panel = pltpu.make_async_copy(panel_ref, panel_hbm, sems.at[0])
    put_panel.start()
    part = jnp.zeros((rows, NB), jnp.float32)
    for k in range(col_blocks):
        part = part + mult(a_ref[pl.ds(k, rows, col_blocks), :], panel_ref[rows + k * NB : rows + (k + 1) * NB, :])
    for m in range(rows // NB):
        k, f = divmod(m, fold)
        send_ref[k * per : (k + 1) * per, f * slim : (f + 1) * slim, :] = part[m * NB : (m + 1) * NB].reshape(per, slim, NB)
    put_share = pltpu.make_async_copy(send_ref.at[:, :share, :], send_hbm.at[:, :share, :], sems.at[1])
    put_share.start()
    hold_ref[...] = mult(panel_ref[:rows, :], part, 0, 0)
    lead = jnp.where(ids_ref[0] == 1, part[:NB], 0.0)
    for c in range(col_count):
        send_ref[c, share : share + step, :] = hold_ref[c * step : (c + 1) * step, :]
        send_ref[c, share + step : share + 2 * step, :] = lead[c * step : (c + 1) * step]
    put_piece = pltpu.make_async_copy(send_ref.at[:, share:, :], send_hbm.at[:, share:, :], sems.at[2])
    put_piece.start()
    put_panel.wait()
    put_share.wait()
    put_piece.wait()


def factor_kernel(share, step, got_ref, state_hbm, state_ref, hold_ref, lead_ref, sem):
    count = NB // SUB
    sub_id, lane_id = lane_ids()
    for c in range(got_ref.shape[0]):
        hold_ref[c * step : (c + 1) * step, :] = got_ref[c, share : share + step, :]
        lead_ref[c * step : (c + 1) * step, :] = got_ref[c, share + step : share + 2 * step, :]
    out = inverse_factor([hold_ref[SUB * i : SUB * i + SUB, :] for i in range(count)])
    for i in range(count):
        state_ref[SUB * i : SUB * i + SUB, :] = out[i]
    inverse = state_ref[:NB, :]
    lead = lead_ref[...]
    signs = jnp.where(jnp.sum(lead * inverse, axis=1, keepdims=True) >= 0, -1.0, 1.0)
    state_ref[2 * NB :, :] = signs * mult(lead, inverse, 1, 1)
    for i in range(count):
        here = jnp.where(lane_id == sub_id + SUB * i, 1.0, 0.0)
        state_ref[NB + SUB * i : NB + SUB * i + SUB, :] = here * signs[SUB * i : SUB * i + SUB]
    fetch([pltpu.make_async_copy(state_ref, state_hbm, sem)])


def spread_kernel(share, step, ids_ref, got_hbm, own_hbm, state_hbm, send_ref, got_ref, own_ref, state_ref, sems):
    fetch(
        [
            pltpu.make_async_copy(got_hbm, got_ref, sems.at[0]),
            pltpu.make_async_copy(own_hbm, own_ref, sems.at[1]),
            pltpu.make_async_copy(state_hbm.at[: 2 * NB, :], state_ref, sems.at[2]),
        ]
    )
    total = jnp.sum(got_ref[...], 0)
    own = own_ref[...]
    line = jnp.sum(state_ref[NB:, :], axis=0, keepdims=True)
    turned = mult(total, state_ref[:NB, :], 1, 1)
    rows = turned[:share] - own[:share] * line
    lead = jnp.where(ids_ref[0] == 1, turned[share + step :] - 0.5 * own[share + step :] * line, 0.0)
    out = jnp.concatenate([rows, total[share : share + step], lead], 0)
    send_ref[...] = jnp.broadcast_to(out[None], send_ref.shape)


def halves(value):
    high = value.astype(jnp.bfloat16)
    return high, (value - high.astype(jnp.float32)).astype(jnp.bfloat16)


def mult_half(left, right):
    return lax.dot_general(left, right, (((1,), (1,)), ((), ())), preferred_element_type=jnp.float32)


def update_kernel(
    col_blocks, fold, slim, got_ref, pack_ref, a_ref, out_ref, high_ref, low_ref, hold_ref, lead_ref, new_ref, sems
):
    col_count = got_ref.shape[0]
    share, step, per = fold * slim, NB // col_count, NB // slim
    cols = col_blocks * NB
    for c in range(col_count):
        hold_ref[c * step : (c + 1) * step, :] = got_ref[c, share + slim : share + slim + step, :]
        lead_ref[c * step : (c + 1) * step, :] = got_ref[c, share + slim + step : share + slim + 2 * step, :]
    coupling, inverse, v = pack_ref[:NB, :], pack_ref[NB : 2 * NB, :], pack_ref[3 * NB : 3 * NB + cols, :]
    y_ref = pack_ref.at[3 * NB + cols :, :]
    cross = jnp.sum(pack_ref[2 * NB : 3 * NB, :], axis=1, keepdims=True) * lead_ref[...]
    middle = mult(mult(inverse, hold_ref[...]), inverse, 1, 1) - cross - cross.T
    z_cols = got_ref[:, share : share + slim, :].reshape(cols, NB)
    u = mult(z_cols - mult(v, middle), coupling, 1, 1)
    for at, part in enumerate((u, v)):
        high, low = halves(part)
        high_ref[:, at * NB : (at + 1) * NB] = high
        low_ref[:, at * NB : (at + 1) * NB] = low
    right_high, right_low = high_ref[...], low_ref[...]
    copies = []
    for m in range(a_ref.shape[0] // cols):
        k, f = divmod(m, fold)
        z = got_ref[k * per : (k + 1) * per, f * slim : (f + 1) * slim, :].reshape(NB, NB)
        high, low = halves(jnp.concatenate([y_ref[m * NB : (m + 1) * NB, :], z], 1))
        change = mult_half(low, right_high) + mult_half(high, right_low) + mult_half(high, right_high)
        for n in range(col_blocks):
            here = pl.ds(m * NB * col_blocks + n, NB, col_blocks)
            new_ref[here, :] = a_ref[here, :] - change[:, n * NB : (n + 1) * NB]
        there = pl.ds(m * NB * col_blocks, NB * col_blocks)
        copy = pltpu.make_async_copy(new_ref.at[there, :], out_ref.at[there, :], sems.at[m])
        copy.start()
        copies.append(copy)
    for copy in copies:
        copy.wait()


def exchange(pieces, axis):
    return lax.all_to_all(pieces, axis, 0, 0)


def body(kernel):
    row_blocks, _, _, col_blocks, _, _ = kernel.shape
    rows, cols = row_blocks * NB, col_blocks * NB
    row_count, col_count = lax.axis_size("row"), lax.axis_size("col")
    fold = col_count // row_count
    row_index, col_index = lax.axis_index("row"), lax.axis_index("col")
    ids = jnp.stack([row_index, col_index]).astype(jnp.int32)
    lines = kernel.reshape(rows * col_blocks, NB)
    slim, step = cols // col_count, NB // col_count
    share = fold * slim
    pad = 2 * step

    def relay(got):
        return pl.pallas_call(
            lambda *refs: relay_kernel(fold, slim, *refs),
            out_shape=shape(col_count, share + slim + pad, NB),
            in_specs=[SMEM, VMEM],
            out_specs=VMEM,
            compiler_params=PARAMS,
            name="relay",
            cost_estimate=cost(1_000_000, 1_000_000),
        )(ids, got)

    send = pl.pallas_call(
        lambda *refs: prepare_kernel(col_blocks, fold, slim, *refs),
        out_shape=shape(col_count, share + pad, NB),
        in_specs=[SMEM, VMEM],
        out_specs=VMEM,
        compiler_params=PARAMS,
        name="prepare",
        cost_estimate=cost(2 * rows * NB * NB * 6, 3_000_000),
    )(ids, lines)
    got = exchange(send, "col")
    own = got[1]
    got = jnp.broadcast_to(got[0][None], (row_count,) + got.shape[1:])
    got = exchange(relay(exchange(got, "row")), "col")

    send, panel = pl.pallas_call(
        lambda *refs: product_kernel(col_blocks, fold, slim, *refs),
        out_shape=(shape(col_count, share + pad, NB), shape(rows + cols, NB)),
        in_specs=[SMEM, VMEM, VMEM],
        out_specs=(HBM, HBM),
        scratch_shapes=[
            pltpu.VMEM((col_count, share + pad, NB), jnp.float32),
            pltpu.VMEM((rows + cols, NB), jnp.float32),
            pltpu.VMEM((NB, NB), jnp.float32),
            pltpu.SemaphoreType.DMA((3,)),
        ],
        compiler_params=PARAMS,
        name="product",
        cost_estimate=cost(2 * rows * cols * NB * 6, 4_000_000),
    )(ids, got, lines)
    summed = exchange(send, "col")
    state = pl.pallas_call(
        lambda *refs: factor_kernel(share + slim, step, *refs),
        out_shape=shape(3 * NB, NB),
        in_specs=[VMEM],
        out_specs=HBM,
        scratch_shapes=[pltpu.VMEM((3 * NB, NB), jnp.float32)]
        + [pltpu.VMEM((NB, NB), jnp.float32)] * 2
        + [pltpu.SemaphoreType.DMA],
        compiler_params=PARAMS,
        name="factor",
        cost_estimate=cost(4_000_000_000, 2_000_000),
    )(got)

    send = pl.pallas_call(
        lambda *refs: spread_kernel(share, step, *refs),
        out_shape=shape(row_count, share + pad, NB),
        in_specs=[SMEM, HBM, HBM, HBM],
        out_specs=VMEM,
        scratch_shapes=[
            pltpu.VMEM((col_count, share + pad, NB), jnp.float32),
            pltpu.VMEM((share + pad, NB), jnp.float32),
            pltpu.VMEM((2 * NB, NB), jnp.float32),
            pltpu.SemaphoreType.DMA((3,)),
        ],
        compiler_params=PARAMS,
        name="spread",
        cost_estimate=cost(10_000_000, 1_000_000),
    )(ids, summed, own, state)
    got = exchange(send, "row")
    pack = pl.pallas_call(
        lambda *refs: invert_kernel(rows, cols, *refs),
        out_shape=shape(3 * NB + cols + rows, NB),
        in_specs=[SMEM, HBM, HBM],
        out_specs=VMEM,
        scratch_shapes=[
            pltpu.VMEM((3 * NB, NB), jnp.float32),
            pltpu.VMEM((rows + cols, NB), jnp.float32),
            pltpu.SemaphoreType.DMA((2,)),
        ],
        compiler_params=PARAMS,
        name="invert",
        cost_estimate=cost(4_000_000_000, 1_000_000),
    )(ids, state, panel)
    got, pack = lax.optimization_barrier((got, pack))
    last = exchange(relay(got), "col")

    updated = pl.pallas_call(
        lambda *refs: update_kernel(col_blocks, fold, slim, *refs),
        out_shape=shape(rows * col_blocks, NB),
        in_specs=[VMEM] * 3,
        out_specs=pl.BlockSpec(memory_space=pl.ANY),
        scratch_shapes=[
            pltpu.VMEM((cols, 2 * NB), jnp.bfloat16),
            pltpu.VMEM((cols, 2 * NB), jnp.bfloat16),
            pltpu.VMEM((NB, NB), jnp.float32),
            pltpu.VMEM((NB, NB), jnp.float32),
            pltpu.VMEM((rows * col_blocks, NB), jnp.float32),
            pltpu.SemaphoreType.DMA((row_blocks,)),
        ],
        compiler_params=PARAMS,
        name="update",
        cost_estimate=cost(4 * rows * cols * NB * 6, 6_000_000),
    )(last, pack, lines)
    return updated.reshape(kernel.shape)


def solution(mesh):
    return jax.shard_map(
        body,
        mesh=mesh,
        in_specs=(P(None, "row", None, None, "col", None),),
        out_specs=P(None, "row", None, None, "col", None),
        check_vma=False,
    )
```

```python
import jax
import jax.numpy as jnp
from jax import lax
from jax.experimental import pallas as pl
from jax.experimental.pallas import tpu as pltpu
from jax.sharding import PartitionSpec as P

NB = 128
SUB = 8
VMEM = pl.BlockSpec(memory_space=pltpu.VMEM)
SMEM = pl.BlockSpec(memory_space=pltpu.SMEM)
HBM = pl.BlockSpec(memory_space=pltpu.HBM)
PARAMS = pltpu.CompilerParams(vmem_limit_bytes=40 * 1024 * 1024)


def mult(left, right, left_dim=1, right_dim=0):
    return lax.dot_general(
        left,
        right,
        (((left_dim,), (right_dim,)), ((), ())),
        precision=lax.Precision.HIGHEST,
        preferred_element_type=jnp.float32,
    )


def shape(*dims):
    return jax.ShapeDtypeStruct(dims, jnp.float32)


def cost(flops, nbytes):
    return pl.CostEstimate(flops=flops, bytes_accessed=nbytes, transcendentals=0)


def lane(block, k):
    return jnp.broadcast_to(block[:, k : k + 1], (SUB, NB))


def row(block, s):
    return jnp.broadcast_to(block[s : s + 1, :], (SUB, NB))


def lane_ids():
    sub_id = lax.broadcasted_iota(jnp.int32, (SUB, NB), 0)
    lane_id = lax.broadcasted_iota(jnp.int32, (SUB, NB), 1)
    return sub_id, lane_id


def inverse_factor(left):
    count = NB // SUB
    sub_id, lane_id = lane_ids()
    eye = [jnp.where(lane_id == sub_id + SUB * i, 1.0, 0.0) for i in range(count)]
    right = list(eye)
    for k in range(0, NB, 4):
        b, s = divmod(k, SUB)
        r = [row(left[b], s + j) for j in range(4)]
        e = [row(right[b], s + j) for j in range(4)]
        a = [[lane(r[i], k + j) if j >= i else None for j in range(4)] for i in range(4)]
        scale = 1.0 / (a[0][0] * a[1][1] - a[0][1] * a[0][1])
        i00, i01, i11 = a[1][1] * scale, -a[0][1] * scale, a[0][0] * scale
        t = [(i00 * a[0][j] + i01 * a[1][j], i01 * a[0][j] + i11 * a[1][j]) for j in (2, 3)]
        s22 = a[2][2] - t[0][0] * a[0][2] - t[0][1] * a[1][2]
        s23 = a[2][3] - t[0][0] * a[0][3] - t[0][1] * a[1][3]
        s33 = a[3][3] - t[1][0] * a[0][3] - t[1][1] * a[1][3]
        scale = 1.0 / (s22 * s33 - s23 * s23)
        j22, j23, j33 = s33 * scale, -s23 * scale, s22 * scale

        def rank(x):
            x2 = x[2] - t[0][0] * x[0] - t[0][1] * x[1]
            x3 = x[3] - t[1][0] * x[0] - t[1][1] * x[1]
            q2, q3 = j22 * x2 + j23 * x3, j23 * x2 + j33 * x3
            u0 = i00 * x[0] + i01 * x[1] - t[0][0] * q2 - t[1][0] * q3
            u1 = i01 * x[0] + i11 * x[1] - t[0][1] * q2 - t[1][1] * q3
            return x2, x3, (u0, u1, q2, q3)

        l2, l3, lu = rank(r)
        e2, e3, eu = rank(e)
        for i in range(b, count):
            c = [lane(left[i], k + j) for j in range(4)]
            if i == b:
                c = [jnp.where(sub_id > s + 3, x, 0.0) for x in c]
            left[i] = left[i] - (c[0] * lu[0] + c[1] * lu[1]) - (c[2] * lu[2] + c[3] * lu[3])
            right[i] = right[i] - (c[0] * eu[0] + c[1] * eu[1]) - (c[2] * eu[2] + c[3] * eu[3])
        left[b] = jnp.where(sub_id == s + 2, l2, jnp.where(sub_id == s + 3, l3, left[b]))
        right[b] = jnp.where(sub_id == s + 2, e2, jnp.where(sub_id == s + 3, e3, right[b]))
    odd = (sub_id % 2) == 1
    out = []
    for i in range(count):
        diag = jnp.sum(left[i] * eye[i], axis=1, keepdims=True)
        below = jnp.sum(jnp.where(lane_id == sub_id + (SUB * i - 1), left[i], 0.0), axis=1, keepdims=True)
        diag, below = jnp.broadcast_to(diag, (SUB, NB)), jnp.broadcast_to(below, (SUB, NB))
        ratio = jnp.where(odd, below / pltpu.roll(diag, 1, 0), 0.0)
        rows = right[i] - ratio * pltpu.roll(right[i], 1, 0)
        out.append(rows * lax.rsqrt(diag - ratio * below))
    return out


def fetch(copies):
    for copy in copies:
        copy.start()
    for copy in copies:
        copy.wait()


def invert_kernel(rows, cols, ids_ref, state_hbm, panel_hbm, pack_ref, state_ref, panel_ref, sems):
    get_state = pltpu.make_async_copy(state_hbm, state_ref, sems.at[0])
    get_panel = pltpu.make_async_copy(panel_hbm, panel_ref, sems.at[1])
    get_state.start()
    get_panel.start()
    get_state.wait()
    count = NB // SUB
    sub_id, lane_id = lane_ids()
    held = [
        jnp.where(lane_id == sub_id + SUB * i, 1.0, 0.0) - state_ref[2 * NB + SUB * i : 2 * NB + SUB * i + SUB, :] for i in range(count)
    ]
    for k in range(0, NB, 2):
        b, s = divmod(k, SUB)
        one, two = row(held[b], s), row(held[b], s + 1)
        a11, a12, a21, a22 = lane(one, k), lane(one, k + 1), lane(two, k), lane(two, k + 1)
        scale = 1.0 / (a11 * a22 - a12 * a21)
        i11, i12, i21, i22 = a22 * scale, -a12 * scale, -a21 * scale, a11 * scale
        h1, h2 = lane_id == k, lane_id == k + 1
        o1 = jnp.where(h1, 1.0, jnp.where(h2, 0.0, one))
        o2 = jnp.where(h1, 0.0, jnp.where(h2, 1.0, two))
        n1, n2 = i11 * o1 + i12 * o2, i21 * o1 + i22 * o2
        for i in range(count):
            c1, c2 = lane(held[i], k), lane(held[i], k + 1)
            new = jnp.where(h1 | h2, 0.0, held[i]) - c1 * n1 - c2 * n2
            if i == b:
                new = jnp.where(sub_id == s, n1, jnp.where(sub_id == s + 1, n2, new))
            held[i] = new
    for i in range(count):
        pack_ref[SUB * i : SUB * i + SUB, :] = held[i]
    pack_ref[NB : 3 * NB, :] = state_ref[: 2 * NB, :]
    get_panel.wait()
    inverse, sign = state_ref[:NB, :], state_ref[NB : 2 * NB, :]
    y = mult(panel_ref[...], inverse, 1, 1)
    y_cols = jnp.concatenate([y[rows : rows + NB] - jnp.where(ids_ref[1] == 1, sign, 0.0), y[rows + NB :]], 0)
    pack_ref[3 * NB : 3 * NB + cols, :] = mult(y_cols, pack_ref[:NB, :])
    pack_ref[3 * NB + cols : 4 * NB + cols, :] = y[:NB] - jnp.where(ids_ref[0] == 1, sign, 0.0)
    pack_ref[4 * NB + cols :, :] = y[NB:rows]


def prepare_kernel(col_blocks, fold, slim, ids_ref, a_ref, send_ref, top_ref):
    rows = a_ref.shape[0] // col_blocks
    col_count = send_ref.shape[0]
    share, step, per = fold * slim, NB // col_count, NB // slim
    panel = a_ref[pl.ds(0, rows, col_blocks), :]
    first = jnp.where((ids_ref[0] == 0) & (ids_ref[1] == 0), 0.0, panel[:NB])
    panel = jnp.concatenate([first, panel[NB:]], 0)
    gram = mult(panel, panel, 0, 0)
    lead = jnp.where(ids_ref[0] == 1, first, 0.0)
    for m in range(rows // NB):
        k, f = divmod(m, fold)
        send_ref[k * per : (k + 1) * per, f * slim : (f + 1) * slim, :] = panel[m * NB : (m + 1) * NB].reshape(per, slim, NB)
    for c in range(col_count):
        send_ref[c, share : share + step, :] = gram[c * step : (c + 1) * step]
        send_ref[c, share + step : share + 2 * step, :] = lead[c * step : (c + 1) * step]
    for k in range(col_blocks):
        block = a_ref[pl.ds(k, NB, col_blocks), :].T
        if k == 0:
            block = jnp.where(ids_ref[1] == 0, 0.0, block)
        top_ref[k * NB : (k + 1) * NB, :] = block


def join_kernel(share_ref, got_ref, send_ref):
    mine = share_ref[...]
    piece = jnp.sum(got_ref[...], 0)
    send_ref[:, : mine.shape[0], :] = jnp.broadcast_to(mine[None], (send_ref.shape[0],) + mine.shape)
    send_ref[:, mine.shape[0] :, :] = jnp.broadcast_to(piece[None], (send_ref.shape[0],) + piece.shape)


def relay_kernel(fold, slim, ids_ref, got_ref, send_ref):
    row_count = got_ref.shape[0]
    share = fold * slim
    mine = got_ref[ids_ref[0], :share, :]
    piece = jnp.sum(got_ref[:, share:, :], 0)
    send_ref[:, :share, :] = jnp.broadcast_to(mine[None], (fold * row_count,) + mine.shape)
    send_ref[:, share + slim :, :] = jnp.broadcast_to(piece[None], (fold * row_count,) + piece.shape)
    for f in range(fold):
        send_ref[f * row_count : (f + 1) * row_count, share : share + slim, :] = got_ref[:, f * slim : (f + 1) * slim, :]


def product_kernel(col_blocks, fold, slim, ids_ref, got_ref, top_ref, a_ref, send_hbm, panel_hbm, send_ref, panel_ref, hold_ref, sems):
    col_count = got_ref.shape[0]
    rows, cols = a_ref.shape[0] // col_blocks, col_blocks * NB
    share, step, per = fold * slim, NB // col_count, NB // slim
    panel_ref[rows:, :] = top_ref[...]
    for m in range(rows // NB):
        k, f = divmod(m, fold)
        panel_ref[m * NB : (m + 1) * NB, :] = got_ref[k * per : (k + 1) * per, f * slim : (f + 1) * slim, :].reshape(NB, NB)
    put_panel = pltpu.make_async_copy(panel_ref, panel_hbm, sems.at[0])
    put_panel.start()
    part = jnp.zeros((rows, NB), jnp.float32)
    for k in range(col_blocks):
        part = part + mult(a_ref[pl.ds(k, rows, col_blocks), :], panel_ref[rows + k * NB : rows + (k + 1) * NB, :])
    for m in range(rows // NB):
        k, f = divmod(m, fold)
        send_ref[k * per : (k + 1) * per, f * slim : (f + 1) * slim, :] = part[m * NB : (m + 1) * NB].reshape(per, slim, NB)
    put_share = pltpu.make_async_copy(send_ref.at[:, :share, :], send_hbm.at[:, :share, :], sems.at[1])
    put_share.start()
    hold_ref[...] = mult(panel_ref[:rows, :], part, 0, 0)
    lead = jnp.where(ids_ref[0] == 1, part[:NB], 0.0)
    for c in range(col_count):
        send_ref[c, share : share + step, :] = hold_ref[c * step : (c + 1) * step, :]
        send_ref[c, share + step : share + 2 * step, :] = lead[c * step : (c + 1) * step]
    put_piece = pltpu.make_async_copy(send_ref.at[:, share:, :], send_hbm.at[:, share:, :], sems.at[2])
    put_piece.start()
    put_panel.wait()
    put_share.wait()
    put_piece.wait()


def factor_kernel(share, step, got_ref, state_hbm, state_ref, hold_ref, lead_ref, sem):
    count = NB // SUB
    sub_id, lane_id = lane_ids()
    for c in range(got_ref.shape[0]):
        hold_ref[c * step : (c + 1) * step, :] = got_ref[c, share : share + step, :]
        lead_ref[c * step : (c + 1) * step, :] = got_ref[c, share + step : share + 2 * step, :]
    out = inverse_factor([hold_ref[SUB * i : SUB * i + SUB, :] for i in range(count)])
    for i in range(count):
        state_ref[SUB * i : SUB * i + SUB, :] = out[i]
    inverse = state_ref[:NB, :]
    lead = lead_ref[...]
    signs = jnp.where(jnp.sum(lead * inverse, axis=1, keepdims=True) >= 0, -1.0, 1.0)
    state_ref[2 * NB :, :] = signs * mult(lead, inverse, 1, 1)
    for i in range(count):
        here = jnp.where(lane_id == sub_id + SUB * i, 1.0, 0.0)
        state_ref[NB + SUB * i : NB + SUB * i + SUB, :] = here * signs[SUB * i : SUB * i + SUB]
    fetch([pltpu.make_async_copy(state_ref, state_hbm, sem)])


def spread_kernel(share, step, ids_ref, got_hbm, own_hbm, state_hbm, send_ref, got_ref, own_ref, state_ref, sems):
    fetch(
        [
            pltpu.make_async_copy(got_hbm, got_ref, sems.at[0]),
            pltpu.make_async_copy(own_hbm, own_ref, sems.at[1]),
            pltpu.make_async_copy(state_hbm.at[: 2 * NB, :], state_ref, sems.at[2]),
        ]
    )
    total = jnp.sum(got_ref[...], 0)
    own = own_ref[...]
    line = jnp.sum(state_ref[NB:, :], axis=0, keepdims=True)
    turned = mult(total, state_ref[:NB, :], 1, 1)
    rows = turned[:share] - own[:share] * line
    lead = jnp.where(ids_ref[0] == 1, turned[share + step :] - 0.5 * own[share + step :] * line, 0.0)
    out = jnp.concatenate([rows, total[share : share + step], lead], 0)
    send_ref[...] = jnp.broadcast_to(out[None], send_ref.shape)


def halves(value):
    high = value.astype(jnp.bfloat16)
    return high, (value - high.astype(jnp.float32)).astype(jnp.bfloat16)


def mult_half(left, right):
    return lax.dot_general(left, right, (((1,), (1,)), ((), ())), preferred_element_type=jnp.float32)


def update_kernel(
    col_blocks, fold, slim, got_ref, pack_ref, a_ref, out_ref, high_ref, low_ref, hold_ref, lead_ref, new_ref, sems
):
    col_count = got_ref.shape[0]
    share, step, per = fold * slim, NB // col_count, NB // slim
    cols = col_blocks * NB
    for c in range(col_count):
        hold_ref[c * step : (c + 1) * step, :] = got_ref[c, share + slim : share + slim + step, :]
        lead_ref[c * step : (c + 1) * step, :] = got_ref[c, share + slim + step : share + slim + 2 * step, :]
    coupling, inverse, v = pack_ref[:NB, :], pack_ref[NB : 2 * NB, :], pack_ref[3 * NB : 3 * NB + cols, :]
    y_ref = pack_ref.at[3 * NB + cols :, :]
    cross = jnp.sum(pack_ref[2 * NB : 3 * NB, :], axis=1, keepdims=True) * lead_ref[...]
    middle = mult(mult(inverse, hold_ref[...]), inverse, 1, 1) - cross - cross.T
    z_cols = got_ref[:, share : share + slim, :].reshape(cols, NB)
    u = mult(z_cols - mult(v, middle), coupling, 1, 1)
    for at, part in enumerate((u, v)):
        high, low = halves(part)
        high_ref[:, at * NB : (at + 1) * NB] = high
        low_ref[:, at * NB : (at + 1) * NB] = low
    right_high, right_low = high_ref[...], low_ref[...]
    copies = []
    for m in range(a_ref.shape[0] // cols):
        k, f = divmod(m, fold)
        z = got_ref[k * per : (k + 1) * per, f * slim : (f + 1) * slim, :].reshape(NB, NB)
        high, low = halves(jnp.concatenate([y_ref[m * NB : (m + 1) * NB, :], z], 1))
        change = mult_half(low, right_high) + mult_half(high, right_low) + mult_half(high, right_high)
        for n in range(col_blocks):
            here = pl.ds(m * NB * col_blocks + n, NB, col_blocks)
            new_ref[here, :] = a_ref[here, :] - change[:, n * NB : (n + 1) * NB]
        there = pl.ds(m * NB * col_blocks, NB * col_blocks)
        copy = pltpu.make_async_copy(new_ref.at[there, :], out_ref.at[there, :], sems.at[m])
        copy.start()
        copies.append(copy)
    for copy in copies:
        copy.wait()


def exchange(pieces, axis):
    return lax.all_to_all(pieces, axis, 0, 0)


def body(kernel):
    row_blocks, _, _, col_blocks, _, _ = kernel.shape
    rows, cols = row_blocks * NB, col_blocks * NB
    row_count, col_count = lax.axis_size("row"), lax.axis_size("col")
    fold = col_count // row_count
    row_index, col_index = lax.axis_index("row"), lax.axis_index("col")
    ids = jnp.stack([row_index, col_index]).astype(jnp.int32)
    lines = kernel.reshape(rows * col_blocks, NB)
    slim, step = cols // col_count, NB // col_count
    share = fold * slim
    pad = 2 * step

    def hbm(*dims):
        return pltpu.HBM(dims, jnp.float32)

    def relay(got):
        return pl.pallas_call(
            lambda *refs: relay_kernel(fold, slim, *refs),
            out_shape=shape(col_count, share + slim + pad, NB),
            in_specs=[SMEM, VMEM],
            out_specs=VMEM,
            compiler_params=PARAMS,
            name="relay",
            cost_estimate=cost(1_000_000, 1_000_000),
        )(ids, got)

    send, top = pl.pallas_call(
        lambda *refs: prepare_kernel(col_blocks, fold, slim, *refs),
        out_shape=(shape(col_count, share + pad, NB), shape(cols, NB)),
        in_specs=[SMEM, VMEM],
        out_specs=(VMEM, VMEM),
        compiler_params=PARAMS,
        name="prepare",
        cost_estimate=cost(2 * rows * NB * NB * 6, 3_000_000),
    )(ids, lines)
    got = exchange(send, "col")
    own, mine, piece = got[1], got[0, :share], got[0, share:]
    distance = row_count // 2
    while distance:
        pairs = [(at, at + distance) for at in range(0, row_count, 2 * distance)]
        moved = lax.ppermute(top, "row", pairs)
        top = jnp.where(row_index % (2 * distance) == distance, moved, top)
        distance //= 2
    pieces = exchange(jnp.broadcast_to(piece[None], (row_count,) + piece.shape), "row")
    send = pl.pallas_call(
        join_kernel,
        out_shape=shape(col_count, share + pad, NB),
        in_specs=[VMEM, VMEM],
        out_specs=VMEM,
        compiler_params=PARAMS,
        name="join",
        cost_estimate=cost(1_000_000, 1_000_000),
    )(mine, pieces)
    got = exchange(send, "col")

    send, panel = pl.pallas_call(
        lambda *refs: product_kernel(col_blocks, fold, slim, *refs),
        out_shape=(hbm(col_count, share + pad, NB), hbm(rows + cols, NB)),
        in_specs=[SMEM, VMEM, VMEM, VMEM],
        out_specs=(HBM, HBM),
        scratch_shapes=[
            pltpu.VMEM((col_count, share + pad, NB), jnp.float32),
            pltpu.VMEM((rows + cols, NB), jnp.float32),
            pltpu.VMEM((NB, NB), jnp.float32),
            pltpu.SemaphoreType.DMA((3,)),
        ],
        compiler_params=PARAMS,
        name="product",
        cost_estimate=cost(2 * rows * cols * NB * 6, 4_000_000),
    )(ids, got, top, lines)
    summed = exchange(send, "col")
    state = pl.pallas_call(
        lambda *refs: factor_kernel(share, step, *refs),
        out_shape=hbm(3 * NB, NB),
        in_specs=[VMEM],
        out_specs=HBM,
        scratch_shapes=[pltpu.VMEM((3 * NB, NB), jnp.float32)]
        + [pltpu.VMEM((NB, NB), jnp.float32)] * 2
        + [pltpu.SemaphoreType.DMA],
        compiler_params=PARAMS,
        name="factor",
        cost_estimate=cost(4_000_000_000, 2_000_000),
    )(got)

    send = pl.pallas_call(
        lambda *refs: spread_kernel(share, step, *refs),
        out_shape=shape(row_count, share + pad, NB),
        in_specs=[SMEM, HBM, HBM, HBM],
        out_specs=VMEM,
        scratch_shapes=[
            pltpu.VMEM((col_count, share + pad, NB), jnp.float32),
            pltpu.VMEM((share + pad, NB), jnp.float32),
            pltpu.VMEM((2 * NB, NB), jnp.float32),
            pltpu.SemaphoreType.DMA((3,)),
        ],
        compiler_params=PARAMS,
        name="spread",
        cost_estimate=cost(10_000_000, 1_000_000),
    )(ids, summed, own, state)
    got = exchange(send, "row")
    pack = pl.pallas_call(
        lambda *refs: invert_kernel(rows, cols, *refs),
        out_shape=shape(3 * NB + cols + rows, NB),
        in_specs=[SMEM, HBM, HBM],
        out_specs=VMEM,
        scratch_shapes=[
            pltpu.VMEM((3 * NB, NB), jnp.float32),
            pltpu.VMEM((rows + cols, NB), jnp.float32),
            pltpu.SemaphoreType.DMA((2,)),
        ],
        compiler_params=PARAMS,
        name="invert",
        cost_estimate=cost(4_000_000_000, 1_000_000),
    )(ids, state, panel)
    got, pack = lax.optimization_barrier((got, pack))
    last = exchange(relay(got), "col")

    updated = pl.pallas_call(
        lambda *refs: update_kernel(col_blocks, fold, slim, *refs),
        out_shape=shape(rows * col_blocks, NB),
        in_specs=[VMEM] * 3,
        out_specs=pl.BlockSpec(memory_space=pl.ANY),
        scratch_shapes=[
            pltpu.VMEM((cols, 2 * NB), jnp.bfloat16),
            pltpu.VMEM((cols, 2 * NB), jnp.bfloat16),
            pltpu.VMEM((NB, NB), jnp.float32),
            pltpu.VMEM((NB, NB), jnp.float32),
            pltpu.VMEM((rows * col_blocks, NB), jnp.float32),
            pltpu.SemaphoreType.DMA((row_blocks,)),
        ],
        compiler_params=PARAMS,
        name="update",
        cost_estimate=cost(4 * rows * cols * NB * 6, 6_000_000),
    )(last, pack, lines)
    return updated.reshape(kernel.shape)


def solution(mesh):
    return jax.shard_map(
        body,
        mesh=mesh,
        in_specs=(P(None, "row", None, None, "col", None),),
        out_specs=P(None, "row", None, None, "col", None),
        check_vma=False,
    )
```

```python
import jax
import jax.numpy as jnp
from jax import lax
from jax.experimental import pallas as pl
from jax.experimental.pallas import tpu as pltpu
from jax.sharding import PartitionSpec as P

NB = 128
SUB = 8
VMEM = pl.BlockSpec(memory_space=pltpu.VMEM)
SMEM = pl.BlockSpec(memory_space=pltpu.SMEM)
HBM = pl.BlockSpec(memory_space=pltpu.HBM)
PARAMS = pltpu.CompilerParams(vmem_limit_bytes=40 * 1024 * 1024)


def mult(left, right, left_dim=1, right_dim=0):
    return lax.dot_general(
        left,
        right,
        (((left_dim,), (right_dim,)), ((), ())),
        precision=lax.Precision.HIGHEST,
        preferred_element_type=jnp.float32,
    )


def shape(*dims):
    return jax.ShapeDtypeStruct(dims, jnp.float32)


def cost(flops, nbytes):
    return pl.CostEstimate(flops=flops, bytes_accessed=nbytes, transcendentals=0)


def lane(block, k):
    return jnp.broadcast_to(block[:, k : k + 1], (SUB, NB))


def row(block, s):
    return jnp.broadcast_to(block[s : s + 1, :], (SUB, NB))


def lane_ids():
    sub_id = lax.broadcasted_iota(jnp.int32, (SUB, NB), 0)
    lane_id = lax.broadcasted_iota(jnp.int32, (SUB, NB), 1)
    return sub_id, lane_id


def inverse_factor(left):
    count = NB // SUB
    sub_id, lane_id = lane_ids()
    eye = [jnp.where(lane_id == sub_id + SUB * i, 1.0, 0.0) for i in range(count)]
    right = list(eye)
    for k in range(0, NB, 4):
        b, s = divmod(k, SUB)
        r = [row(left[b], s + j) for j in range(4)]
        e = [row(right[b], s + j) for j in range(4)]
        a = [[lane(r[i], k + j) if j >= i else None for j in range(4)] for i in range(4)]
        scale = 1.0 / (a[0][0] * a[1][1] - a[0][1] * a[0][1])
        i00, i01, i11 = a[1][1] * scale, -a[0][1] * scale, a[0][0] * scale
        t = [(i00 * a[0][j] + i01 * a[1][j], i01 * a[0][j] + i11 * a[1][j]) for j in (2, 3)]
        s22 = a[2][2] - t[0][0] * a[0][2] - t[0][1] * a[1][2]
        s23 = a[2][3] - t[0][0] * a[0][3] - t[0][1] * a[1][3]
        s33 = a[3][3] - t[1][0] * a[0][3] - t[1][1] * a[1][3]
        scale = 1.0 / (s22 * s33 - s23 * s23)
        j22, j23, j33 = s33 * scale, -s23 * scale, s22 * scale

        def rank(x):
            x2 = x[2] - t[0][0] * x[0] - t[0][1] * x[1]
            x3 = x[3] - t[1][0] * x[0] - t[1][1] * x[1]
            q2, q3 = j22 * x2 + j23 * x3, j23 * x2 + j33 * x3
            u0 = i00 * x[0] + i01 * x[1] - t[0][0] * q2 - t[1][0] * q3
            u1 = i01 * x[0] + i11 * x[1] - t[0][1] * q2 - t[1][1] * q3
            return x2, x3, (u0, u1, q2, q3)

        l2, l3, lu = rank(r)
        e2, e3, eu = rank(e)
        for i in range(b, count):
            c = [lane(left[i], k + j) for j in range(4)]
            if i == b:
                c = [jnp.where(sub_id > s + 3, x, 0.0) for x in c]
            left[i] = left[i] - (c[0] * lu[0] + c[1] * lu[1]) - (c[2] * lu[2] + c[3] * lu[3])
            right[i] = right[i] - (c[0] * eu[0] + c[1] * eu[1]) - (c[2] * eu[2] + c[3] * eu[3])
        left[b] = jnp.where(sub_id == s + 2, l2, jnp.where(sub_id == s + 3, l3, left[b]))
        right[b] = jnp.where(sub_id == s + 2, e2, jnp.where(sub_id == s + 3, e3, right[b]))
    odd = (sub_id % 2) == 1
    out = []
    for i in range(count):
        diag = jnp.sum(left[i] * eye[i], axis=1, keepdims=True)
        below = jnp.sum(jnp.where(lane_id == sub_id + (SUB * i - 1), left[i], 0.0), axis=1, keepdims=True)
        diag, below = jnp.broadcast_to(diag, (SUB, NB)), jnp.broadcast_to(below, (SUB, NB))
        ratio = jnp.where(odd, below / pltpu.roll(diag, 1, 0), 0.0)
        rows = right[i] - ratio * pltpu.roll(right[i], 1, 0)
        out.append(rows * lax.rsqrt(diag - ratio * below))
    return out


def invert_kernel(rows, cols, ids_ref, state_hbm, panel_hbm, pack_ref, state_ref, panel_ref, sems):
    get_state = pltpu.make_async_copy(state_hbm, state_ref, sems.at[0])
    get_panel = pltpu.make_async_copy(panel_hbm, panel_ref, sems.at[1])
    get_state.start()
    get_panel.start()
    get_state.wait()
    count = NB // SUB
    sub_id, lane_id = lane_ids()
    held = [
        jnp.where(lane_id == sub_id + SUB * i, 1.0, 0.0) - state_ref[2 * NB + SUB * i : 2 * NB + SUB * i + SUB, :] for i in range(count)
    ]
    for k in range(0, NB, 2):
        b, s = divmod(k, SUB)
        one, two = row(held[b], s), row(held[b], s + 1)
        a11, a12, a21, a22 = lane(one, k), lane(one, k + 1), lane(two, k), lane(two, k + 1)
        scale = 1.0 / (a11 * a22 - a12 * a21)
        i11, i12, i21, i22 = a22 * scale, -a12 * scale, -a21 * scale, a11 * scale
        h1, h2 = lane_id == k, lane_id == k + 1
        o1 = jnp.where(h1, 1.0, jnp.where(h2, 0.0, one))
        o2 = jnp.where(h1, 0.0, jnp.where(h2, 1.0, two))
        n1, n2 = i11 * o1 + i12 * o2, i21 * o1 + i22 * o2
        for i in range(count):
            c1, c2 = lane(held[i], k), lane(held[i], k + 1)
            new = jnp.where(h1 | h2, 0.0, held[i]) - c1 * n1 - c2 * n2
            if i == b:
                new = jnp.where(sub_id == s, n1, jnp.where(sub_id == s + 1, n2, new))
            held[i] = new
    for i in range(count):
        pack_ref[SUB * i : SUB * i + SUB, :] = held[i]
    pack_ref[NB : 3 * NB, :] = state_ref[: 2 * NB, :]
    get_panel.wait()
    inverse, sign = state_ref[:NB, :], state_ref[NB : 2 * NB, :]
    y = mult(panel_ref[...], inverse, 1, 1)
    y_cols = jnp.concatenate([y[rows : rows + NB] - jnp.where(ids_ref[1] == 1, sign, 0.0), y[rows + NB :]], 0)
    pack_ref[3 * NB : 3 * NB + cols, :] = mult(y_cols, pack_ref[:NB, :])
    pack_ref[3 * NB + cols : 4 * NB + cols, :] = y[:NB] - jnp.where(ids_ref[0] == 1, sign, 0.0)
    pack_ref[4 * NB + cols :, :] = y[NB:rows]


def prepare_kernel(col_blocks, fold, slim, ids_ref, a_ref, send_ref):
    rows = a_ref.shape[0] // col_blocks
    col_count = send_ref.shape[0]
    share, step, per = fold * slim, NB // col_count, NB // slim
    panel = a_ref[pl.ds(0, rows, col_blocks), :]
    first = jnp.where((ids_ref[0] == 0) & (ids_ref[1] == 0), 0.0, panel[:NB])
    panel = jnp.concatenate([first, panel[NB:]], 0)
    gram = mult(panel, panel, 0, 0)
    lead = jnp.where(ids_ref[0] == 1, first, 0.0)
    for m in range(rows // NB):
        k, f = divmod(m, fold)
        send_ref[k * per : (k + 1) * per, f * slim : (f + 1) * slim, :] = panel[m * NB : (m + 1) * NB].reshape(per, slim, NB)
    for c in range(col_count):
        send_ref[c, share : share + step, :] = gram[c * step : (c + 1) * step]
        send_ref[c, share + step : share + 2 * step, :] = lead[c * step : (c + 1) * step]


def top_kernel(col_blocks, ids_ref, a_ref, top_ref):
    for k in range(col_blocks):
        block = a_ref[pl.ds(k, NB, col_blocks), :].T
        if k == 0:
            block = jnp.where(ids_ref[1] == 0, 0.0, block)
        top_ref[k * NB : (k + 1) * NB, :] = block


def join_kernel(share_ref, got_ref, send_ref):
    mine = share_ref[...]
    piece = jnp.sum(got_ref[...], 0)
    send_ref[:, : mine.shape[0], :] = jnp.broadcast_to(mine[None], (send_ref.shape[0],) + mine.shape)
    send_ref[:, mine.shape[0] :, :] = jnp.broadcast_to(piece[None], (send_ref.shape[0],) + piece.shape)


def relay_kernel(fold, slim, ids_ref, got_ref, send_ref):
    row_count = got_ref.shape[0]
    share = fold * slim
    mine = got_ref[ids_ref[0], :share, :]
    piece = jnp.sum(got_ref[:, share:, :], 0)
    send_ref[:, :share, :] = jnp.broadcast_to(mine[None], (fold * row_count,) + mine.shape)
    send_ref[:, share + slim :, :] = jnp.broadcast_to(piece[None], (fold * row_count,) + piece.shape)
    for f in range(fold):
        send_ref[f * row_count : (f + 1) * row_count, share : share + slim, :] = got_ref[:, f * slim : (f + 1) * slim, :]


def product_kernel(col_blocks, fold, slim, ids_ref, got_ref, top_ref, a_ref, send_hbm, panel_hbm, send_ref, panel_ref, hold_ref, sems):
    col_count = got_ref.shape[0]
    rows, cols = a_ref.shape[0] // col_blocks, col_blocks * NB
    share, step, per = fold * slim, NB // col_count, NB // slim
    panel_ref[rows:, :] = top_ref[...]
    for m in range(rows // NB):
        k, f = divmod(m, fold)
        panel_ref[m * NB : (m + 1) * NB, :] = got_ref[k * per : (k + 1) * per, f * slim : (f + 1) * slim, :].reshape(NB, NB)
    put_panel = pltpu.make_async_copy(panel_ref, panel_hbm, sems.at[0])
    put_panel.start()
    part = jnp.zeros((rows, NB), jnp.float32)
    for k in range(col_blocks):
        part = part + mult(a_ref[pl.ds(k, rows, col_blocks), :], panel_ref[rows + k * NB : rows + (k + 1) * NB, :])
    for m in range(rows // NB):
        k, f = divmod(m, fold)
        send_ref[k * per : (k + 1) * per, f * slim : (f + 1) * slim, :] = part[m * NB : (m + 1) * NB].reshape(per, slim, NB)
    put_share = pltpu.make_async_copy(send_ref.at[:, :share, :], send_hbm.at[:, :share, :], sems.at[1])
    put_share.start()
    hold_ref[...] = mult(panel_ref[:rows, :], part, 0, 0)
    lead = jnp.where(ids_ref[0] == 1, part[:NB], 0.0)
    for c in range(col_count):
        send_ref[c, share : share + step, :] = hold_ref[c * step : (c + 1) * step, :]
        send_ref[c, share + step : share + 2 * step, :] = lead[c * step : (c + 1) * step]
    put_piece = pltpu.make_async_copy(send_ref.at[:, share:, :], send_hbm.at[:, share:, :], sems.at[2])
    put_piece.start()
    put_panel.wait()
    put_share.wait()
    put_piece.wait()


def factor_kernel(share, step, got_ref, state_hbm, state_ref, hold_ref, lead_ref, sem):
    count = NB // SUB
    sub_id, lane_id = lane_ids()
    for c in range(got_ref.shape[0]):
        hold_ref[c * step : (c + 1) * step, :] = got_ref[c, share : share + step, :]
        lead_ref[c * step : (c + 1) * step, :] = got_ref[c, share + step : share + 2 * step, :]
    out = inverse_factor([hold_ref[SUB * i : SUB * i + SUB, :] for i in range(count)])
    for i in range(count):
        state_ref[SUB * i : SUB * i + SUB, :] = out[i]
    inverse = state_ref[:NB, :]
    lead = lead_ref[...]
    signs = jnp.where(jnp.sum(lead * inverse, axis=1, keepdims=True) >= 0, -1.0, 1.0)
    state_ref[2 * NB :, :] = signs * mult(lead, inverse, 1, 1)
    for i in range(count):
        here = jnp.where(lane_id == sub_id + SUB * i, 1.0, 0.0)
        state_ref[NB + SUB * i : NB + SUB * i + SUB, :] = here * signs[SUB * i : SUB * i + SUB]
    put_state = pltpu.make_async_copy(state_ref, state_hbm, sem)
    put_state.start()
    put_state.wait()


def spread_kernel(share, step, ids_ref, got_ref, own_ref, state_hbm, send_ref, state_ref, sem):
    get_state = pltpu.make_async_copy(state_hbm.at[: 2 * NB, :], state_ref, sem)
    get_state.start()
    total = jnp.sum(got_ref[...], 0)
    get_state.wait()
    own = own_ref[...]
    line = jnp.sum(state_ref[NB:, :], axis=0, keepdims=True)
    turned = mult(total, state_ref[:NB, :], 1, 1)
    rows = turned[:share] - own[:share] * line
    lead = jnp.where(ids_ref[0] == 1, turned[share + step :] - 0.5 * own[share + step :] * line, 0.0)
    out = jnp.concatenate([rows, total[share : share + step], lead], 0)
    send_ref[...] = jnp.broadcast_to(out[None], send_ref.shape)


def halves(value):
    high = value.astype(jnp.bfloat16)
    return high, (value - high.astype(jnp.float32)).astype(jnp.bfloat16)


def mult_half(left, right):
    return lax.dot_general(left, right, (((1,), (1,)), ((), ())), preferred_element_type=jnp.float32)


def update_kernel(
    col_blocks, fold, slim, got_ref, pack_ref, a_ref, out_ref, high_ref, low_ref, hold_ref, lead_ref, new_ref, sems
):
    col_count = got_ref.shape[0]
    share, step, per = fold * slim, NB // col_count, NB // slim
    cols = col_blocks * NB
    for c in range(col_count):
        hold_ref[c * step : (c + 1) * step, :] = got_ref[c, share + slim : share + slim + step, :]
        lead_ref[c * step : (c + 1) * step, :] = got_ref[c, share + slim + step : share + slim + 2 * step, :]
    coupling, inverse, v = pack_ref[:NB, :], pack_ref[NB : 2 * NB, :], pack_ref[3 * NB : 3 * NB + cols, :]
    y_ref = pack_ref.at[3 * NB + cols :, :]
    cross = jnp.sum(pack_ref[2 * NB : 3 * NB, :], axis=1, keepdims=True) * lead_ref[...]
    middle = mult(mult(inverse, hold_ref[...]), inverse, 1, 1) - cross - cross.T
    z_cols = got_ref[:, share : share + slim, :].reshape(cols, NB)
    u = mult(z_cols - mult(v, middle), coupling, 1, 1)
    for at, part in enumerate((u, v)):
        high, low = halves(part)
        high_ref[:, at * NB : (at + 1) * NB] = high
        low_ref[:, at * NB : (at + 1) * NB] = low
    right_high, right_low = high_ref[...], low_ref[...]
    copies = []
    for k in range(a_ref.shape[0] // (fold * cols)):
        z = [got_ref[k * per : (k + 1) * per, f * slim : (f + 1) * slim, :].reshape(NB, NB) for f in range(fold)]
        y = y_ref[k * fold * NB : (k + 1) * fold * NB, :]
        high, low = halves(jnp.concatenate([y, jnp.concatenate(z, 0)], 1))
        change = mult_half(low, right_high) + mult_half(high, right_low) + mult_half(high, right_high)
        for n in range(col_blocks):
            here = pl.ds(k * fold * cols + n, fold * NB, col_blocks)
            new_ref[here, :] = a_ref[here, :] - change[:, n * NB : (n + 1) * NB]
        there = pl.ds(k * fold * cols, fold * cols)
        copy = pltpu.make_async_copy(new_ref.at[there, :], out_ref.at[there, :], sems.at[k])
        copy.start()
        copies.append(copy)
    for copy in copies:
        copy.wait()


def exchange(pieces, axis):
    return lax.all_to_all(pieces, axis, 0, 0)


def body(kernel):
    row_blocks, _, _, col_blocks, _, _ = kernel.shape
    rows, cols = row_blocks * NB, col_blocks * NB
    row_count, col_count = lax.axis_size("row"), lax.axis_size("col")
    fold = col_count // row_count
    row_index, col_index = lax.axis_index("row"), lax.axis_index("col")
    ids = jnp.stack([row_index, col_index]).astype(jnp.int32)
    lines = kernel.reshape(rows * col_blocks, NB)
    slim, step = cols // col_count, NB // col_count
    share = fold * slim
    pad = 2 * step

    def hbm(*dims):
        return pltpu.HBM(dims, jnp.float32)

    def relay(got):
        return pl.pallas_call(
            lambda *refs: relay_kernel(fold, slim, *refs),
            out_shape=shape(col_count, share + slim + pad, NB),
            in_specs=[SMEM, VMEM],
            out_specs=VMEM,
            compiler_params=PARAMS,
            name="relay",
            cost_estimate=cost(1_000_000, 1_000_000),
        )(ids, got)

    send = pl.pallas_call(
        lambda *refs: prepare_kernel(col_blocks, fold, slim, *refs),
        out_shape=shape(col_count, share + pad, NB),
        in_specs=[SMEM, VMEM],
        out_specs=VMEM,
        compiler_params=PARAMS,
        name="prepare",
        cost_estimate=cost(2 * rows * NB * NB * 6, 3_000_000),
    )(ids, lines)
    top = pl.pallas_call(
        lambda *refs: top_kernel(col_blocks, *refs),
        out_shape=shape(cols, NB),
        in_specs=[SMEM, VMEM],
        out_specs=VMEM,
        compiler_params=PARAMS,
        name="top",
        cost_estimate=cost(1_000_000, 1_000_000),
    )(ids, lines)
    got, top = lax.optimization_barrier((exchange(send, "col"), top))
    own, mine, piece = got[1], got[0, :share], got[0, share:]
    pieces = exchange(jnp.broadcast_to(piece[None], (row_count,) + piece.shape), "row")
    stride = max(row_count // 4, 1)

    def fan(block, leap, rest):
        sent = []
        for hop in range(1, min(4, row_count // leap)):
            pairs = [(at, at + hop * leap) for at in range(0, row_count, 4 * leap)]
            sent.append(lax.ppermute(block, "row", pairs))
        rest, *sent = lax.optimization_barrier((rest, *sent))
        for hop, part in enumerate(sent, 1):
            block = jnp.where(row_index % (4 * leap) == hop * leap, part, block)
        return block, rest

    top, pieces = fan(top, stride, pieces)
    send = pl.pallas_call(
        join_kernel,
        out_shape=shape(col_count, share + pad, NB),
        in_specs=[VMEM, VMEM],
        out_specs=VMEM,
        compiler_params=PARAMS,
        name="join",
        cost_estimate=cost(1_000_000, 1_000_000),
    )(mine, pieces)
    got = exchange(send, "col")
    if stride > 1:
        top, got = fan(top, 1, got)

    send, panel = pl.pallas_call(
        lambda *refs: product_kernel(col_blocks, fold, slim, *refs),
        out_shape=(hbm(col_count, share + pad, NB), hbm(rows + cols, NB)),
        in_specs=[SMEM, VMEM, VMEM, VMEM],
        out_specs=(HBM, HBM),
        scratch_shapes=[
            pltpu.VMEM((col_count, share + pad, NB), jnp.float32),
            pltpu.VMEM((rows + cols, NB), jnp.float32),
            pltpu.VMEM((NB, NB), jnp.float32),
            pltpu.SemaphoreType.DMA((3,)),
        ],
        compiler_params=PARAMS,
        name="product",
        cost_estimate=cost(2 * rows * cols * NB * 6, 4_000_000),
    )(ids, got, top, lines)
    summed = exchange(send, "col")
    state = pl.pallas_call(
        lambda *refs: factor_kernel(share, step, *refs),
        out_shape=hbm(3 * NB, NB),
        in_specs=[VMEM],
        out_specs=HBM,
        scratch_shapes=[pltpu.VMEM((3 * NB, NB), jnp.float32)]
        + [pltpu.VMEM((NB, NB), jnp.float32)] * 2
        + [pltpu.SemaphoreType.DMA],
        compiler_params=PARAMS,
        name="factor",
        cost_estimate=cost(4_000_000_000, 2_000_000),
    )(got)

    state = pltpu.with_memory_space_constraint(state, pltpu.HBM)
    panel = pltpu.with_memory_space_constraint(panel, pltpu.HBM)

    send = pl.pallas_call(
        lambda *refs: spread_kernel(share, step, *refs),
        out_shape=shape(row_count, share + pad, NB),
        in_specs=[SMEM, VMEM, VMEM, HBM],
        out_specs=VMEM,
        scratch_shapes=[pltpu.VMEM((2 * NB, NB), jnp.float32), pltpu.SemaphoreType.DMA],
        compiler_params=PARAMS,
        name="spread",
        cost_estimate=cost(10_000_000, 1_000_000),
    )(ids, summed, own, state)
    got = exchange(send, "row")
    pack = pl.pallas_call(
        lambda *refs: invert_kernel(rows, cols, *refs),
        out_shape=shape(3 * NB + cols + rows, NB),
        in_specs=[SMEM, HBM, HBM],
        out_specs=VMEM,
        scratch_shapes=[
            pltpu.VMEM((3 * NB, NB), jnp.float32),
            pltpu.VMEM((rows + cols, NB), jnp.float32),
            pltpu.SemaphoreType.DMA((2,)),
        ],
        compiler_params=PARAMS,
        name="invert",
        cost_estimate=cost(4_000_000_000, 1_000_000),
    )(ids, state, panel)
    got, pack = lax.optimization_barrier((got, pack))
    last = exchange(relay(got), "col")

    updated = pl.pallas_call(
        lambda *refs: update_kernel(col_blocks, fold, slim, *refs),
        out_shape=shape(rows * col_blocks, NB),
        in_specs=[VMEM] * 3,
        out_specs=pl.BlockSpec(memory_space=pl.ANY),
        scratch_shapes=[
            pltpu.VMEM((cols, 2 * NB), jnp.bfloat16),
            pltpu.VMEM((cols, 2 * NB), jnp.bfloat16),
            pltpu.VMEM((NB, NB), jnp.float32),
            pltpu.VMEM((NB, NB), jnp.float32),
            pltpu.VMEM((rows * col_blocks, NB), jnp.float32),
            pltpu.SemaphoreType.DMA((row_blocks // fold,)),
        ],
        compiler_params=PARAMS,
        name="update",
        cost_estimate=cost(4 * rows * cols * NB * 6, 6_000_000),
    )(last, pack, lines)
    return updated.reshape(kernel.shape)


def solution(mesh):
    return jax.shard_map(
        body,
        mesh=mesh,
        in_specs=(P(None, "row", None, None, "col", None),),
        out_specs=P(None, "row", None, None, "col", None),
        check_vma=False,
    )
```

```python
import jax
import jax.numpy as jnp
from jax import lax
from jax.experimental import pallas as pl
from jax.experimental.pallas import tpu as pltpu
from jax.sharding import PartitionSpec as P

NB = 128
SUB = 8
VMEM = pl.BlockSpec(memory_space=pltpu.VMEM)
SMEM = pl.BlockSpec(memory_space=pltpu.SMEM)
HBM = pl.BlockSpec(memory_space=pltpu.HBM)
PARAMS = pltpu.CompilerParams(vmem_limit_bytes=40 * 1024 * 1024)


def mult(left, right, left_dim=1, right_dim=0):
    return lax.dot_general(
        left,
        right,
        (((left_dim,), (right_dim,)), ((), ())),
        precision=lax.Precision.HIGHEST,
        preferred_element_type=jnp.float32,
    )


def shape(*dims):
    return jax.ShapeDtypeStruct(dims, jnp.float32)


def cost(flops, nbytes):
    return pl.CostEstimate(flops=flops, bytes_accessed=nbytes, transcendentals=0)


def lane(block, k):
    return jnp.broadcast_to(block[:, k : k + 1], (SUB, NB))


def row(block, s):
    return jnp.broadcast_to(block[s : s + 1, :], (SUB, NB))


def lane_ids():
    sub_id = lax.broadcasted_iota(jnp.int32, (SUB, NB), 0)
    lane_id = lax.broadcasted_iota(jnp.int32, (SUB, NB), 1)
    return sub_id, lane_id


def inverse_factor(left):
    count = NB // SUB
    sub_id, lane_id = lane_ids()
    eye = [jnp.where(lane_id == sub_id + SUB * i, 1.0, 0.0) for i in range(count)]
    right = list(eye)
    for k in range(0, NB, 4):
        b, s = divmod(k, SUB)
        r = [row(left[b], s + j) for j in range(4)]
        e = [row(right[b], s + j) for j in range(4)]
        a = [[lane(r[i], k + j) if j >= i else None for j in range(4)] for i in range(4)]
        scale = 1.0 / (a[0][0] * a[1][1] - a[0][1] * a[0][1])
        i00, i01, i11 = a[1][1] * scale, -a[0][1] * scale, a[0][0] * scale
        t = [(i00 * a[0][j] + i01 * a[1][j], i01 * a[0][j] + i11 * a[1][j]) for j in (2, 3)]
        s22 = a[2][2] - t[0][0] * a[0][2] - t[0][1] * a[1][2]
        s23 = a[2][3] - t[0][0] * a[0][3] - t[0][1] * a[1][3]
        s33 = a[3][3] - t[1][0] * a[0][3] - t[1][1] * a[1][3]
        scale = 1.0 / (s22 * s33 - s23 * s23)
        j22, j23, j33 = s33 * scale, -s23 * scale, s22 * scale

        def rank(x):
            x2 = x[2] - t[0][0] * x[0] - t[0][1] * x[1]
            x3 = x[3] - t[1][0] * x[0] - t[1][1] * x[1]
            q2, q3 = j22 * x2 + j23 * x3, j23 * x2 + j33 * x3
            u0 = i00 * x[0] + i01 * x[1] - t[0][0] * q2 - t[1][0] * q3
            u1 = i01 * x[0] + i11 * x[1] - t[0][1] * q2 - t[1][1] * q3
            return x2, x3, (u0, u1, q2, q3)

        l2, l3, lu = rank(r)
        e2, e3, eu = rank(e)
        for i in range(b, count):
            c = [lane(left[i], k + j) for j in range(4)]
            if i == b:
                c = [jnp.where(sub_id > s + 3, x, 0.0) for x in c]
            left[i] = left[i] - (c[0] * lu[0] + c[1] * lu[1]) - (c[2] * lu[2] + c[3] * lu[3])
            right[i] = right[i] - (c[0] * eu[0] + c[1] * eu[1]) - (c[2] * eu[2] + c[3] * eu[3])
        left[b] = jnp.where(sub_id == s + 2, l2, jnp.where(sub_id == s + 3, l3, left[b]))
        right[b] = jnp.where(sub_id == s + 2, e2, jnp.where(sub_id == s + 3, e3, right[b]))
    odd = (sub_id % 2) == 1
    out = []
    for i in range(count):
        diag = jnp.sum(left[i] * eye[i], axis=1, keepdims=True)
        below = jnp.sum(jnp.where(lane_id == sub_id + (SUB * i - 1), left[i], 0.0), axis=1, keepdims=True)
        diag, below = jnp.broadcast_to(diag, (SUB, NB)), jnp.broadcast_to(below, (SUB, NB))
        ratio = jnp.where(odd, below / pltpu.roll(diag, 1, 0), 0.0)
        rows = right[i] - ratio * pltpu.roll(right[i], 1, 0)
        out.append(rows * lax.rsqrt(diag - ratio * below))
    return out


def invert_kernel(rows, cols, ids_ref, state_hbm, panel_hbm, pack_ref, state_ref, panel_ref, sems):
    get_state = pltpu.make_async_copy(state_hbm, state_ref, sems.at[0])
    get_panel = pltpu.make_async_copy(panel_hbm, panel_ref, sems.at[1])
    get_state.start()
    get_panel.start()
    get_state.wait()
    count = NB // SUB
    sub_id, lane_id = lane_ids()
    held = [
        jnp.where(lane_id == sub_id + SUB * i, 1.0, 0.0) - state_ref[2 * NB + SUB * i : 2 * NB + SUB * i + SUB, :] for i in range(count)
    ]
    for k in range(0, NB, 2):
        b, s = divmod(k, SUB)
        one, two = row(held[b], s), row(held[b], s + 1)
        a11, a12, a21, a22 = lane(one, k), lane(one, k + 1), lane(two, k), lane(two, k + 1)
        scale = 1.0 / (a11 * a22 - a12 * a21)
        i11, i12, i21, i22 = a22 * scale, -a12 * scale, -a21 * scale, a11 * scale
        h1, h2 = lane_id == k, lane_id == k + 1
        o1 = jnp.where(h1, 1.0, jnp.where(h2, 0.0, one))
        o2 = jnp.where(h1, 0.0, jnp.where(h2, 1.0, two))
        n1, n2 = i11 * o1 + i12 * o2, i21 * o1 + i22 * o2
        for i in range(count):
            c1, c2 = lane(held[i], k), lane(held[i], k + 1)
            new = jnp.where(h1 | h2, 0.0, held[i]) - c1 * n1 - c2 * n2
            if i == b:
                new = jnp.where(sub_id == s, n1, jnp.where(sub_id == s + 1, n2, new))
            held[i] = new
    for i in range(count):
        pack_ref[SUB * i : SUB * i + SUB, :] = held[i]
    pack_ref[NB : 3 * NB, :] = state_ref[: 2 * NB, :]
    get_panel.wait()
    inverse, sign = state_ref[:NB, :], state_ref[NB : 2 * NB, :]
    y = mult(panel_ref[...], inverse, 1, 1)
    y_cols = jnp.concatenate([y[rows : rows + NB] - jnp.where(ids_ref[1] == 1, sign, 0.0), y[rows + NB :]], 0)
    pack_ref[3 * NB : 3 * NB + cols, :] = mult(y_cols, pack_ref[:NB, :])
    pack_ref[3 * NB + cols : 4 * NB + cols, :] = y[:NB] - jnp.where(ids_ref[0] == 1, sign, 0.0)
    pack_ref[4 * NB + cols :, :] = y[NB:rows]


def prepare_kernel(fold, slim, ids_ref, a_hbm, send_ref, panel_ref, sem):
    rows, col_count = a_hbm.shape[0], send_ref.shape[0]
    share, step, per = fold * slim, NB // col_count, NB // slim
    get_panel = pltpu.make_async_copy(a_hbm.at[:, 0, :], panel_ref, sem)
    get_panel.start()
    get_panel.wait()
    panel = panel_ref[...]
    first = jnp.where((ids_ref[0] == 0) & (ids_ref[1] == 0), 0.0, panel[:NB])
    panel = jnp.concatenate([first, panel[NB:]], 0)
    gram = mult(panel, panel, 0, 0)
    lead = jnp.where(ids_ref[0] == 1, first, 0.0)
    for m in range(rows // NB):
        k, f = divmod(m, fold)
        send_ref[k * per : (k + 1) * per, f * slim : (f + 1) * slim, :] = panel[m * NB : (m + 1) * NB].reshape(per, slim, NB)
    for c in range(col_count):
        send_ref[c, share : share + step, :] = gram[c * step : (c + 1) * step]
        send_ref[c, share + step : share + 2 * step, :] = lead[c * step : (c + 1) * step]


def relay_kernel(fold, slim, ids_ref, got_ref, send_ref):
    row_count = got_ref.shape[0]
    share = fold * slim
    mine = got_ref[ids_ref[0], :share, :]
    piece = jnp.sum(got_ref[:, share:, :], 0)
    send_ref[:, :share, :] = jnp.broadcast_to(mine[None], (fold * row_count,) + mine.shape)
    send_ref[:, share + slim :, :] = jnp.broadcast_to(piece[None], (fold * row_count,) + piece.shape)
    for f in range(fold):
        send_ref[f * row_count : (f + 1) * row_count, share : share + slim, :] = got_ref[:, f * slim : (f + 1) * slim, :]


def product_kernel(col_blocks, fold, slim, ids_ref, got_ref, a_ref, send_hbm, panel_hbm, send_ref, panel_ref, hold_ref, sems):
    col_count = got_ref.shape[0]
    rows, cols = a_ref.shape[0] // col_blocks, col_blocks * NB
    share, step, per = fold * slim, NB // col_count, NB // slim
    panel_ref[rows:, :] = got_ref[:, share : share + slim, :].reshape(cols, NB)
    for m in range(rows // NB):
        k, f = divmod(m, fold)
        panel_ref[m * NB : (m + 1) * NB, :] = got_ref[k * per : (k + 1) * per, f * slim : (f + 1) * slim, :].reshape(NB, NB)
    put_panel = pltpu.make_async_copy(panel_ref, panel_hbm, sems.at[0])
    put_panel.start()
    part = jnp.zeros((rows, NB), jnp.float32)
    for k in range(col_blocks):
        part = part + mult(a_ref[pl.ds(k, rows, col_blocks), :], panel_ref[rows + k * NB : rows + (k + 1) * NB, :])
    for m in range(rows // NB):
        k, f = divmod(m, fold)
        send_ref[k * per : (k + 1) * per, f * slim : (f + 1) * slim, :] = part[m * NB : (m + 1) * NB].reshape(per, slim, NB)
    put_share = pltpu.make_async_copy(send_ref.at[:, :share, :], send_hbm.at[:, :share, :], sems.at[1])
    put_share.start()
    hold_ref[...] = mult(panel_ref[:rows, :], part, 0, 0)
    lead = jnp.where(ids_ref[0] == 1, part[:NB], 0.0)
    for c in range(col_count):
        send_ref[c, share : share + step, :] = hold_ref[c * step : (c + 1) * step, :]
        send_ref[c, share + step : share + 2 * step, :] = lead[c * step : (c + 1) * step]
    put_piece = pltpu.make_async_copy(send_ref.at[:, share:, :], send_hbm.at[:, share:, :], sems.at[2])
    put_piece.start()
    put_panel.wait()
    put_share.wait()
    put_piece.wait()


def factor_kernel(share, step, got_ref, state_hbm, state_ref, hold_ref, lead_ref, sem):
    count = NB // SUB
    sub_id, lane_id = lane_ids()
    for c in range(got_ref.shape[0]):
        hold_ref[c * step : (c + 1) * step, :] = got_ref[c, share : share + step, :]
        lead_ref[c * step : (c + 1) * step, :] = got_ref[c, share + step : share + 2 * step, :]
    out = inverse_factor([hold_ref[SUB * i : SUB * i + SUB, :] for i in range(count)])
    for i in range(count):
        state_ref[SUB * i : SUB * i + SUB, :] = out[i]
    inverse = state_ref[:NB, :]
    lead = lead_ref[...]
    signs = jnp.where(jnp.sum(lead * inverse, axis=1, keepdims=True) >= 0, -1.0, 1.0)
    state_ref[2 * NB :, :] = signs * mult(lead, inverse, 1, 1)
    for i in range(count):
        here = jnp.where(lane_id == sub_id + SUB * i, 1.0, 0.0)
        state_ref[NB + SUB * i : NB + SUB * i + SUB, :] = here * signs[SUB * i : SUB * i + SUB]
    put_state = pltpu.make_async_copy(state_ref, state_hbm, sem)
    put_state.start()
    put_state.wait()


def spread_kernel(share, step, ids_ref, got_ref, own_ref, state_hbm, send_ref, state_ref, sem):
    get_state = pltpu.make_async_copy(state_hbm.at[: 2 * NB, :], state_ref, sem)
    get_state.start()
    total = jnp.sum(got_ref[...], 0)
    get_state.wait()
    own = own_ref[...]
    line = jnp.sum(state_ref[NB:, :], axis=0, keepdims=True)
    turned = mult(total, state_ref[:NB, :], 1, 1)
    rows = turned[:share] - own[:share] * line
    lead = jnp.where(ids_ref[0] == 1, turned[share + step :] - 0.5 * own[share + step :] * line, 0.0)
    out = jnp.concatenate([rows, total[share : share + step], lead], 0)
    send_ref[...] = jnp.broadcast_to(out[None], send_ref.shape)


def halves(value):
    high = value.astype(jnp.bfloat16)
    return high, (value - high.astype(jnp.float32)).astype(jnp.bfloat16)


def mult_half(left, right):
    return lax.dot_general(left, right, (((1,), (1,)), ((), ())), preferred_element_type=jnp.float32)


def update_kernel(
    col_blocks, fold, slim, got_ref, pack_ref, a_ref, out_ref, high_ref, low_ref, hold_ref, lead_ref, new_ref, sems
):
    col_count = got_ref.shape[0]
    share, step, per = fold * slim, NB // col_count, NB // slim
    cols = col_blocks * NB
    for c in range(col_count):
        hold_ref[c * step : (c + 1) * step, :] = got_ref[c, share + slim : share + slim + step, :]
        lead_ref[c * step : (c + 1) * step, :] = got_ref[c, share + slim + step : share + slim + 2 * step, :]
    coupling, inverse, v = pack_ref[:NB, :], pack_ref[NB : 2 * NB, :], pack_ref[3 * NB : 3 * NB + cols, :]
    y_ref = pack_ref.at[3 * NB + cols :, :]
    cross = jnp.sum(pack_ref[2 * NB : 3 * NB, :], axis=1, keepdims=True) * lead_ref[...]
    middle = mult(mult(inverse, hold_ref[...]), inverse, 1, 1) - cross - cross.T
    z_cols = got_ref[:, share : share + slim, :].reshape(cols, NB)
    u = mult(z_cols - mult(v, middle), coupling, 1, 1)
    for at, part in enumerate((u, v)):
        high, low = halves(part)
        high_ref[:, at * NB : (at + 1) * NB] = high
        low_ref[:, at * NB : (at + 1) * NB] = low
    right_high, right_low = high_ref[...], low_ref[...]
    copies = []
    for k in range(a_ref.shape[0] // (fold * cols)):
        z = [got_ref[k * per : (k + 1) * per, f * slim : (f + 1) * slim, :].reshape(NB, NB) for f in range(fold)]
        y = y_ref[k * fold * NB : (k + 1) * fold * NB, :]
        high, low = halves(jnp.concatenate([y, jnp.concatenate(z, 0)], 1))
        change = mult_half(low, right_high) + mult_half(high, right_low) + mult_half(high, right_high)
        for n in range(col_blocks):
            here = pl.ds(k * fold * cols + n, fold * NB, col_blocks)
            new_ref[here, :] = a_ref[here, :] - change[:, n * NB : (n + 1) * NB]
        there = pl.ds(k * fold * cols, fold * cols)
        copy = pltpu.make_async_copy(new_ref.at[there, :], out_ref.at[there, :], sems.at[k])
        copy.start()
        copies.append(copy)
    for copy in copies:
        copy.wait()


def exchange(pieces, axis):
    return lax.all_to_all(pieces, axis, 0, 0)


def body(kernel):
    row_blocks, _, _, col_blocks, _, _ = kernel.shape
    rows, cols = row_blocks * NB, col_blocks * NB
    row_count, col_count = lax.axis_size("row"), lax.axis_size("col")
    fold = col_count // row_count
    row_index, col_index = lax.axis_index("row"), lax.axis_index("col")
    ids = jnp.stack([row_index, col_index]).astype(jnp.int32)
    lines = kernel.reshape(rows * col_blocks, NB)
    slim, step = cols // col_count, NB // col_count
    share = fold * slim
    pad = 2 * step

    def hbm(*dims):
        return pltpu.HBM(dims, jnp.float32)

    def relay(got):
        return pl.pallas_call(
            lambda *refs: relay_kernel(fold, slim, *refs),
            out_shape=shape(col_count, share + slim + pad, NB),
            in_specs=[SMEM, VMEM],
            out_specs=VMEM,
            compiler_params=PARAMS,
            name="relay",
            cost_estimate=cost(1_000_000, 1_000_000),
        )(ids, got)

    send = pl.pallas_call(
        lambda *refs: prepare_kernel(fold, slim, *refs),
        out_shape=shape(col_count, share + pad, NB),
        in_specs=[SMEM, HBM],
        out_specs=VMEM,
        scratch_shapes=[pltpu.VMEM((rows, NB), jnp.float32), pltpu.SemaphoreType.DMA],
        compiler_params=PARAMS,
        name="prepare",
        cost_estimate=cost(2 * rows * NB * NB * 6, 3_000_000),
    )(ids, pltpu.with_memory_space_constraint(kernel.reshape(rows, col_blocks, NB), pltpu.HBM))
    got = exchange(send, "col")
    own = got[1]
    got = jnp.broadcast_to(got[0][None], (row_count,) + got.shape[1:])
    got = exchange(relay(exchange(got, "row")), "col")

    send, panel = pl.pallas_call(
        lambda *refs: product_kernel(col_blocks, fold, slim, *refs),
        out_shape=(hbm(col_count, share + pad, NB), hbm(rows + cols, NB)),
        in_specs=[SMEM, VMEM, VMEM],
        out_specs=(HBM, HBM),
        scratch_shapes=[
            pltpu.VMEM((col_count, share + pad, NB), jnp.float32),
            pltpu.VMEM((rows + cols, NB), jnp.float32),
            pltpu.VMEM((NB, NB), jnp.float32),
            pltpu.SemaphoreType.DMA((3,)),
        ],
        compiler_params=PARAMS,
        name="product",
        cost_estimate=cost(2 * rows * cols * NB * 6, 4_000_000),
    )(ids, got, lines)
    summed = exchange(send, "col")
    state = pl.pallas_call(
        lambda *refs: factor_kernel(share + slim, step, *refs),
        out_shape=hbm(3 * NB, NB),
        in_specs=[VMEM],
        out_specs=HBM,
        scratch_shapes=[pltpu.VMEM((3 * NB, NB), jnp.float32)]
        + [pltpu.VMEM((NB, NB), jnp.float32)] * 2
        + [pltpu.SemaphoreType.DMA],
        compiler_params=PARAMS,
        name="factor",
        cost_estimate=cost(4_000_000_000, 2_000_000),
    )(got)

    state = pltpu.with_memory_space_constraint(state, pltpu.HBM)
    panel = pltpu.with_memory_space_constraint(panel, pltpu.HBM)

    send = pl.pallas_call(
        lambda *refs: spread_kernel(share, step, *refs),
        out_shape=shape(row_count, share + pad, NB),
        in_specs=[SMEM, VMEM, VMEM, HBM],
        out_specs=VMEM,
        scratch_shapes=[pltpu.VMEM((2 * NB, NB), jnp.float32), pltpu.SemaphoreType.DMA],
        compiler_params=PARAMS,
        name="spread",
        cost_estimate=cost(10_000_000, 1_000_000),
    )(ids, summed, own, state)
    got = exchange(send, "row")
    pack = pl.pallas_call(
        lambda *refs: invert_kernel(rows, cols, *refs),
        out_shape=shape(3 * NB + cols + rows, NB),
        in_specs=[SMEM, HBM, HBM],
        out_specs=VMEM,
        scratch_shapes=[
            pltpu.VMEM((3 * NB, NB), jnp.float32),
            pltpu.VMEM((rows + cols, NB), jnp.float32),
            pltpu.SemaphoreType.DMA((2,)),
        ],
        compiler_params=PARAMS,
        name="invert",
        cost_estimate=cost(4_000_000_000, 1_000_000),
    )(ids, state, panel)
    got, pack = lax.optimization_barrier((got, pack))
    last = exchange(relay(got), "col")

    updated = pl.pallas_call(
        lambda *refs: update_kernel(col_blocks, fold, slim, *refs),
        out_shape=shape(rows * col_blocks, NB),
        in_specs=[VMEM] * 3,
        out_specs=pl.BlockSpec(memory_space=pl.ANY),
        scratch_shapes=[
            pltpu.VMEM((cols, 2 * NB), jnp.bfloat16),
            pltpu.VMEM((cols, 2 * NB), jnp.bfloat16),
            pltpu.VMEM((NB, NB), jnp.float32),
            pltpu.VMEM((NB, NB), jnp.float32),
            pltpu.VMEM((rows * col_blocks, NB), jnp.float32),
            pltpu.SemaphoreType.DMA((row_blocks // fold,)),
        ],
        compiler_params=PARAMS,
        name="update",
        cost_estimate=cost(4 * rows * cols * NB * 6, 6_000_000),
    )(last, pack, lines)
    return updated.reshape(kernel.shape)


def solution(mesh):
    return jax.shard_map(
        body,
        mesh=mesh,
        in_specs=(P(None, "row", None, None, "col", None),),
        out_specs=P(None, "row", None, None, "col", None),
        check_vma=False,
    )
```

```python
import jax
import jax.numpy as jnp
from jax import lax
from jax.experimental import pallas as pl
from jax.experimental.pallas import tpu as pltpu
from jax.sharding import PartitionSpec as P

NB = 128
SUB = 8
VMEM = pl.BlockSpec(memory_space=pltpu.VMEM)
SMEM = pl.BlockSpec(memory_space=pltpu.SMEM)
HBM = pl.BlockSpec(memory_space=pltpu.HBM)
PARAMS = pltpu.CompilerParams(vmem_limit_bytes=40 * 1024 * 1024)


def mult(left, right, left_dim=1, right_dim=0):
    return lax.dot_general(
        left,
        right,
        (((left_dim,), (right_dim,)), ((), ())),
        precision=lax.Precision.HIGHEST,
        preferred_element_type=jnp.float32,
    )


def shape(*dims):
    return jax.ShapeDtypeStruct(dims, jnp.float32)


def cost(flops, nbytes):
    return pl.CostEstimate(flops=flops, bytes_accessed=nbytes, transcendentals=0)


def lane(block, k):
    return jnp.broadcast_to(block[:, k : k + 1], (SUB, NB))


def row(block, s):
    return jnp.broadcast_to(block[s : s + 1, :], (SUB, NB))


def lane_ids():
    sub_id = lax.broadcasted_iota(jnp.int32, (SUB, NB), 0)
    lane_id = lax.broadcasted_iota(jnp.int32, (SUB, NB), 1)
    return sub_id, lane_id


def inverse_factor(left):
    count = NB // SUB
    sub_id, lane_id = lane_ids()
    eye = [jnp.where(lane_id == sub_id + SUB * i, 1.0, 0.0) for i in range(count)]
    right = list(eye)
    for k in range(0, NB, 4):
        b, s = divmod(k, SUB)
        r = [row(left[b], s + j) for j in range(4)]
        e = [row(right[b], s + j) for j in range(4)]
        a = [[lane(r[i], k + j) if j >= i else None for j in range(4)] for i in range(4)]
        scale = 1.0 / (a[0][0] * a[1][1] - a[0][1] * a[0][1])
        i00, i01, i11 = a[1][1] * scale, -a[0][1] * scale, a[0][0] * scale
        t = [(i00 * a[0][j] + i01 * a[1][j], i01 * a[0][j] + i11 * a[1][j]) for j in (2, 3)]
        s22 = a[2][2] - t[0][0] * a[0][2] - t[0][1] * a[1][2]
        s23 = a[2][3] - t[0][0] * a[0][3] - t[0][1] * a[1][3]
        s33 = a[3][3] - t[1][0] * a[0][3] - t[1][1] * a[1][3]
        scale = 1.0 / (s22 * s33 - s23 * s23)
        j22, j23, j33 = s33 * scale, -s23 * scale, s22 * scale

        def rank(x):
            x2 = x[2] - t[0][0] * x[0] - t[0][1] * x[1]
            x3 = x[3] - t[1][0] * x[0] - t[1][1] * x[1]
            q2, q3 = j22 * x2 + j23 * x3, j23 * x2 + j33 * x3
            u0 = i00 * x[0] + i01 * x[1] - t[0][0] * q2 - t[1][0] * q3
            u1 = i01 * x[0] + i11 * x[1] - t[0][1] * q2 - t[1][1] * q3
            return x2, x3, (u0, u1, q2, q3)

        l2, l3, lu = rank(r)
        e2, e3, eu = rank(e)
        for i in range(b, count):
            c = [lane(left[i], k + j) for j in range(4)]
            if i == b:
                c = [jnp.where(sub_id > s + 3, x, 0.0) for x in c]
            left[i] = left[i] - (c[0] * lu[0] + c[1] * lu[1]) - (c[2] * lu[2] + c[3] * lu[3])
            right[i] = right[i] - (c[0] * eu[0] + c[1] * eu[1]) - (c[2] * eu[2] + c[3] * eu[3])
        left[b] = jnp.where(sub_id == s + 2, l2, jnp.where(sub_id == s + 3, l3, left[b]))
        right[b] = jnp.where(sub_id == s + 2, e2, jnp.where(sub_id == s + 3, e3, right[b]))
    odd = (sub_id % 2) == 1
    out = []
    for i in range(count):
        diag = jnp.sum(left[i] * eye[i], axis=1, keepdims=True)
        below = jnp.sum(jnp.where(lane_id == sub_id + (SUB * i - 1), left[i], 0.0), axis=1, keepdims=True)
        diag, below = jnp.broadcast_to(diag, (SUB, NB)), jnp.broadcast_to(below, (SUB, NB))
        ratio = jnp.where(odd, below / pltpu.roll(diag, 1, 0), 0.0)
        rows = right[i] - ratio * pltpu.roll(right[i], 1, 0)
        out.append(rows * lax.rsqrt(diag - ratio * below))
    return out


def invert_kernel(rows, cols, ids_ref, state_hbm, panel_hbm, pack_ref, state_ref, panel_ref, sems):
    get_state = pltpu.make_async_copy(state_hbm, state_ref, sems.at[0])
    get_panel = pltpu.make_async_copy(panel_hbm, panel_ref, sems.at[1])
    get_state.start()
    get_panel.start()
    get_state.wait()
    count = NB // SUB
    sub_id, lane_id = lane_ids()
    held = [
        jnp.where(lane_id == sub_id + SUB * i, 1.0, 0.0) - state_ref[2 * NB + SUB * i : 2 * NB + SUB * i + SUB, :] for i in range(count)
    ]
    for k in range(0, NB, 2):
        b, s = divmod(k, SUB)
        one, two = row(held[b], s), row(held[b], s + 1)
        a11, a12, a21, a22 = lane(one, k), lane(one, k + 1), lane(two, k), lane(two, k + 1)
        scale = 1.0 / (a11 * a22 - a12 * a21)
        i11, i12, i21, i22 = a22 * scale, -a12 * scale, -a21 * scale, a11 * scale
        h1, h2 = lane_id == k, lane_id == k + 1
        o1 = jnp.where(h1, 1.0, jnp.where(h2, 0.0, one))
        o2 = jnp.where(h1, 0.0, jnp.where(h2, 1.0, two))
        n1, n2 = i11 * o1 + i12 * o2, i21 * o1 + i22 * o2
        for i in range(count):
            c1, c2 = lane(held[i], k), lane(held[i], k + 1)
            new = jnp.where(h1 | h2, 0.0, held[i]) - c1 * n1 - c2 * n2
            if i == b:
                new = jnp.where(sub_id == s, n1, jnp.where(sub_id == s + 1, n2, new))
            held[i] = new
    for i in range(count):
        pack_ref[SUB * i : SUB * i + SUB, :] = held[i]
    pack_ref[NB : 3 * NB, :] = state_ref[: 2 * NB, :]
    get_panel.wait()
    inverse, sign = state_ref[:NB, :], state_ref[NB : 2 * NB, :]
    y = mult(panel_ref[...], inverse, 1, 1)
    y_cols = jnp.concatenate([y[rows : rows + NB] - jnp.where(ids_ref[1] == 1, sign, 0.0), y[rows + NB :]], 0)
    pack_ref[3 * NB : 3 * NB + cols, :] = mult(y_cols, pack_ref[:NB, :])
    pack_ref[3 * NB + cols : 4 * NB + cols, :] = y[:NB] - jnp.where(ids_ref[0] == 1, sign, 0.0)
    pack_ref[4 * NB + cols :, :] = y[NB:rows]


def prepare_kernel(fold, slim, ids_ref, a_hbm, send_ref, panel_ref, sem):
    rows, col_count = a_hbm.shape[0], send_ref.shape[0]
    share, step, per = fold * slim, NB // col_count, NB // slim
    get_panel = pltpu.make_async_copy(a_hbm.at[:, 0, :], panel_ref, sem)
    get_panel.start()
    get_panel.wait()
    panel = panel_ref[...]
    first = jnp.where((ids_ref[0] == 0) & (ids_ref[1] == 0), 0.0, panel[:NB])
    panel = jnp.concatenate([first, panel[NB:]], 0)
    gram = mult(panel, panel, 0, 0)
    lead = jnp.where(ids_ref[0] == 1, first, 0.0)
    for m in range(rows // NB):
        k, f = divmod(m, fold)
        send_ref[k * per : (k + 1) * per, f * slim : (f + 1) * slim, :] = panel[m * NB : (m + 1) * NB].reshape(per, slim, NB)
    for c in range(col_count):
        send_ref[c, share : share + step, :] = gram[c * step : (c + 1) * step]
        send_ref[c, share + step : share + 2 * step, :] = lead[c * step : (c + 1) * step]


def relay_kernel(fold, slim, ids_ref, got_ref, send_ref):
    row_count = got_ref.shape[0]
    share = fold * slim
    mine = got_ref[ids_ref[0], :share, :]
    piece = jnp.sum(got_ref[:, share:, :], 0)
    send_ref[:, :share, :] = jnp.broadcast_to(mine[None], (fold * row_count,) + mine.shape)
    send_ref[:, share + slim :, :] = jnp.broadcast_to(piece[None], (fold * row_count,) + piece.shape)
    for f in range(fold):
        send_ref[f * row_count : (f + 1) * row_count, share : share + slim, :] = got_ref[:, f * slim : (f + 1) * slim, :]


def thirds(value):
    one = value.astype(jnp.bfloat16)
    rest = value - one.astype(jnp.float32)
    two = rest.astype(jnp.bfloat16)
    return one, two, (rest - two.astype(jnp.float32)).astype(jnp.bfloat16)


def mult_packed(left, right):
    one, two, three = thirds(left)
    first, second, third = thirds(right)
    pair = jnp.concatenate([first, second], 1)
    width = right.shape[1]

    def dot(x, y):
        return lax.dot_general(x, y, (((1,), (0,)), ((), ())), preferred_element_type=jnp.float32)

    high, low = dot(one, pair), dot(two, pair)
    tail = dot(one, third) + dot(three, first)
    return ((low[:, width:] + tail) + (high[:, width:] + low[:, :width])) + high[:, :width]


def product_kernel(col_blocks, fold, slim, ids_ref, got_ref, a_ref, send_hbm, send_ref, hold_ref, sems):
    col_count = got_ref.shape[0]
    rows, cols = a_ref.shape[0] // col_blocks, col_blocks * NB
    share, step, per = fold * slim, NB // col_count, NB // slim
    block = jnp.concatenate([a_ref[pl.ds(k, rows, col_blocks), :] for k in range(col_blocks)], 1)
    part = mult_packed(block, got_ref[:, share : share + slim, :].reshape(cols, NB))
    panel = []
    for m in range(rows // NB):
        k, f = divmod(m, fold)
        send_ref[k * per : (k + 1) * per, f * slim : (f + 1) * slim, :] = part[m * NB : (m + 1) * NB].reshape(per, slim, NB)
        panel.append(got_ref[k * per : (k + 1) * per, f * slim : (f + 1) * slim, :].reshape(NB, NB))
    put_share = pltpu.make_async_copy(send_ref.at[:, :share, :], send_hbm.at[:, :share, :], sems.at[0])
    put_share.start()
    hold_ref[...] = mult(jnp.concatenate(panel, 0), part, 0, 0)
    lead = jnp.where(ids_ref[0] == 1, part[:NB], 0.0)
    for c in range(col_count):
        send_ref[c, share : share + step, :] = hold_ref[c * step : (c + 1) * step, :]
        send_ref[c, share + step : share + 2 * step, :] = lead[c * step : (c + 1) * step]
    put_piece = pltpu.make_async_copy(send_ref.at[:, share:, :], send_hbm.at[:, share:, :], sems.at[1])
    put_piece.start()
    put_share.wait()
    put_piece.wait()


def factor_kernel(rows, fold, slim, step, got_ref, state_hbm, panel_hbm, state_ref, panel_ref, hold_ref, lead_ref, sems):
    share, per = (fold + 1) * slim, NB // slim
    for m in range(rows // NB):
        k, f = divmod(m, fold)
        panel_ref[m * NB : (m + 1) * NB, :] = got_ref[k * per : (k + 1) * per, f * slim : (f + 1) * slim, :].reshape(NB, NB)
    panel_ref[rows:, :] = got_ref[:, fold * slim : share, :].reshape(panel_ref.shape[0] - rows, NB)
    put_panel = pltpu.make_async_copy(panel_ref, panel_hbm, sems.at[1])
    put_panel.start()
    count = NB // SUB
    sub_id, lane_id = lane_ids()
    for c in range(got_ref.shape[0]):
        hold_ref[c * step : (c + 1) * step, :] = got_ref[c, share : share + step, :]
        lead_ref[c * step : (c + 1) * step, :] = got_ref[c, share + step : share + 2 * step, :]
    out = inverse_factor([hold_ref[SUB * i : SUB * i + SUB, :] for i in range(count)])
    for i in range(count):
        state_ref[SUB * i : SUB * i + SUB, :] = out[i]
    inverse = state_ref[:NB, :]
    lead = lead_ref[...]
    signs = jnp.where(jnp.sum(lead * inverse, axis=1, keepdims=True) >= 0, -1.0, 1.0)
    state_ref[2 * NB :, :] = signs * mult(lead, inverse, 1, 1)
    for i in range(count):
        here = jnp.where(lane_id == sub_id + SUB * i, 1.0, 0.0)
        state_ref[NB + SUB * i : NB + SUB * i + SUB, :] = here * signs[SUB * i : SUB * i + SUB]
    put_state = pltpu.make_async_copy(state_ref, state_hbm, sems.at[0])
    put_state.start()
    put_state.wait()
    put_panel.wait()


def spread_kernel(share, step, ids_ref, got_hbm, own_ref, state_hbm, send_ref, got_ref, state_ref, sems):
    get_got = pltpu.make_async_copy(got_hbm, got_ref, sems.at[0])
    get_state = pltpu.make_async_copy(state_hbm.at[: 2 * NB, :], state_ref, sems.at[1])
    get_got.start()
    get_state.start()
    get_got.wait()
    total = jnp.sum(got_ref[...], 0)
    get_state.wait()
    own = own_ref[...]
    line = jnp.sum(state_ref[NB:, :], axis=0, keepdims=True)
    turned = mult(total, state_ref[:NB, :], 1, 1)
    rows = turned[:share] - own[:share] * line
    lead = jnp.where(ids_ref[0] == 1, turned[share + step :] - 0.5 * own[share + step :] * line, 0.0)
    out = jnp.concatenate([rows, total[share : share + step], lead], 0)
    send_ref[...] = jnp.broadcast_to(out[None], send_ref.shape)


def halves(value):
    high = value.astype(jnp.bfloat16)
    return high, (value - high.astype(jnp.float32)).astype(jnp.bfloat16)


def mult_half(left, right, right_dim=1):
    return lax.dot_general(left, right, (((1,), (right_dim,)), ((), ())), preferred_element_type=jnp.float32)


def mult_halves(left, right, right_dim):
    high, low = halves(left)
    right_high, right_low = halves(right)
    small = mult_half(low, right_high, right_dim) + mult_half(high, right_low, right_dim)
    return small + mult_half(high, right_high, right_dim)


def update_kernel(
    col_blocks, fold, slim, got_ref, pack_ref, a_ref, out_ref, high_ref, low_ref, hold_ref, lead_ref, new_ref, sems
):
    col_count = got_ref.shape[0]
    share, step, per = fold * slim, NB // col_count, NB // slim
    cols = col_blocks * NB
    for c in range(col_count):
        hold_ref[c * step : (c + 1) * step, :] = got_ref[c, share + slim : share + slim + step, :]
        lead_ref[c * step : (c + 1) * step, :] = got_ref[c, share + slim + step : share + slim + 2 * step, :]
    coupling, inverse, v = pack_ref[:NB, :], pack_ref[NB : 2 * NB, :], pack_ref[3 * NB : 3 * NB + cols, :]
    y_ref = pack_ref.at[3 * NB + cols :, :]
    cross = jnp.sum(pack_ref[2 * NB : 3 * NB, :], axis=1, keepdims=True) * lead_ref[...]
    middle = mult(mult(inverse, hold_ref[...]), inverse, 1, 1) - cross - cross.T
    z_cols = got_ref[:, share : share + slim, :].reshape(cols, NB)
    u = mult_halves(z_cols - mult_halves(v, middle, 0), coupling, 1)
    for at, part in enumerate((u, v)):
        high, low = halves(part)
        high_ref[:, at * NB : (at + 1) * NB] = high
        low_ref[:, at * NB : (at + 1) * NB] = low
    right_high, right_low = high_ref[...], low_ref[...]
    copies = []
    for k in range(a_ref.shape[0] // (fold * cols)):
        z = [got_ref[k * per : (k + 1) * per, f * slim : (f + 1) * slim, :].reshape(NB, NB) for f in range(fold)]
        y = y_ref[k * fold * NB : (k + 1) * fold * NB, :]
        high, low = halves(jnp.concatenate([y, jnp.concatenate(z, 0)], 1))
        change = mult_half(low, right_high) + mult_half(high, right_low) + mult_half(high, right_high)
        for n in range(col_blocks):
            here = pl.ds(k * fold * cols + n, fold * NB, col_blocks)
            new_ref[here, :] = a_ref[here, :] - change[:, n * NB : (n + 1) * NB]
        there = pl.ds(k * fold * cols, fold * cols)
        copy = pltpu.make_async_copy(new_ref.at[there, :], out_ref.at[there, :], sems.at[k])
        copy.start()
        copies.append(copy)
    for copy in copies:
        copy.wait()


def exchange(pieces, axis):
    return lax.all_to_all(pieces, axis, 0, 0)


def body(kernel):
    row_blocks, _, _, col_blocks, _, _ = kernel.shape
    rows, cols = row_blocks * NB, col_blocks * NB
    row_count, col_count = lax.axis_size("row"), lax.axis_size("col")
    fold = col_count // row_count
    row_index, col_index = lax.axis_index("row"), lax.axis_index("col")
    ids = jnp.stack([row_index, col_index]).astype(jnp.int32)
    lines = kernel.reshape(rows * col_blocks, NB)
    slim, step = cols // col_count, NB // col_count
    share = fold * slim
    pad = 2 * step

    def hbm(*dims):
        return pltpu.HBM(dims, jnp.float32)

    def relay(got):
        return pl.pallas_call(
            lambda *refs: relay_kernel(fold, slim, *refs),
            out_shape=shape(col_count, share + slim + pad, NB),
            in_specs=[SMEM, VMEM],
            out_specs=VMEM,
            compiler_params=PARAMS,
            name="relay",
            cost_estimate=cost(1_000_000, 1_000_000),
        )(ids, got)

    send = pl.pallas_call(
        lambda *refs: prepare_kernel(fold, slim, *refs),
        out_shape=shape(col_count, share + pad, NB),
        in_specs=[SMEM, HBM],
        out_specs=VMEM,
        scratch_shapes=[pltpu.VMEM((rows, NB), jnp.float32), pltpu.SemaphoreType.DMA],
        compiler_params=PARAMS,
        name="prepare",
        cost_estimate=cost(2 * rows * NB * NB * 6, 3_000_000),
    )(ids, pltpu.with_memory_space_constraint(kernel.reshape(rows, col_blocks, NB), pltpu.HBM))
    got = exchange(send, "col")
    own = got[1]
    got = jnp.broadcast_to(got[0][None], (row_count,) + got.shape[1:])
    got = exchange(relay(exchange(got, "row")), "col")

    send = pl.pallas_call(
        lambda *refs: product_kernel(col_blocks, fold, slim, *refs),
        out_shape=hbm(col_count, share + pad, NB),
        in_specs=[SMEM, VMEM, VMEM],
        out_specs=HBM,
        scratch_shapes=[
            pltpu.VMEM((col_count, share + pad, NB), jnp.float32),
            pltpu.VMEM((NB, NB), jnp.float32),
            pltpu.SemaphoreType.DMA((2,)),
        ],
        compiler_params=PARAMS,
        name="product",
        cost_estimate=cost(2 * rows * cols * NB * 6, 4_000_000),
    )(ids, got, lines)
    summed = exchange(send, "col")
    state, panel = pl.pallas_call(
        lambda *refs: factor_kernel(rows, fold, slim, step, *refs),
        out_shape=(hbm(3 * NB, NB), hbm(rows + cols, NB)),
        in_specs=[VMEM],
        out_specs=(HBM, HBM),
        scratch_shapes=[pltpu.VMEM((3 * NB, NB), jnp.float32), pltpu.VMEM((rows + cols, NB), jnp.float32)]
        + [pltpu.VMEM((NB, NB), jnp.float32)] * 2
        + [pltpu.SemaphoreType.DMA((2,))],
        compiler_params=PARAMS,
        name="factor",
        cost_estimate=cost(4_000_000_000, 2_000_000),
    )(got)
    state = pltpu.with_memory_space_constraint(state, pltpu.HBM)
    panel = pltpu.with_memory_space_constraint(panel, pltpu.HBM)

    send = pl.pallas_call(
        lambda *refs: spread_kernel(share, step, *refs),
        out_shape=shape(row_count, share + pad, NB),
        in_specs=[SMEM, HBM, VMEM, HBM],
        out_specs=VMEM,
        scratch_shapes=[
            pltpu.VMEM((col_count, share + pad, NB), jnp.float32),
            pltpu.VMEM((2 * NB, NB), jnp.float32),
            pltpu.SemaphoreType.DMA((2,)),
        ],
        compiler_params=PARAMS,
        name="spread",
        cost_estimate=cost(10_000_000, 1_000_000),
    )(ids, summed, own, state)
    got = exchange(send, "row")
    pack = pl.pallas_call(
        lambda *refs: invert_kernel(rows, cols, *refs),
        out_shape=shape(3 * NB + cols + rows, NB),
        in_specs=[SMEM, HBM, HBM],
        out_specs=VMEM,
        scratch_shapes=[
            pltpu.VMEM((3 * NB, NB), jnp.float32),
            pltpu.VMEM((rows + cols, NB), jnp.float32),
            pltpu.SemaphoreType.DMA((2,)),
        ],
        compiler_params=PARAMS,
        name="invert",
        cost_estimate=cost(4_000_000_000, 1_000_000),
    )(ids, state, panel)
    got, pack = lax.optimization_barrier((got, pack))
    last = exchange(relay(got), "col")

    updated = pl.pallas_call(
        lambda *refs: update_kernel(col_blocks, fold, slim, *refs),
        out_shape=shape(rows * col_blocks, NB),
        in_specs=[VMEM] * 3,
        out_specs=pl.BlockSpec(memory_space=pl.ANY),
        scratch_shapes=[
            pltpu.VMEM((cols, 2 * NB), jnp.bfloat16),
            pltpu.VMEM((cols, 2 * NB), jnp.bfloat16),
            pltpu.VMEM((NB, NB), jnp.float32),
            pltpu.VMEM((NB, NB), jnp.float32),
            pltpu.VMEM((rows * col_blocks, NB), jnp.float32),
            pltpu.SemaphoreType.DMA((row_blocks // fold,)),
        ],
        compiler_params=PARAMS,
        name="update",
        cost_estimate=cost(4 * rows * cols * NB * 6, 6_000_000),
    )(last, pack, lines)
    return updated.reshape(kernel.shape)


def solution(mesh):
    return jax.shard_map(
        body,
        mesh=mesh,
        in_specs=(P(None, "row", None, None, "col", None),),
        out_specs=P(None, "row", None, None, "col", None),
        check_vma=False,
    )
```

```python
import jax
import jax.numpy as jnp
from jax import lax
from jax.experimental import pallas as pl
from jax.experimental.pallas import tpu as pltpu
from jax.sharding import PartitionSpec as P

NB = 128
SUB = 8
VMEM = pl.BlockSpec(memory_space=pltpu.VMEM)
SMEM = pl.BlockSpec(memory_space=pltpu.SMEM)
HBM = pl.BlockSpec(memory_space=pltpu.HBM)
PARAMS = pltpu.CompilerParams(vmem_limit_bytes=40 * 1024 * 1024)


def mult(left, right, left_dim=1, right_dim=0):
    return lax.dot_general(
        left,
        right,
        (((left_dim,), (right_dim,)), ((), ())),
        precision=lax.Precision.HIGHEST,
        preferred_element_type=jnp.float32,
    )


def shape(*dims):
    return jax.ShapeDtypeStruct(dims, jnp.float32)


def cost(flops, nbytes):
    return pl.CostEstimate(flops=flops, bytes_accessed=nbytes, transcendentals=0)


def lane(block, k):
    return jnp.broadcast_to(block[:, k : k + 1], (SUB, NB))


def row(block, s):
    return jnp.broadcast_to(block[s : s + 1, :], (SUB, NB))


def lane_ids():
    sub_id = lax.broadcasted_iota(jnp.int32, (SUB, NB), 0)
    lane_id = lax.broadcasted_iota(jnp.int32, (SUB, NB), 1)
    return sub_id, lane_id


def inverse_factor(left):
    count = NB // SUB
    sub_id, lane_id = lane_ids()
    eye = [jnp.where(lane_id == sub_id + SUB * i, 1.0, 0.0) for i in range(count)]
    right = list(eye)
    for k in range(0, NB, 4):
        b, s = divmod(k, SUB)
        r = [row(left[b], s + j) for j in range(4)]
        e = [row(right[b], s + j) for j in range(4)]
        a = [[lane(r[i], k + j) if j >= i else None for j in range(4)] for i in range(4)]
        scale = 1.0 / (a[0][0] * a[1][1] - a[0][1] * a[0][1])
        i00, i01, i11 = a[1][1] * scale, -a[0][1] * scale, a[0][0] * scale
        t = [(i00 * a[0][j] + i01 * a[1][j], i01 * a[0][j] + i11 * a[1][j]) for j in (2, 3)]
        s22 = a[2][2] - t[0][0] * a[0][2] - t[0][1] * a[1][2]
        s23 = a[2][3] - t[0][0] * a[0][3] - t[0][1] * a[1][3]
        s33 = a[3][3] - t[1][0] * a[0][3] - t[1][1] * a[1][3]
        scale = 1.0 / (s22 * s33 - s23 * s23)
        j22, j23, j33 = s33 * scale, -s23 * scale, s22 * scale

        def rank(x):
            x2 = x[2] - t[0][0] * x[0] - t[0][1] * x[1]
            x3 = x[3] - t[1][0] * x[0] - t[1][1] * x[1]
            q2, q3 = j22 * x2 + j23 * x3, j23 * x2 + j33 * x3
            u0 = i00 * x[0] + i01 * x[1] - t[0][0] * q2 - t[1][0] * q3
            u1 = i01 * x[0] + i11 * x[1] - t[0][1] * q2 - t[1][1] * q3
            return x2, x3, (u0, u1, q2, q3)

        l2, l3, lu = rank(r)
        e2, e3, eu = rank(e)
        for i in range(b, count):
            c = [lane(left[i], k + j) for j in range(4)]
            if i == b:
                c = [jnp.where(sub_id > s + 3, x, 0.0) for x in c]
            left[i] = left[i] - (c[0] * lu[0] + c[1] * lu[1]) - (c[2] * lu[2] + c[3] * lu[3])
            right[i] = right[i] - (c[0] * eu[0] + c[1] * eu[1]) - (c[2] * eu[2] + c[3] * eu[3])
        left[b] = jnp.where(sub_id == s + 2, l2, jnp.where(sub_id == s + 3, l3, left[b]))
        right[b] = jnp.where(sub_id == s + 2, e2, jnp.where(sub_id == s + 3, e3, right[b]))
    odd = (sub_id % 2) == 1
    out = []
    for i in range(count):
        diag = jnp.sum(left[i] * eye[i], axis=1, keepdims=True)
        below = jnp.sum(jnp.where(lane_id == sub_id + (SUB * i - 1), left[i], 0.0), axis=1, keepdims=True)
        diag, below = jnp.broadcast_to(diag, (SUB, NB)), jnp.broadcast_to(below, (SUB, NB))
        ratio = jnp.where(odd, below / pltpu.roll(diag, 1, 0), 0.0)
        rows = right[i] - ratio * pltpu.roll(right[i], 1, 0)
        out.append(rows * lax.rsqrt(diag - ratio * below))
    return out


def invert_kernel(rows, cols, ids_ref, state_hbm, panel_hbm, pack_ref, state_ref, panel_ref, sems):
    get_state = pltpu.make_async_copy(state_hbm, state_ref, sems.at[0])
    get_panel = pltpu.make_async_copy(panel_hbm, panel_ref, sems.at[1])
    get_state.start()
    get_panel.start()
    get_state.wait()
    count = NB // SUB
    sub_id, lane_id = lane_ids()
    held = [
        jnp.where(lane_id == sub_id + SUB * i, 1.0, 0.0) - state_ref[2 * NB + SUB * i : 2 * NB + SUB * i + SUB, :] for i in range(count)
    ]
    for k in range(0, NB, 2):
        b, s = divmod(k, SUB)
        one, two = row(held[b], s), row(held[b], s + 1)
        a11, a12, a21, a22 = lane(one, k), lane(one, k + 1), lane(two, k), lane(two, k + 1)
        scale = 1.0 / (a11 * a22 - a12 * a21)
        i11, i12, i21, i22 = a22 * scale, -a12 * scale, -a21 * scale, a11 * scale
        h1, h2 = lane_id == k, lane_id == k + 1
        o1 = jnp.where(h1, 1.0, jnp.where(h2, 0.0, one))
        o2 = jnp.where(h1, 0.0, jnp.where(h2, 1.0, two))
        n1, n2 = i11 * o1 + i12 * o2, i21 * o1 + i22 * o2
        for i in range(count):
            c1, c2 = lane(held[i], k), lane(held[i], k + 1)
            new = jnp.where(h1 | h2, 0.0, held[i]) - c1 * n1 - c2 * n2
            if i == b:
                new = jnp.where(sub_id == s, n1, jnp.where(sub_id == s + 1, n2, new))
            held[i] = new
    for i in range(count):
        pack_ref[SUB * i : SUB * i + SUB, :] = held[i]
    pack_ref[NB : 3 * NB, :] = state_ref[: 2 * NB, :]
    get_panel.wait()
    inverse, sign = state_ref[:NB, :], state_ref[NB : 2 * NB, :]
    y = mult(panel_ref[...], inverse, 1, 1)
    y_cols = jnp.concatenate([y[rows : rows + NB] - jnp.where(ids_ref[1] == 1, sign, 0.0), y[rows + NB :]], 0)
    pack_ref[3 * NB : 3 * NB + cols, :] = mult(y_cols, pack_ref[:NB, :])
    pack_ref[3 * NB + cols : 4 * NB + cols, :] = y[:NB] - jnp.where(ids_ref[0] == 1, sign, 0.0)
    pack_ref[4 * NB + cols :, :] = y[NB:rows]


def prepare_kernel(fold, slim, ids_ref, a_hbm, send_ref, panel_ref, sems):
    rows, col_count = a_hbm.shape[0], send_ref.shape[0]
    share, step, per = fold * slim, NB // col_count, NB // slim
    parts = sems.shape[0]
    size = rows // parts
    copies = [
        pltpu.make_async_copy(a_hbm.at[pl.ds(at * size, size), 0, :], panel_ref.at[pl.ds(at * size, size), :], sems.at[at])
        for at in range(parts)
    ]
    for copy in copies:
        copy.start()
    gram = jnp.zeros((NB, NB), jnp.float32)
    for at, copy in enumerate(copies):
        copy.wait()
        if at == 0:
            panel_ref[:NB, :] = jnp.where((ids_ref[0] == 0) & (ids_ref[1] == 0), 0.0, panel_ref[:NB, :])
        for m in range(at * size // NB, (at + 1) * size // NB):
            k, f = divmod(m, fold)
            block = panel_ref[m * NB : (m + 1) * NB, :]
            send_ref[k * per : (k + 1) * per, f * slim : (f + 1) * slim, :] = block.reshape(per, slim, NB)
        part = panel_ref[at * size : (at + 1) * size, :]
        gram = gram + mult(part, part, 0, 0)
    lead = jnp.where(ids_ref[0] == 1, panel_ref[:NB, :], 0.0)
    for c in range(col_count):
        send_ref[c, share : share + step, :] = gram[c * step : (c + 1) * step]
        send_ref[c, share + step : share + 2 * step, :] = lead[c * step : (c + 1) * step]


def relay_kernel(fold, slim, ids_ref, got_ref, send_ref):
    row_count = got_ref.shape[0]
    share = fold * slim
    mine = got_ref[ids_ref[0], :share, :]
    piece = jnp.sum(got_ref[:, share:, :], 0)
    send_ref[:, :share, :] = jnp.broadcast_to(mine[None], (fold * row_count,) + mine.shape)
    send_ref[:, share + slim :, :] = jnp.broadcast_to(piece[None], (fold * row_count,) + piece.shape)
    for f in range(fold):
        send_ref[f * row_count : (f + 1) * row_count, share : share + slim, :] = got_ref[:, f * slim : (f + 1) * slim, :]


def thirds(value):
    one = value.astype(jnp.bfloat16)
    rest = value - one.astype(jnp.float32)
    two = rest.astype(jnp.bfloat16)
    return one, two, (rest - two.astype(jnp.float32)).astype(jnp.bfloat16)


def mult_packed(left, right):
    one, two, three = thirds(left)
    first, second, third = thirds(right)
    pair = jnp.concatenate([first, second], 1)
    width = right.shape[1]

    def dot(x, y):
        return lax.dot_general(x, y, (((1,), (0,)), ((), ())), preferred_element_type=jnp.float32)

    high, low = dot(one, pair), dot(two, pair)
    tail = dot(one, third) + dot(three, first)
    return ((low[:, width:] + tail) + (high[:, width:] + low[:, :width])) + high[:, :width]


def product_kernel(col_blocks, fold, slim, ids_ref, got_ref, a_ref, send_hbm, send_ref, hold_ref, sems):
    col_count = got_ref.shape[0]
    rows, cols = a_ref.shape[0] // col_blocks, col_blocks * NB
    share, step, per = fold * slim, NB // col_count, NB // slim
    block = jnp.concatenate([a_ref[pl.ds(k, rows, col_blocks), :] for k in range(col_blocks)], 1)
    part = mult_packed(block, got_ref[:, share : share + slim, :].reshape(cols, NB))
    panel = []
    for m in range(rows // NB):
        k, f = divmod(m, fold)
        send_ref[k * per : (k + 1) * per, f * slim : (f + 1) * slim, :] = part[m * NB : (m + 1) * NB].reshape(per, slim, NB)
        panel.append(got_ref[k * per : (k + 1) * per, f * slim : (f + 1) * slim, :].reshape(NB, NB))
    put_share = pltpu.make_async_copy(send_ref.at[:, :share, :], send_hbm.at[:, :share, :], sems.at[0])
    put_share.start()
    hold_ref[...] = mult_packed(jnp.concatenate(panel, 0).T, part)
    lead = jnp.where(ids_ref[0] == 1, part[:NB], 0.0)
    for c in range(col_count):
        send_ref[c, share : share + step, :] = hold_ref[c * step : (c + 1) * step, :]
        send_ref[c, share + step : share + 2 * step, :] = lead[c * step : (c + 1) * step]
    put_piece = pltpu.make_async_copy(send_ref.at[:, share:, :], send_hbm.at[:, share:, :], sems.at[1])
    put_piece.start()
    put_share.wait()
    put_piece.wait()


def factor_kernel(rows, fold, slim, step, got_ref, state_hbm, panel_hbm, state_ref, panel_ref, hold_ref, lead_ref, sems):
    share, per = (fold + 1) * slim, NB // slim
    for m in range(rows // NB):
        k, f = divmod(m, fold)
        panel_ref[m * NB : (m + 1) * NB, :] = got_ref[k * per : (k + 1) * per, f * slim : (f + 1) * slim, :].reshape(NB, NB)
    panel_ref[rows:, :] = got_ref[:, fold * slim : share, :].reshape(panel_ref.shape[0] - rows, NB)
    put_panel = pltpu.make_async_copy(panel_ref, panel_hbm, sems.at[1])
    put_panel.start()
    count = NB // SUB
    sub_id, lane_id = lane_ids()
    for c in range(got_ref.shape[0]):
        hold_ref[c * step : (c + 1) * step, :] = got_ref[c, share : share + step, :]
        lead_ref[c * step : (c + 1) * step, :] = got_ref[c, share + step : share + 2 * step, :]
    out = inverse_factor([hold_ref[SUB * i : SUB * i + SUB, :] for i in range(count)])
    for i in range(count):
        state_ref[SUB * i : SUB * i + SUB, :] = out[i]
    inverse = state_ref[:NB, :]
    lead = lead_ref[...]
    signs = jnp.where(jnp.sum(lead * inverse, axis=1, keepdims=True) >= 0, -1.0, 1.0)
    state_ref[2 * NB :, :] = signs * mult(lead, inverse, 1, 1)
    for i in range(count):
        here = jnp.where(lane_id == sub_id + SUB * i, 1.0, 0.0)
        state_ref[NB + SUB * i : NB + SUB * i + SUB, :] = here * signs[SUB * i : SUB * i + SUB]
    put_state = pltpu.make_async_copy(state_ref, state_hbm, sems.at[0])
    put_state.start()
    put_state.wait()
    put_panel.wait()


def spread_kernel(share, step, ids_ref, got_hbm, own_ref, state_hbm, send_hbm, got_ref, state_ref, out_ref, sems):
    get_got = pltpu.make_async_copy(got_hbm, got_ref, sems.at[0])
    get_state = pltpu.make_async_copy(state_hbm.at[: 2 * NB, :], state_ref, sems.at[1])
    get_got.start()
    get_state.start()
    get_got.wait()
    total = jnp.sum(got_ref[...], 0)
    get_state.wait()
    own = own_ref[...]
    line = jnp.sum(state_ref[NB:, :], axis=0, keepdims=True)
    turned = mult(total, state_ref[:NB, :], 1, 1)
    rows = turned[:share] - own[:share] * line
    lead = jnp.where(ids_ref[0] == 1, turned[share + step :] - 0.5 * own[share + step :] * line, 0.0)
    out_ref[...] = jnp.concatenate([rows, total[share : share + step], lead], 0)
    copies = [pltpu.make_async_copy(out_ref, send_hbm.at[at], sems.at[2 + at]) for at in range(send_hbm.shape[0])]
    for copy in copies:
        copy.start()
    for copy in copies:
        copy.wait()


def halves(value):
    high = value.astype(jnp.bfloat16)
    return high, (value - high.astype(jnp.float32)).astype(jnp.bfloat16)


def mult_half(left, right, right_dim=1):
    return lax.dot_general(left, right, (((1,), (right_dim,)), ((), ())), preferred_element_type=jnp.float32)


def mult_halves(left, right, right_dim):
    high, low = halves(left)
    right_high, right_low = halves(right)
    small = mult_half(low, right_high, right_dim) + mult_half(high, right_low, right_dim)
    return small + mult_half(high, right_high, right_dim)


def update_kernel(
    col_blocks, fold, slim, got_ref, pack_ref, a_ref, out_ref, high_ref, low_ref, hold_ref, lead_ref, new_ref, sems
):
    col_count = got_ref.shape[0]
    share, step, per = fold * slim, NB // col_count, NB // slim
    cols = col_blocks * NB
    for c in range(col_count):
        hold_ref[c * step : (c + 1) * step, :] = got_ref[c, share + slim : share + slim + step, :]
        lead_ref[c * step : (c + 1) * step, :] = got_ref[c, share + slim + step : share + slim + 2 * step, :]
    coupling, inverse, v = pack_ref[:NB, :], pack_ref[NB : 2 * NB, :], pack_ref[3 * NB : 3 * NB + cols, :]
    y_ref = pack_ref.at[3 * NB + cols :, :]
    cross = jnp.sum(pack_ref[2 * NB : 3 * NB, :], axis=1, keepdims=True) * lead_ref[...]
    middle = mult(mult(inverse, hold_ref[...]), inverse, 1, 1) - cross - cross.T
    z_cols = got_ref[:, share : share + slim, :].reshape(cols, NB)
    u = mult_halves(z_cols - mult_halves(v, middle, 0), coupling, 1)
    for at, part in enumerate((u, v)):
        high, low = halves(part)
        high_ref[:, at * NB : (at + 1) * NB] = high
        low_ref[:, at * NB : (at + 1) * NB] = low
    right_high, right_low = high_ref[...], low_ref[...]
    copies = []
    for k in range(a_ref.shape[0] // (fold * cols)):
        z = [got_ref[k * per : (k + 1) * per, f * slim : (f + 1) * slim, :].reshape(NB, NB) for f in range(fold)]
        y = y_ref[k * fold * NB : (k + 1) * fold * NB, :]
        high, low = halves(jnp.concatenate([y, jnp.concatenate(z, 0)], 1))
        change = mult_half(low, right_high) + mult_half(high, right_low) + mult_half(high, right_high)
        for n in range(col_blocks):
            here = pl.ds(k * fold * cols + n, fold * NB, col_blocks)
            new_ref[here, :] = a_ref[here, :] - change[:, n * NB : (n + 1) * NB]
        there = pl.ds(k * fold * cols, fold * cols)
        copy = pltpu.make_async_copy(new_ref.at[there, :], out_ref.at[there, :], sems.at[k])
        copy.start()
        copies.append(copy)
    for copy in copies:
        copy.wait()


def exchange(pieces, axis):
    return lax.all_to_all(pieces, axis, 0, 0)


def body(kernel):
    row_blocks, _, _, col_blocks, _, _ = kernel.shape
    rows, cols = row_blocks * NB, col_blocks * NB
    row_count, col_count = lax.axis_size("row"), lax.axis_size("col")
    fold = col_count // row_count
    row_index, col_index = lax.axis_index("row"), lax.axis_index("col")
    ids = jnp.stack([row_index, col_index]).astype(jnp.int32)
    lines = kernel.reshape(rows * col_blocks, NB)
    slim, step = cols // col_count, NB // col_count
    share = fold * slim
    pad = 2 * step

    def hbm(*dims):
        return pltpu.HBM(dims, jnp.float32)

    def relay(got):
        return pl.pallas_call(
            lambda *refs: relay_kernel(fold, slim, *refs),
            out_shape=shape(col_count, share + slim + pad, NB),
            in_specs=[SMEM, VMEM],
            out_specs=VMEM,
            compiler_params=PARAMS,
            name="relay",
            cost_estimate=cost(1_000_000, 1_000_000),
        )(ids, got)

    send = pl.pallas_call(
        lambda *refs: prepare_kernel(fold, slim, *refs),
        out_shape=shape(col_count, share + pad, NB),
        in_specs=[SMEM, HBM],
        out_specs=VMEM,
        scratch_shapes=[pltpu.VMEM((rows, NB), jnp.float32), pltpu.SemaphoreType.DMA((min(4, row_blocks),))],
        compiler_params=PARAMS,
        name="prepare",
        cost_estimate=cost(2 * rows * NB * NB * 6, 3_000_000),
    )(ids, pltpu.with_memory_space_constraint(kernel.reshape(rows, col_blocks, NB), pltpu.HBM))
    got = exchange(send, "col")
    own = got[1]
    got = jnp.broadcast_to(got[0][None], (row_count,) + got.shape[1:])
    got = exchange(relay(exchange(got, "row")), "col")

    send = pl.pallas_call(
        lambda *refs: product_kernel(col_blocks, fold, slim, *refs),
        out_shape=hbm(col_count, share + pad, NB),
        in_specs=[SMEM, VMEM, VMEM],
        out_specs=HBM,
        scratch_shapes=[
            pltpu.VMEM((col_count, share + pad, NB), jnp.float32),
            pltpu.VMEM((NB, NB), jnp.float32),
            pltpu.SemaphoreType.DMA((2,)),
        ],
        compiler_params=PARAMS,
        name="product",
        cost_estimate=cost(2 * rows * cols * NB * 6, 4_000_000),
    )(ids, got, lines)
    summed = exchange(send, "col")
    state, panel = pl.pallas_call(
        lambda *refs: factor_kernel(rows, fold, slim, step, *refs),
        out_shape=(hbm(3 * NB, NB), hbm(rows + cols, NB)),
        in_specs=[VMEM],
        out_specs=(HBM, HBM),
        scratch_shapes=[pltpu.VMEM((3 * NB, NB), jnp.float32), pltpu.VMEM((rows + cols, NB), jnp.float32)]
        + [pltpu.VMEM((NB, NB), jnp.float32)] * 2
        + [pltpu.SemaphoreType.DMA((2,))],
        compiler_params=PARAMS,
        name="factor",
        cost_estimate=cost(4_000_000_000, 2_000_000),
    )(got)
    state = pltpu.with_memory_space_constraint(state, pltpu.HBM)
    panel = pltpu.with_memory_space_constraint(panel, pltpu.HBM)

    send = pl.pallas_call(
        lambda *refs: spread_kernel(share, step, *refs),
        out_shape=hbm(row_count, share + pad, NB),
        in_specs=[SMEM, HBM, VMEM, HBM],
        out_specs=HBM,
        scratch_shapes=[
            pltpu.VMEM((col_count, share + pad, NB), jnp.float32),
            pltpu.VMEM((2 * NB, NB), jnp.float32),
            pltpu.VMEM((share + pad, NB), jnp.float32),
            pltpu.SemaphoreType.DMA((2 + row_count,)),
        ],
        compiler_params=PARAMS,
        name="spread",
        cost_estimate=cost(10_000_000, 1_000_000),
    )(ids, summed, own, state)
    got = exchange(send, "row")
    pack = pl.pallas_call(
        lambda *refs: invert_kernel(rows, cols, *refs),
        out_shape=shape(3 * NB + cols + rows, NB),
        in_specs=[SMEM, HBM, HBM],
        out_specs=VMEM,
        scratch_shapes=[
            pltpu.VMEM((3 * NB, NB), jnp.float32),
            pltpu.VMEM((rows + cols, NB), jnp.float32),
            pltpu.SemaphoreType.DMA((2,)),
        ],
        compiler_params=PARAMS,
        name="invert",
        cost_estimate=cost(4_000_000_000, 1_000_000),
    )(ids, state, panel)
    got, pack = lax.optimization_barrier((got, pack))
    last = exchange(relay(got), "col")

    updated = pl.pallas_call(
        lambda *refs: update_kernel(col_blocks, fold, slim, *refs),
        out_shape=shape(rows * col_blocks, NB),
        in_specs=[VMEM] * 3,
        out_specs=pl.BlockSpec(memory_space=pl.ANY),
        scratch_shapes=[
            pltpu.VMEM((cols, 2 * NB), jnp.bfloat16),
            pltpu.VMEM((cols, 2 * NB), jnp.bfloat16),
            pltpu.VMEM((NB, NB), jnp.float32),
            pltpu.VMEM((NB, NB), jnp.float32),
            pltpu.VMEM((rows * col_blocks, NB), jnp.float32),
            pltpu.SemaphoreType.DMA((row_blocks // fold,)),
        ],
        compiler_params=PARAMS,
        name="update",
        cost_estimate=cost(4 * rows * cols * NB * 6, 6_000_000),
    )(last, pack, lines)
    return updated.reshape(kernel.shape)


def solution(mesh):
    return jax.shard_map(
        body,
        mesh=mesh,
        in_specs=(P(None, "row", None, None, "col", None),),
        out_specs=P(None, "row", None, None, "col", None),
        check_vma=False,
    )
```

```python
import jax
import jax.numpy as jnp
from jax import lax
from jax.experimental import pallas as pl
from jax.experimental.pallas import tpu as pltpu
from jax.sharding import PartitionSpec as P

NB = 128
SUB = 8
VMEM = pl.BlockSpec(memory_space=pltpu.VMEM)
SMEM = pl.BlockSpec(memory_space=pltpu.SMEM)
HBM = pl.BlockSpec(memory_space=pltpu.HBM)
PARAMS = pltpu.CompilerParams(vmem_limit_bytes=40 * 1024 * 1024)


def mult(left, right, left_dim=1, right_dim=0):
    return lax.dot_general(
        left,
        right,
        (((left_dim,), (right_dim,)), ((), ())),
        precision=lax.Precision.HIGHEST,
        preferred_element_type=jnp.float32,
    )


def shape(*dims):
    return jax.ShapeDtypeStruct(dims, jnp.float32)


def cost(flops, nbytes):
    return pl.CostEstimate(flops=flops, bytes_accessed=nbytes, transcendentals=0)


def lane(block, k):
    return jnp.broadcast_to(block[:, k : k + 1], (SUB, NB))


def row(block, s):
    return jnp.broadcast_to(block[s : s + 1, :], (SUB, NB))


def lane_ids():
    sub_id = lax.broadcasted_iota(jnp.int32, (SUB, NB), 0)
    lane_id = lax.broadcasted_iota(jnp.int32, (SUB, NB), 1)
    return sub_id, lane_id


def inverse_factor(left):
    count = NB // SUB
    sub_id, lane_id = lane_ids()
    eye = [jnp.where(lane_id == sub_id + SUB * i, 1.0, 0.0) for i in range(count)]
    right = list(eye)
    for k in range(0, NB, 4):
        b, s = divmod(k, SUB)
        r = [row(left[b], s + j) for j in range(4)]
        e = [row(right[b], s + j) for j in range(4)]
        a = [[lane(r[i], k + j) if j >= i else None for j in range(4)] for i in range(4)]
        scale = 1.0 / (a[0][0] * a[1][1] - a[0][1] * a[0][1])
        i00, i01, i11 = a[1][1] * scale, -a[0][1] * scale, a[0][0] * scale
        t = [(i00 * a[0][j] + i01 * a[1][j], i01 * a[0][j] + i11 * a[1][j]) for j in (2, 3)]
        s22 = a[2][2] - t[0][0] * a[0][2] - t[0][1] * a[1][2]
        s23 = a[2][3] - t[0][0] * a[0][3] - t[0][1] * a[1][3]
        s33 = a[3][3] - t[1][0] * a[0][3] - t[1][1] * a[1][3]
        scale = 1.0 / (s22 * s33 - s23 * s23)
        j22, j23, j33 = s33 * scale, -s23 * scale, s22 * scale

        def rank(x):
            x2 = x[2] - t[0][0] * x[0] - t[0][1] * x[1]
            x3 = x[3] - t[1][0] * x[0] - t[1][1] * x[1]
            q2, q3 = j22 * x2 + j23 * x3, j23 * x2 + j33 * x3
            u0 = i00 * x[0] + i01 * x[1] - t[0][0] * q2 - t[1][0] * q3
            u1 = i01 * x[0] + i11 * x[1] - t[0][1] * q2 - t[1][1] * q3
            return x2, x3, (u0, u1, q2, q3)

        l2, l3, lu = rank(r)
        e2, e3, eu = rank(e)
        for i in range(b, count):
            c = [lane(left[i], k + j) for j in range(4)]
            if i == b:
                c = [jnp.where(sub_id > s + 3, x, 0.0) for x in c]
            left[i] = left[i] - (c[0] * lu[0] + c[1] * lu[1]) - (c[2] * lu[2] + c[3] * lu[3])
            right[i] = right[i] - (c[0] * eu[0] + c[1] * eu[1]) - (c[2] * eu[2] + c[3] * eu[3])
        left[b] = jnp.where(sub_id == s + 2, l2, jnp.where(sub_id == s + 3, l3, left[b]))
        right[b] = jnp.where(sub_id == s + 2, e2, jnp.where(sub_id == s + 3, e3, right[b]))
    odd = (sub_id % 2) == 1
    out = []
    for i in range(count):
        diag = jnp.sum(left[i] * eye[i], axis=1, keepdims=True)
        below = jnp.sum(jnp.where(lane_id == sub_id + (SUB * i - 1), left[i], 0.0), axis=1, keepdims=True)
        diag, below = jnp.broadcast_to(diag, (SUB, NB)), jnp.broadcast_to(below, (SUB, NB))
        ratio = jnp.where(odd, below / pltpu.roll(diag, 1, 0), 0.0)
        rows = right[i] - ratio * pltpu.roll(right[i], 1, 0)
        out.append(rows * lax.rsqrt(diag - ratio * below))
    return out


def invert_kernel(rows, cols, ids_ref, state_hbm, panel_hbm, pack_ref, state_ref, panel_ref, sems):
    get_state = pltpu.make_async_copy(state_hbm, state_ref, sems.at[0])
    get_panel = pltpu.make_async_copy(panel_hbm, panel_ref, sems.at[1])
    get_state.start()
    get_panel.start()
    get_state.wait()
    count = NB // SUB
    sub_id, lane_id = lane_ids()
    held = [
        jnp.where(lane_id == sub_id + SUB * i, 1.0, 0.0) - state_ref[2 * NB + SUB * i : 2 * NB + SUB * i + SUB, :] for i in range(count)
    ]
    for k in range(0, NB, 2):
        b, s = divmod(k, SUB)
        one, two = row(held[b], s), row(held[b], s + 1)
        a11, a12, a21, a22 = lane(one, k), lane(one, k + 1), lane(two, k), lane(two, k + 1)
        scale = 1.0 / (a11 * a22 - a12 * a21)
        i11, i12, i21, i22 = a22 * scale, -a12 * scale, -a21 * scale, a11 * scale
        h1, h2 = lane_id == k, lane_id == k + 1
        o1 = jnp.where(h1, 1.0, jnp.where(h2, 0.0, one))
        o2 = jnp.where(h1, 0.0, jnp.where(h2, 1.0, two))
        n1, n2 = i11 * o1 + i12 * o2, i21 * o1 + i22 * o2
        for i in range(count):
            c1, c2 = lane(held[i], k), lane(held[i], k + 1)
            new = jnp.where(h1 | h2, 0.0, held[i]) - c1 * n1 - c2 * n2
            if i == b:
                new = jnp.where(sub_id == s, n1, jnp.where(sub_id == s + 1, n2, new))
            held[i] = new
    for i in range(count):
        pack_ref[SUB * i : SUB * i + SUB, :] = held[i]
    pack_ref[NB : 3 * NB, :] = state_ref[: 2 * NB, :]
    get_panel.wait()
    inverse, sign = state_ref[:NB, :], state_ref[NB : 2 * NB, :]
    y = mult(panel_ref[...], inverse, 1, 1)
    y_cols = jnp.concatenate([y[rows : rows + NB] - jnp.where(ids_ref[1] == 1, sign, 0.0), y[rows + NB :]], 0)
    pack_ref[3 * NB : 3 * NB + cols, :] = mult(y_cols, pack_ref[:NB, :])
    pack_ref[3 * NB + cols : 4 * NB + cols, :] = y[:NB] - jnp.where(ids_ref[0] == 1, sign, 0.0)
    pack_ref[4 * NB + cols :, :] = y[NB:rows]


def prepare_kernel(fold, slim, ids_ref, a_hbm, send_ref, panel_ref, sem):
    rows, col_count = a_hbm.shape[0], send_ref.shape[0]
    share, step, per = fold * slim, NB // col_count, NB // slim
    get_panel = pltpu.make_async_copy(a_hbm.at[:, 0, :], panel_ref, sem)
    get_panel.start()
    get_panel.wait()
    panel = panel_ref[...]
    first = jnp.where((ids_ref[0] == 0) & (ids_ref[1] == 0), 0.0, panel[:NB])
    panel = jnp.concatenate([first, panel[NB:]], 0)
    gram = mult_packed(panel.T, panel)
    lead = jnp.where(ids_ref[0] == 1, first, 0.0)
    for m in range(rows // NB):
        k, f = divmod(m, fold)
        send_ref[k * per : (k + 1) * per, f * slim : (f + 1) * slim, :] = panel[m * NB : (m + 1) * NB].reshape(per, slim, NB)
    for c in range(col_count):
        send_ref[c, share : share + step, :] = gram[c * step : (c + 1) * step]
        send_ref[c, share + step : share + 2 * step, :] = lead[c * step : (c + 1) * step]


def relay_kernel(fold, slim, ids_ref, got_ref, send_ref):
    row_count = got_ref.shape[0]
    share = fold * slim
    mine = got_ref[ids_ref[0], :share, :]
    piece = jnp.sum(got_ref[:, share:, :], 0)
    send_ref[:, :share, :] = jnp.broadcast_to(mine[None], (fold * row_count,) + mine.shape)
    send_ref[:, share + slim :, :] = jnp.broadcast_to(piece[None], (fold * row_count,) + piece.shape)
    for f in range(fold):
        send_ref[f * row_count : (f + 1) * row_count, share : share + slim, :] = got_ref[:, f * slim : (f + 1) * slim, :]


def thirds(value):
    one = value.astype(jnp.bfloat16)
    rest = value - one.astype(jnp.float32)
    two = rest.astype(jnp.bfloat16)
    return one, two, (rest - two.astype(jnp.float32)).astype(jnp.bfloat16)


def mult_packed(left, right):
    one, two, three = thirds(left)
    first, second, third = thirds(right)
    pair = jnp.concatenate([first, second], 1)
    width = right.shape[1]

    def dot(x, y):
        return lax.dot_general(x, y, (((1,), (0,)), ((), ())), preferred_element_type=jnp.float32)

    high, low = dot(one, pair), dot(two, pair)
    tail = dot(one, third) + dot(three, first)
    return ((low[:, width:] + tail) + (high[:, width:] + low[:, :width])) + high[:, :width]


def product_kernel(col_blocks, fold, slim, ids_ref, got_ref, a_ref, send_hbm, send_ref, hold_ref, sems):
    col_count = got_ref.shape[0]
    rows, cols = a_ref.shape[0] // col_blocks, col_blocks * NB
    share, step, per = fold * slim, NB // col_count, NB // slim
    block = jnp.concatenate([a_ref[pl.ds(k, rows, col_blocks), :] for k in range(col_blocks)], 1)
    part = mult_packed(block, got_ref[:, share : share + slim, :].reshape(cols, NB))
    panel = []
    for m in range(rows // NB):
        k, f = divmod(m, fold)
        send_ref[k * per : (k + 1) * per, f * slim : (f + 1) * slim, :] = part[m * NB : (m + 1) * NB].reshape(per, slim, NB)
        panel.append(got_ref[k * per : (k + 1) * per, f * slim : (f + 1) * slim, :].reshape(NB, NB))
    put_share = pltpu.make_async_copy(send_ref.at[:, :share, :], send_hbm.at[:, :share, :], sems.at[0])
    put_share.start()
    hold_ref[...] = mult_packed(jnp.concatenate(panel, 0).T, part)
    lead = jnp.where(ids_ref[0] == 1, part[:NB], 0.0)
    for c in range(col_count):
        send_ref[c, share : share + step, :] = hold_ref[c * step : (c + 1) * step, :]
        send_ref[c, share + step : share + 2 * step, :] = lead[c * step : (c + 1) * step]
    put_piece = pltpu.make_async_copy(send_ref.at[:, share:, :], send_hbm.at[:, share:, :], sems.at[1])
    put_piece.start()
    put_share.wait()
    put_piece.wait()


def factor_kernel(rows, fold, slim, step, got_ref, state_hbm, panel_hbm, state_ref, panel_ref, hold_ref, lead_ref, sems):
    share, per = (fold + 1) * slim, NB // slim
    for m in range(rows // NB):
        k, f = divmod(m, fold)
        panel_ref[m * NB : (m + 1) * NB, :] = got_ref[k * per : (k + 1) * per, f * slim : (f + 1) * slim, :].reshape(NB, NB)
    panel_ref[rows:, :] = got_ref[:, fold * slim : share, :].reshape(panel_ref.shape[0] - rows, NB)
    put_panel = pltpu.make_async_copy(panel_ref, panel_hbm, sems.at[1])
    put_panel.start()
    count = NB // SUB
    sub_id, lane_id = lane_ids()
    for c in range(got_ref.shape[0]):
        hold_ref[c * step : (c + 1) * step, :] = got_ref[c, share : share + step, :]
        lead_ref[c * step : (c + 1) * step, :] = got_ref[c, share + step : share + 2 * step, :]
    out = inverse_factor([hold_ref[SUB * i : SUB * i + SUB, :] for i in range(count)])
    for i in range(count):
        state_ref[SUB * i : SUB * i + SUB, :] = out[i]
    inverse = state_ref[:NB, :]
    lead = lead_ref[...]
    signs = jnp.where(jnp.sum(lead * inverse, axis=1, keepdims=True) >= 0, -1.0, 1.0)
    state_ref[2 * NB :, :] = signs * mult(lead, inverse, 1, 1)
    for i in range(count):
        here = jnp.where(lane_id == sub_id + SUB * i, 1.0, 0.0)
        state_ref[NB + SUB * i : NB + SUB * i + SUB, :] = here * signs[SUB * i : SUB * i + SUB]
    put_state = pltpu.make_async_copy(state_ref, state_hbm, sems.at[0])
    put_state.start()
    put_state.wait()
    put_panel.wait()


def spread_kernel(share, step, ids_ref, got_hbm, own_ref, state_hbm, send_ref, got_ref, state_ref, sems):
    get_got = pltpu.make_async_copy(got_hbm, got_ref, sems.at[0])
    get_state = pltpu.make_async_copy(state_hbm.at[: 2 * NB, :], state_ref, sems.at[1])
    get_got.start()
    get_state.start()
    get_got.wait()
    total = jnp.sum(got_ref[...], 0)
    get_state.wait()
    own = own_ref[...]
    line = jnp.sum(state_ref[NB:, :], axis=0, keepdims=True)
    turned = mult(total, state_ref[:NB, :], 1, 1)
    rows = turned[:share] - own[:share] * line
    lead = jnp.where(ids_ref[0] == 1, turned[share + step :] - 0.5 * own[share + step :] * line, 0.0)
    out = jnp.concatenate([rows, total[share : share + step], lead], 0)
    send_ref[...] = jnp.broadcast_to(out[None], send_ref.shape)


def halves(value):
    high = value.astype(jnp.bfloat16)
    return high, (value - high.astype(jnp.float32)).astype(jnp.bfloat16)


def mult_half(left, right, right_dim=1):
    return lax.dot_general(left, right, (((1,), (right_dim,)), ((), ())), preferred_element_type=jnp.float32)


def mult_halves(left, right, right_dim):
    high, low = halves(left)
    right_high, right_low = halves(right)
    small = mult_half(low, right_high, right_dim) + mult_half(high, right_low, right_dim)
    return small + mult_half(high, right_high, right_dim)


def update_kernel(
    col_blocks, fold, slim, got_ref, pack_ref, a_ref, out_ref, high_ref, low_ref, hold_ref, lead_ref, new_ref, sems
):
    col_count = got_ref.shape[0]
    share, step, per = fold * slim, NB // col_count, NB // slim
    cols = col_blocks * NB
    for c in range(col_count):
        hold_ref[c * step : (c + 1) * step, :] = got_ref[c, share + slim : share + slim + step, :]
        lead_ref[c * step : (c + 1) * step, :] = got_ref[c, share + slim + step : share + slim + 2 * step, :]
    coupling, inverse, v = pack_ref[:NB, :], pack_ref[NB : 2 * NB, :], pack_ref[3 * NB : 3 * NB + cols, :]
    y_ref = pack_ref.at[3 * NB + cols :, :]
    cross = jnp.sum(pack_ref[2 * NB : 3 * NB, :], axis=1, keepdims=True) * lead_ref[...]
    middle = mult(mult(inverse, hold_ref[...]), inverse, 1, 1) - cross - cross.T
    z_cols = got_ref[:, share : share + slim, :].reshape(cols, NB)
    u = mult_halves(z_cols - mult_halves(v, middle, 0), coupling, 1)
    for at, part in enumerate((u, v)):
        high, low = halves(part)
        high_ref[:, at * NB : (at + 1) * NB] = high
        low_ref[:, at * NB : (at + 1) * NB] = low
    right_high, right_low = high_ref[...], low_ref[...]
    copies = []
    for k in range(a_ref.shape[0] // (fold * cols)):
        z = [got_ref[k * per : (k + 1) * per, f * slim : (f + 1) * slim, :].reshape(NB, NB) for f in range(fold)]
        y = y_ref[k * fold * NB : (k + 1) * fold * NB, :]
        high, low = halves(jnp.concatenate([y, jnp.concatenate(z, 0)], 1))
        change = mult_half(low, right_high) + mult_half(high, right_low) + mult_half(high, right_high)
        for n in range(col_blocks):
            here = pl.ds(k * fold * cols + n, fold * NB, col_blocks)
            new_ref[here, :] = a_ref[here, :] - change[:, n * NB : (n + 1) * NB]
        there = pl.ds(k * fold * cols, fold * cols)
        copy = pltpu.make_async_copy(new_ref.at[there, :], out_ref.at[there, :], sems.at[k])
        copy.start()
        copies.append(copy)
    for copy in copies:
        copy.wait()


def exchange(pieces, axis):
    return lax.all_to_all(pieces, axis, 0, 0)


def body(kernel):
    row_blocks, _, _, col_blocks, _, _ = kernel.shape
    rows, cols = row_blocks * NB, col_blocks * NB
    row_count, col_count = lax.axis_size("row"), lax.axis_size("col")
    fold = col_count // row_count
    row_index, col_index = lax.axis_index("row"), lax.axis_index("col")
    ids = jnp.stack([row_index, col_index]).astype(jnp.int32)
    lines = kernel.reshape(rows * col_blocks, NB)
    slim, step = cols // col_count, NB // col_count
    share = fold * slim
    pad = 2 * step

    def hbm(*dims):
        return pltpu.HBM(dims, jnp.float32)

    def relay(got):
        return pl.pallas_call(
            lambda *refs: relay_kernel(fold, slim, *refs),
            out_shape=shape(col_count, share + slim + pad, NB),
            in_specs=[SMEM, VMEM],
            out_specs=VMEM,
            compiler_params=PARAMS,
            name="relay",
            cost_estimate=cost(1_000_000, 1_000_000),
        )(ids, got)

    send = pl.pallas_call(
        lambda *refs: prepare_kernel(fold, slim, *refs),
        out_shape=shape(col_count, share + pad, NB),
        in_specs=[SMEM, HBM],
        out_specs=VMEM,
        scratch_shapes=[pltpu.VMEM((rows, NB), jnp.float32), pltpu.SemaphoreType.DMA],
        compiler_params=PARAMS,
        name="prepare",
        cost_estimate=cost(2 * rows * NB * NB * 6, 3_000_000),
    )(ids, pltpu.with_memory_space_constraint(kernel.reshape(rows, col_blocks, NB), pltpu.HBM))
    got = exchange(send, "col")
    own = got[1]
    got = jnp.broadcast_to(got[0][None], (row_count,) + got.shape[1:])
    got = exchange(relay(exchange(got, "row")), "col")

    send = pl.pallas_call(
        lambda *refs: product_kernel(col_blocks, fold, slim, *refs),
        out_shape=hbm(col_count, share + pad, NB),
        in_specs=[SMEM, VMEM, VMEM],
        out_specs=HBM,
        scratch_shapes=[
            pltpu.VMEM((col_count, share + pad, NB), jnp.float32),
            pltpu.VMEM((NB, NB), jnp.float32),
            pltpu.SemaphoreType.DMA((2,)),
        ],
        compiler_params=PARAMS,
        name="product",
        cost_estimate=cost(2 * rows * cols * NB * 6, 4_000_000),
    )(ids, got, lines)
    summed = exchange(send, "col")
    state, panel = pl.pallas_call(
        lambda *refs: factor_kernel(rows, fold, slim, step, *refs),
        out_shape=(hbm(3 * NB, NB), hbm(rows + cols, NB)),
        in_specs=[VMEM],
        out_specs=(HBM, HBM),
        scratch_shapes=[pltpu.VMEM((3 * NB, NB), jnp.float32), pltpu.VMEM((rows + cols, NB), jnp.float32)]
        + [pltpu.VMEM((NB, NB), jnp.float32)] * 2
        + [pltpu.SemaphoreType.DMA((2,))],
        compiler_params=PARAMS,
        name="factor",
        cost_estimate=cost(4_000_000_000, 2_000_000),
    )(got)
    state = pltpu.with_memory_space_constraint(state, pltpu.HBM)
    panel = pltpu.with_memory_space_constraint(panel, pltpu.HBM)

    send = pl.pallas_call(
        lambda *refs: spread_kernel(share, step, *refs),
        out_shape=shape(row_count, share + pad, NB),
        in_specs=[SMEM, HBM, VMEM, HBM],
        out_specs=VMEM,
        scratch_shapes=[
            pltpu.VMEM((col_count, share + pad, NB), jnp.float32),
            pltpu.VMEM((2 * NB, NB), jnp.float32),
            pltpu.SemaphoreType.DMA((2,)),
        ],
        compiler_params=PARAMS,
        name="spread",
        cost_estimate=cost(10_000_000, 1_000_000),
    )(ids, summed, own, state)
    got = exchange(send, "row")
    pack = pl.pallas_call(
        lambda *refs: invert_kernel(rows, cols, *refs),
        out_shape=shape(3 * NB + cols + rows, NB),
        in_specs=[SMEM, HBM, HBM],
        out_specs=VMEM,
        scratch_shapes=[
            pltpu.VMEM((3 * NB, NB), jnp.float32),
            pltpu.VMEM((rows + cols, NB), jnp.float32),
            pltpu.SemaphoreType.DMA((2,)),
        ],
        compiler_params=PARAMS,
        name="invert",
        cost_estimate=cost(4_000_000_000, 1_000_000),
    )(ids, state, panel)
    got, pack = lax.optimization_barrier((got, pack))
    last = exchange(relay(got), "col")

    updated = pl.pallas_call(
        lambda *refs: update_kernel(col_blocks, fold, slim, *refs),
        out_shape=shape(rows * col_blocks, NB),
        in_specs=[VMEM] * 3,
        out_specs=pl.BlockSpec(memory_space=pl.ANY),
        scratch_shapes=[
            pltpu.VMEM((cols, 2 * NB), jnp.bfloat16),
            pltpu.VMEM((cols, 2 * NB), jnp.bfloat16),
            pltpu.VMEM((NB, NB), jnp.float32),
            pltpu.VMEM((NB, NB), jnp.float32),
            pltpu.VMEM((rows * col_blocks, NB), jnp.float32),
            pltpu.SemaphoreType.DMA((row_blocks // fold,)),
        ],
        compiler_params=PARAMS,
        name="update",
        cost_estimate=cost(4 * rows * cols * NB * 6, 6_000_000),
    )(last, pack, lines)
    return updated.reshape(kernel.shape)


def solution(mesh):
    return jax.shard_map(
        body,
        mesh=mesh,
        in_specs=(P(None, "row", None, None, "col", None),),
        out_specs=P(None, "row", None, None, "col", None),
        check_vma=False,
    )
```

```python
import jax
import jax.numpy as jnp
from jax import lax
from jax.experimental import pallas as pl
from jax.experimental.pallas import tpu as pltpu
from jax.sharding import PartitionSpec as P

NB = 128
SUB = 8
VMEM = pl.BlockSpec(memory_space=pltpu.VMEM)
SMEM = pl.BlockSpec(memory_space=pltpu.SMEM)
HBM = pl.BlockSpec(memory_space=pltpu.HBM)
PARAMS = pltpu.CompilerParams(vmem_limit_bytes=40 * 1024 * 1024)


def mult(left, right, left_dim=1, right_dim=0):
    return lax.dot_general(
        left,
        right,
        (((left_dim,), (right_dim,)), ((), ())),
        precision=lax.Precision.HIGHEST,
        preferred_element_type=jnp.float32,
    )


def shape(*dims):
    return jax.ShapeDtypeStruct(dims, jnp.float32)


def cost(flops, nbytes):
    return pl.CostEstimate(flops=flops, bytes_accessed=nbytes, transcendentals=0)


def lane(block, k):
    return jnp.broadcast_to(block[:, k : k + 1], (SUB, NB))


def row(block, s):
    return jnp.broadcast_to(block[s : s + 1, :], (SUB, NB))


def lane_ids():
    sub_id = lax.broadcasted_iota(jnp.int32, (SUB, NB), 0)
    lane_id = lax.broadcasted_iota(jnp.int32, (SUB, NB), 1)
    return sub_id, lane_id


def inverse_factor(left):
    count = NB // SUB
    sub_id, lane_id = lane_ids()
    eye = [jnp.where(lane_id == sub_id + SUB * i, 1.0, 0.0) for i in range(count)]
    right = list(eye)
    for k in range(0, NB, 4):
        b, s = divmod(k, SUB)
        r = [row(left[b], s + j) for j in range(4)]
        e = [row(right[b], s + j) for j in range(4)]
        a = [[lane(r[i], k + j) if j >= i else None for j in range(4)] for i in range(4)]
        scale = 1.0 / (a[0][0] * a[1][1] - a[0][1] * a[0][1])
        i00, i01, i11 = a[1][1] * scale, -a[0][1] * scale, a[0][0] * scale
        t = [(i00 * a[0][j] + i01 * a[1][j], i01 * a[0][j] + i11 * a[1][j]) for j in (2, 3)]
        s22 = a[2][2] - t[0][0] * a[0][2] - t[0][1] * a[1][2]
        s23 = a[2][3] - t[0][0] * a[0][3] - t[0][1] * a[1][3]
        s33 = a[3][3] - t[1][0] * a[0][3] - t[1][1] * a[1][3]
        scale = 1.0 / (s22 * s33 - s23 * s23)
        j22, j23, j33 = s33 * scale, -s23 * scale, s22 * scale

        def rank(x):
            x2 = x[2] - t[0][0] * x[0] - t[0][1] * x[1]
            x3 = x[3] - t[1][0] * x[0] - t[1][1] * x[1]
            q2, q3 = j22 * x2 + j23 * x3, j23 * x2 + j33 * x3
            u0 = i00 * x[0] + i01 * x[1] - t[0][0] * q2 - t[1][0] * q3
            u1 = i01 * x[0] + i11 * x[1] - t[0][1] * q2 - t[1][1] * q3
            return x2, x3, (u0, u1, q2, q3)

        l2, l3, lu = rank(r)
        e2, e3, eu = rank(e)
        for i in range(b, count):
            c = [lane(left[i], k + j) for j in range(4)]
            if i == b:
                c = [jnp.where(sub_id > s + 3, x, 0.0) for x in c]
            left[i] = left[i] - (c[0] * lu[0] + c[1] * lu[1]) - (c[2] * lu[2] + c[3] * lu[3])
            right[i] = right[i] - (c[0] * eu[0] + c[1] * eu[1]) - (c[2] * eu[2] + c[3] * eu[3])
        left[b] = jnp.where(sub_id == s + 2, l2, jnp.where(sub_id == s + 3, l3, left[b]))
        right[b] = jnp.where(sub_id == s + 2, e2, jnp.where(sub_id == s + 3, e3, right[b]))
    odd = (sub_id % 2) == 1
    out = []
    for i in range(count):
        diag = jnp.sum(left[i] * eye[i], axis=1, keepdims=True)
        below = jnp.sum(jnp.where(lane_id == sub_id + (SUB * i - 1), left[i], 0.0), axis=1, keepdims=True)
        diag, below = jnp.broadcast_to(diag, (SUB, NB)), jnp.broadcast_to(below, (SUB, NB))
        ratio = jnp.where(odd, below / pltpu.roll(diag, 1, 0), 0.0)
        rows = right[i] - ratio * pltpu.roll(right[i], 1, 0)
        out.append(rows * lax.rsqrt(diag - ratio * below))
    return out


def invert_kernel(rows, cols, ids_ref, state_hbm, panel_hbm, pack_ref, state_ref, panel_ref, sems):
    get_state = pltpu.make_async_copy(state_hbm, state_ref, sems.at[0])
    get_panel = pltpu.make_async_copy(panel_hbm, panel_ref, sems.at[1])
    get_state.start()
    get_panel.start()
    get_state.wait()
    count = NB // SUB
    sub_id, lane_id = lane_ids()
    held = [
        jnp.where(lane_id == sub_id + SUB * i, 1.0, 0.0) - state_ref[2 * NB + SUB * i : 2 * NB + SUB * i + SUB, :] for i in range(count)
    ]
    for k in range(0, NB, 2):
        b, s = divmod(k, SUB)
        one, two = row(held[b], s), row(held[b], s + 1)
        a11, a12, a21, a22 = lane(one, k), lane(one, k + 1), lane(two, k), lane(two, k + 1)
        scale = 1.0 / (a11 * a22 - a12 * a21)
        i11, i12, i21, i22 = a22 * scale, -a12 * scale, -a21 * scale, a11 * scale
        h1, h2 = lane_id == k, lane_id == k + 1
        o1 = jnp.where(h1, 1.0, jnp.where(h2, 0.0, one))
        o2 = jnp.where(h1, 0.0, jnp.where(h2, 1.0, two))
        n1, n2 = i11 * o1 + i12 * o2, i21 * o1 + i22 * o2
        for i in range(count):
            c1, c2 = lane(held[i], k), lane(held[i], k + 1)
            new = jnp.where(h1 | h2, 0.0, held[i]) - c1 * n1 - c2 * n2
            if i == b:
                new = jnp.where(sub_id == s, n1, jnp.where(sub_id == s + 1, n2, new))
            held[i] = new
    for i in range(count):
        pack_ref[SUB * i : SUB * i + SUB, :] = held[i]
    pack_ref[NB : 3 * NB, :] = state_ref[: 2 * NB, :]
    get_panel.wait()
    inverse, sign = state_ref[:NB, :], state_ref[NB : 2 * NB, :]
    y = mult(panel_ref[...], inverse, 1, 1)
    y_cols = jnp.concatenate([y[rows : rows + NB] - jnp.where(ids_ref[1] == 1, sign, 0.0), y[rows + NB :]], 0)
    pack_ref[3 * NB : 3 * NB + cols, :] = mult(y_cols, pack_ref[:NB, :])
    pack_ref[3 * NB + cols : 4 * NB + cols, :] = y[:NB] - jnp.where(ids_ref[0] == 1, sign, 0.0)
    pack_ref[4 * NB + cols :, :] = y[NB:rows]


def prepare_kernel(fold, slim, ids_ref, a_hbm, send_ref, panel_ref, sem):
    rows, col_count = a_hbm.shape[0], send_ref.shape[0]
    share, step, per = fold * slim, NB // col_count, NB // slim
    get_panel = pltpu.make_async_copy(a_hbm.at[:, 0, :], panel_ref, sem)
    get_panel.start()
    get_panel.wait()
    panel = panel_ref[...]
    first = jnp.where((ids_ref[0] == 0) & (ids_ref[1] == 0), 0.0, panel[:NB])
    panel = jnp.concatenate([first, panel[NB:]], 0)
    gram = mult_packed(panel.T, panel)
    lead = jnp.where(ids_ref[0] == 1, first, 0.0)
    for m in range(rows // NB):
        k, f = divmod(m, fold)
        send_ref[k * per : (k + 1) * per, f * slim : (f + 1) * slim, :] = panel[m * NB : (m + 1) * NB].reshape(per, slim, NB)
    for c in range(col_count):
        send_ref[c, share : share + step, :] = gram[c * step : (c + 1) * step]
        send_ref[c, share + step : share + 2 * step, :] = lead[c * step : (c + 1) * step]


def relay_kernel(fold, slim, ids_ref, got_ref, send_ref):
    row_count = got_ref.shape[0]
    share = fold * slim
    mine = got_ref[ids_ref[0], :share, :]
    piece = jnp.sum(got_ref[:, share:, :], 0)
    send_ref[:, :share, :] = jnp.broadcast_to(mine[None], (fold * row_count,) + mine.shape)
    send_ref[:, share + slim :, :] = jnp.broadcast_to(piece[None], (fold * row_count,) + piece.shape)
    for f in range(fold):
        send_ref[f * row_count : (f + 1) * row_count, share : share + slim, :] = got_ref[:, f * slim : (f + 1) * slim, :]


def thirds(value):
    one = value.astype(jnp.bfloat16)
    rest = value - one.astype(jnp.float32)
    two = rest.astype(jnp.bfloat16)
    return one, two, (rest - two.astype(jnp.float32)).astype(jnp.bfloat16)


def mult_packed(left, right):
    one, two, three = thirds(left)
    first, second, third = thirds(right)
    pair = jnp.concatenate([first, second], 1)
    width = right.shape[1]

    def dot(x, y):
        return lax.dot_general(x, y, (((1,), (0,)), ((), ())), preferred_element_type=jnp.float32)

    high, low = dot(one, pair), dot(two, pair)
    tail = dot(one, third) + dot(three, first)
    return ((low[:, width:] + tail) + (high[:, width:] + low[:, :width])) + high[:, :width]


def product_kernel(col_blocks, fold, slim, ids_ref, got_ref, a_ref, send_hbm, send_ref, hold_ref, sems):
    col_count = got_ref.shape[0]
    rows, cols = a_ref.shape[0] // col_blocks, col_blocks * NB
    share, step, per = fold * slim, NB // col_count, NB // slim
    block = jnp.concatenate([a_ref[pl.ds(k, rows, col_blocks), :] for k in range(col_blocks)], 1)
    part = mult_packed(block, got_ref[:, share : share + slim, :].reshape(cols, NB))
    panel = []
    for m in range(rows // NB):
        k, f = divmod(m, fold)
        send_ref[k * per : (k + 1) * per, f * slim : (f + 1) * slim, :] = part[m * NB : (m + 1) * NB].reshape(per, slim, NB)
        panel.append(got_ref[k * per : (k + 1) * per, f * slim : (f + 1) * slim, :].reshape(NB, NB))
    put_share = pltpu.make_async_copy(send_ref.at[:, :share, :], send_hbm.at[:, :share, :], sems.at[0])
    put_share.start()
    hold_ref[...] = mult_packed(jnp.concatenate(panel, 0).T, part)
    lead = jnp.where(ids_ref[0] == 1, part[:NB], 0.0)
    for c in range(col_count):
        send_ref[c, share : share + step, :] = hold_ref[c * step : (c + 1) * step, :]
        send_ref[c, share + step : share + 2 * step, :] = lead[c * step : (c + 1) * step]
    put_piece = pltpu.make_async_copy(send_ref.at[:, share:, :], send_hbm.at[:, share:, :], sems.at[1])
    put_piece.start()
    put_share.wait()
    put_piece.wait()


def factor_kernel(rows, fold, slim, step, got_ref, state_hbm, panel_hbm, state_ref, panel_ref, hold_ref, lead_ref, sems):
    share, per = (fold + 1) * slim, NB // slim
    for m in range(rows // NB):
        k, f = divmod(m, fold)
        panel_ref[m * NB : (m + 1) * NB, :] = got_ref[k * per : (k + 1) * per, f * slim : (f + 1) * slim, :].reshape(NB, NB)
    panel_ref[rows:, :] = got_ref[:, fold * slim : share, :].reshape(panel_ref.shape[0] - rows, NB)
    put_panel = pltpu.make_async_copy(panel_ref, panel_hbm, sems.at[1])
    put_panel.start()
    count = NB // SUB
    sub_id, lane_id = lane_ids()
    for c in range(got_ref.shape[0]):
        hold_ref[c * step : (c + 1) * step, :] = got_ref[c, share : share + step, :]
        lead_ref[c * step : (c + 1) * step, :] = got_ref[c, share + step : share + 2 * step, :]
    out = inverse_factor([hold_ref[SUB * i : SUB * i + SUB, :] for i in range(count)])
    for i in range(count):
        state_ref[SUB * i : SUB * i + SUB, :] = out[i]
    inverse = state_ref[:NB, :]
    lead = lead_ref[...]
    signs = jnp.where(jnp.sum(lead * inverse, axis=1, keepdims=True) >= 0, -1.0, 1.0)
    state_ref[2 * NB :, :] = signs * mult(lead, inverse, 1, 1)
    for i in range(count):
        here = jnp.where(lane_id == sub_id + SUB * i, 1.0, 0.0)
        state_ref[NB + SUB * i : NB + SUB * i + SUB, :] = here * signs[SUB * i : SUB * i + SUB]
    put_state = pltpu.make_async_copy(state_ref, state_hbm, sems.at[0])
    put_state.start()
    put_state.wait()
    put_panel.wait()


def spread_kernel(share, step, ids_ref, got_hbm, own_ref, state_hbm, send_ref, got_ref, state_ref, sems):
    get_got = pltpu.make_async_copy(got_hbm, got_ref, sems.at[0])
    get_state = pltpu.make_async_copy(state_hbm.at[: 2 * NB, :], state_ref, sems.at[1])
    get_got.start()
    get_state.start()
    get_got.wait()
    total = jnp.sum(got_ref[...], 0)
    get_state.wait()
    own = own_ref[...]
    line = jnp.sum(state_ref[NB:, :], axis=0, keepdims=True)
    turned = mult(total, state_ref[:NB, :], 1, 1)
    rows = turned[:share] - own[:share] * line
    lead = jnp.where(ids_ref[0] == 1, turned[share + step :] - 0.5 * own[share + step :] * line, 0.0)
    out = jnp.concatenate([rows, total[share : share + step], lead], 0)
    send_ref[...] = jnp.broadcast_to(out[None], send_ref.shape)


def halves(value):
    high = value.astype(jnp.bfloat16)
    return high, (value - high.astype(jnp.float32)).astype(jnp.bfloat16)


def mult_half(left, right, right_dim=1):
    return lax.dot_general(left, right, (((1,), (right_dim,)), ((), ())), preferred_element_type=jnp.float32)


def mult_halves(left, right, right_dim):
    high, low = halves(left)
    right_high, right_low = halves(right)
    small = mult_half(low, right_high, right_dim) + mult_half(high, right_low, right_dim)
    return small + mult_half(high, right_high, right_dim)


def update_kernel(
    col_blocks, fold, slim, got_ref, pack_ref, a_ref, out_ref, high_ref, low_ref, hold_ref, lead_ref, new_ref, sems
):
    col_count = got_ref.shape[0]
    share, step, per = fold * slim, NB // col_count, NB // slim
    cols = col_blocks * NB
    for c in range(col_count):
        hold_ref[c * step : (c + 1) * step, :] = got_ref[c, share + slim : share + slim + step, :]
        lead_ref[c * step : (c + 1) * step, :] = got_ref[c, share + slim + step : share + slim + 2 * step, :]
    coupling, inverse, v = pack_ref[:NB, :], pack_ref[NB : 2 * NB, :], pack_ref[3 * NB : 3 * NB + cols, :]
    y_ref = pack_ref.at[3 * NB + cols :, :]
    cross = jnp.sum(pack_ref[2 * NB : 3 * NB, :], axis=1, keepdims=True) * lead_ref[...]
    middle = mult_packed(mult_packed(inverse, hold_ref[...]), inverse.T) - cross - cross.T
    z_cols = got_ref[:, share : share + slim, :].reshape(cols, NB)
    u = mult_halves(z_cols - mult_halves(v, middle, 0), coupling, 1)
    for at, part in enumerate((u, v)):
        high, low = halves(part)
        high_ref[:, at * NB : (at + 1) * NB] = high
        low_ref[:, at * NB : (at + 1) * NB] = low
    right_high, right_low = high_ref[...], low_ref[...]
    copies = []
    for k in range(a_ref.shape[0] // (fold * cols)):
        z = [got_ref[k * per : (k + 1) * per, f * slim : (f + 1) * slim, :].reshape(NB, NB) for f in range(fold)]
        y = y_ref[k * fold * NB : (k + 1) * fold * NB, :]
        high, low = halves(jnp.concatenate([y, jnp.concatenate(z, 0)], 1))
        change = mult_half(low, right_high) + mult_half(high, right_low) + mult_half(high, right_high)
        for n in range(col_blocks):
            here = pl.ds(k * fold * cols + n, fold * NB, col_blocks)
            new_ref[here, :] = a_ref[here, :] - change[:, n * NB : (n + 1) * NB]
        there = pl.ds(k * fold * cols, fold * cols)
        copy = pltpu.make_async_copy(new_ref.at[there, :], out_ref.at[there, :], sems.at[k])
        copy.start()
        copies.append(copy)
    for copy in copies:
        copy.wait()


def exchange(pieces, axis):
    return lax.all_to_all(pieces, axis, 0, 0)


def body(kernel):
    row_blocks, _, _, col_blocks, _, _ = kernel.shape
    rows, cols = row_blocks * NB, col_blocks * NB
    row_count, col_count = lax.axis_size("row"), lax.axis_size("col")
    fold = col_count // row_count
    row_index, col_index = lax.axis_index("row"), lax.axis_index("col")
    ids = jnp.stack([row_index, col_index]).astype(jnp.int32)
    lines = kernel.reshape(rows * col_blocks, NB)
    slim, step = cols // col_count, NB // col_count
    share = fold * slim
    pad = 2 * step

    def hbm(*dims):
        return pltpu.HBM(dims, jnp.float32)

    def relay(got):
        return pl.pallas_call(
            lambda *refs: relay_kernel(fold, slim, *refs),
            out_shape=shape(col_count, share + slim + pad, NB),
            in_specs=[SMEM, VMEM],
            out_specs=VMEM,
            compiler_params=PARAMS,
            name="relay",
            cost_estimate=cost(1_000_000, 1_000_000),
        )(ids, got)

    send = pl.pallas_call(
        lambda *refs: prepare_kernel(fold, slim, *refs),
        out_shape=shape(col_count, share + pad, NB),
        in_specs=[SMEM, HBM],
        out_specs=VMEM,
        scratch_shapes=[pltpu.VMEM((rows, NB), jnp.float32), pltpu.SemaphoreType.DMA],
        compiler_params=PARAMS,
        name="prepare",
        cost_estimate=cost(2 * rows * NB * NB * 6, 3_000_000),
    )(ids, pltpu.with_memory_space_constraint(kernel.reshape(rows, col_blocks, NB), pltpu.HBM))
    got = exchange(send, "col")
    own = got[1]
    got = jnp.broadcast_to(got[0][None], (row_count,) + got.shape[1:])
    got = exchange(relay(exchange(got, "row")), "col")

    send = pl.pallas_call(
        lambda *refs: product_kernel(col_blocks, fold, slim, *refs),
        out_shape=hbm(col_count, share + pad, NB),
        in_specs=[SMEM, VMEM, VMEM],
        out_specs=HBM,
        scratch_shapes=[
            pltpu.VMEM((col_count, share + pad, NB), jnp.float32),
            pltpu.VMEM((NB, NB), jnp.float32),
            pltpu.SemaphoreType.DMA((2,)),
        ],
        compiler_params=PARAMS,
        name="product",
        cost_estimate=cost(2 * rows * cols * NB * 6, 4_000_000),
    )(ids, got, lines)
    summed = exchange(send, "col")
    state, panel = pl.pallas_call(
        lambda *refs: factor_kernel(rows, fold, slim, step, *refs),
        out_shape=(hbm(3 * NB, NB), hbm(rows + cols, NB)),
        in_specs=[VMEM],
        out_specs=(HBM, HBM),
        scratch_shapes=[pltpu.VMEM((3 * NB, NB), jnp.float32), pltpu.VMEM((rows + cols, NB), jnp.float32)]
        + [pltpu.VMEM((NB, NB), jnp.float32)] * 2
        + [pltpu.SemaphoreType.DMA((2,))],
        compiler_params=PARAMS,
        name="factor",
        cost_estimate=cost(4_000_000_000, 2_000_000),
    )(got)
    state = pltpu.with_memory_space_constraint(state, pltpu.HBM)
    panel = pltpu.with_memory_space_constraint(panel, pltpu.HBM)

    send = pl.pallas_call(
        lambda *refs: spread_kernel(share, step, *refs),
        out_shape=shape(row_count, share + pad, NB),
        in_specs=[SMEM, HBM, VMEM, HBM],
        out_specs=VMEM,
        scratch_shapes=[
            pltpu.VMEM((col_count, share + pad, NB), jnp.float32),
            pltpu.VMEM((2 * NB, NB), jnp.float32),
            pltpu.SemaphoreType.DMA((2,)),
        ],
        compiler_params=PARAMS,
        name="spread",
        cost_estimate=cost(10_000_000, 1_000_000),
    )(ids, summed, own, state)
    got = exchange(send, "row")
    pack = pl.pallas_call(
        lambda *refs: invert_kernel(rows, cols, *refs),
        out_shape=shape(3 * NB + cols + rows, NB),
        in_specs=[SMEM, HBM, HBM],
        out_specs=VMEM,
        scratch_shapes=[
            pltpu.VMEM((3 * NB, NB), jnp.float32),
            pltpu.VMEM((rows + cols, NB), jnp.float32),
            pltpu.SemaphoreType.DMA((2,)),
        ],
        compiler_params=PARAMS,
        name="invert",
        cost_estimate=cost(4_000_000_000, 1_000_000),
    )(ids, state, panel)
    got, pack = lax.optimization_barrier((got, pack))
    last = exchange(relay(got), "col")

    updated = pl.pallas_call(
        lambda *refs: update_kernel(col_blocks, fold, slim, *refs),
        out_shape=shape(rows * col_blocks, NB),
        in_specs=[VMEM] * 3,
        out_specs=pl.BlockSpec(memory_space=pl.ANY),
        scratch_shapes=[
            pltpu.VMEM((cols, 2 * NB), jnp.bfloat16),
            pltpu.VMEM((cols, 2 * NB), jnp.bfloat16),
            pltpu.VMEM((NB, NB), jnp.float32),
            pltpu.VMEM((NB, NB), jnp.float32),
            pltpu.VMEM((rows * col_blocks, NB), jnp.float32),
            pltpu.SemaphoreType.DMA((row_blocks // fold,)),
        ],
        compiler_params=PARAMS,
        name="update",
        cost_estimate=cost(4 * rows * cols * NB * 6, 6_000_000),
    )(last, pack, lines)
    return updated.reshape(kernel.shape)


def solution(mesh):
    return jax.shard_map(
        body,
        mesh=mesh,
        in_specs=(P(None, "row", None, None, "col", None),),
        out_specs=P(None, "row", None, None, "col", None),
        check_vma=False,
    )
```
